32 devices in a mesh: batch: 4 (over x, core), row: 4 (over z), col: 2 (over y).
Axes of the slice: x: 2, y: 2, z: 4, core: 2. Of those that a mesh axis runs over, the one named last changes fastest.
Arguments:
- image_input: bfloat16 [4, 1024, 1536], P('batch', 'row', 'col'), may hold values from -16 to 16
- text_input: bfloat16 [4, 152, 1536], P('batch', 'row', 'col'), may hold values from -16 to 16
- image_cotan: bfloat16 [4, 1024, 1536], P('batch', 'row', 'col'), may hold values from -6 to 6
- text_cotan: bfloat16 [4, 152, 1536], P('batch', 'row', 'col'), may hold values from -6 to 6
- seq_group: int32 [3], replicated, may hold values from 0 to 3, as said below
- w_attend: bfloat16 [2, 1536, 4608], P(None, 'col', 'row'), may hold values from -0.15625 to 0.15625
- w_output: bfloat16 [2, 1536, 1536], P(None, 'row', 'col'), may hold values from -4 to 4
- w_expand: bfloat16 [2, 1536, 6144], P(None, 'col', 'row'), may hold values from -0.15625 to 0.15625
- w_reduce: bfloat16 [2, 6144, 1536], P(None, 'row', 'col'), may hold values from -0.078125 to 0.078125
- m_attend: float32 [2, 1536, 4608], P(None, ('col', 'batch'), 'row'), may hold values from -9.1552734e-05 to 9.1552734e-05
- m_output: float32 [2, 1536, 1536], P(None, ('row', 'batch'), 'col'), may hold values from -9.1552734e-05 to 9.1552734e-05
- m_expand: float32 [2, 1536, 6144], P(None, ('col', 'batch'), 'row'), may hold values from -9.1552734e-05 to 9.1552734e-05
- m_reduce: float32 [2, 6144, 1536], P(None, ('row', 'batch'), 'col'), may hold values from -9.1552734e-05 to 9.1552734e-05
- v_attend: float32 [2, 1536, 4608], P(None, ('col', 'batch'), 'row'), may hold values from 8.8303176e-12 to 3.532127e-11
- v_output: float32 [2, 1536, 1536], P(None, ('row', 'batch'), 'col'), may hold values from 8.8303177e-13 to 3.532127e-12
- v_expand: float32 [2, 1536, 6144], P(None, ('col', 'batch'), 'row'), may hold values from 8.8303176e-12 to 3.532127e-11
- v_reduce: float32 [2, 6144, 1536], P(None, ('row', 'batch'), 'col'), may hold values from 8.8303176e-12 to 3.532127e-11
Outputs:
- image_output: bfloat16 [4, 1024, 1536], P('batch', 'row', 'col')
- text_output: bfloat16 [4, 152, 1536], P('batch', 'row', 'col')
- image_grad: float32 [4, 1024, 1536], P('batch', 'row', 'col')
- text_grad: float32 [4, 152, 1536], P('batch', 'row', 'col')
- g_attend: float32 [2, 1536, 4608], P(None, ('col', 'batch'), 'row')
- g_output: float32 [2, 1536, 1536], P(None, ('row', 'batch'), 'col')
- g_expand: float32 [2, 1536, 6144], P(None, ('col', 'batch'), 'row')
- g_reduce: float32 [2, 6144, 1536], P(None, ('row', 'batch'), 'col')
- mnew_attend: float32 [2, 1536, 4608], P(None, ('col', 'batch'), 'row')
- mnew_output: float32 [2, 1536, 1536], P(None, ('row', 'batch'), 'col')
- mnew_expand: float32 [2, 1536, 6144], P(None, ('col', 'batch'), 'row')
- mnew_reduce: float32 [2, 6144, 1536], P(None, ('row', 'batch'), 'col')
- vnew_attend: float32 [2, 1536, 4608], P(None, ('col', 'batch'), 'row')
- vnew_output: float32 [2, 1536, 1536], P(None, ('row', 'batch'), 'col')
- vnew_expand: float32 [2, 1536, 6144], P(None, ('col', 'batch'), 'row')
- vnew_reduce: float32 [2, 6144, 1536], P(None, ('row', 'batch'), 'col')
- step_attend: float32 [2, 1536, 4608], P(None, ('col', 'batch'), 'row')
- step_output: float32 [2, 1536, 1536], P(None, ('row', 'batch'), 'col')
- step_expand: float32 [2, 1536, 6144], P(None, ('col', 'batch'), 'row')
- step_reduce: float32 [2, 6144, 1536], P(None, ('row', 'batch'), 'col')
- grad_norm: float32 [], replicated
The draws below stay inside these ranges and needn't reach their ends.
Inputs may be any that keep to these rules, and one draw needn't show every extreme that they name: `seq_group`: 3 different groups, each holding one sequence; the slots of other groups hold none.
All inputs are finite; a program needn't handle non-finite values.
Results may differ from the reference program's by a relative error of at most 0.013.
Values may be sent and summed in bfloat16 or wider, within the bound.
A program may use at most 256 MiB of HBM per device.

```python
import math
import jax
import jax.numpy as jnp
from jax import lax

D = 1536
HEADS = 24
HD = 64
FF = 6144
IMG = 1024
TXT = 152
STEP = 10
SEQS = 3
PARAMS = 56623104
N_BATCH = 4
N_COL = 2


def draw_seq_group(key, part):
    middle_groups = 1 + jax.random.permutation(key, N_BATCH - 2)[:SEQS - 2]
    chosen = jnp.concatenate([jnp.array([0, N_BATCH - 1], dtype=jnp.int32), middle_groups.astype(jnp.int32)])
    return chosen[jax.random.permutation(jax.random.fold_in(key, 7), SEQS)].astype(jnp.int32)


def feature_tokens(key, count):
    block = D // N_COL
    position = (jnp.arange(D, dtype=jnp.int32) % block).astype(jnp.float32) / (block - 1)
    amplitude = 10.0 ** (0.5 * position)
    noise = jnp.clip(jax.random.normal(key, (N_BATCH, count, D), jnp.float32), -6.0, 6.0)
    values = noise * amplitude / 2.0
    return jnp.clip(values, -16.0, 16.0)


def draw_image_input(key, part):
    return feature_tokens(jax.random.fold_in(key, 11), IMG).astype(jnp.bfloat16)


def draw_text_input(key, part):
    return feature_tokens(jax.random.fold_in(key, 13), TXT).astype(jnp.bfloat16)


def levels(rng, dims, cuts, smallest, top_value):
    level = 1.0
    for dim, shards_of in cuts:
        steps = jax.random.uniform(jax.random.fold_in(jax.random.fold_in(rng, 6), dim), (shards_of,), jnp.float32, smallest / len(cuts), top_value / len(cuts))
        level = level * jnp.repeat(jnp.exp(steps), dims[dim] // shards_of).reshape((-1,) + (1,) * (len(dims) - 1 - dim))
    return level


def bell_draw(key, shape, width, most, split=(), kind=jnp.bfloat16):
    result = jax.random.normal(key, shape, jnp.float32) * width
    if len(split) > 0:
        result = levels(key, shape, split, -0.22, 0.18) * result
    return jnp.clip(result, min=-most, max=most).astype(kind)


def setup_inputs(seed: int = 0) -> dict:
    arg_keys = jax.random.split(jax.random.key(seed), 18)
    return {
        "image_input": draw_image_input(jax.random.fold_in(arg_keys[17], 71), 0),
        "text_input": draw_text_input(jax.random.fold_in(arg_keys[17], 71), 0),
        "image_cotan": bell_draw(arg_keys[2], (N_BATCH, IMG, D), 1.0, 6.0, ((0, 4), (1, 4), (2, 2))),
        "text_cotan": bell_draw(arg_keys[3], (N_BATCH, TXT, D), 1.0, 6.0, ((0, 4), (1, 4), (2, 2))),
        "seq_group": draw_seq_group(jax.random.fold_in(arg_keys[17], 71), 0),
        "w_attend": bell_draw(arg_keys[5], (2, D, 3 * D), D ** -0.5, 0.15625, ((1, 2), (2, 4))),
        "w_output": bell_draw(arg_keys[6], (2, D, D), (0.8 * (IMG + TXT) ** 0.5 * D ** -0.5), 4.0, ((1, 4), (2, 2))),
        "w_expand": bell_draw(arg_keys[7], (2, D, FF), D ** -0.5, 0.15625, ((1, 2), (2, 4))),
        "w_reduce": bell_draw(arg_keys[8], (2, FF, D), FF ** -0.5, 0.078125, ((1, 4), (2, 2))),
        "m_attend": bell_draw(arg_keys[9], (2, D, 3 * D), (0.11 * PARAMS ** -0.5), 9.1552734375e-05, ((1, 8), (2, 4)), jnp.float32),
        "m_output": bell_draw(arg_keys[10], (2, D, D), (0.11 * PARAMS ** -0.5), 9.1552734375e-05, ((1, 16), (2, 2)), jnp.float32),
        "m_expand": bell_draw(arg_keys[11], (2, D, FF), (0.11 * PARAMS ** -0.5), 9.1552734375e-05, ((1, 8), (2, 4)), jnp.float32),
        "m_reduce": bell_draw(arg_keys[12], (2, FF, D), (0.11 * PARAMS ** -0.5), 9.1552734375e-05, ((1, 16), (2, 2)), jnp.float32),
        "v_attend": jnp.clip(jnp.exp(math.log(3.532127021421694e-11) - 1.3862944 * jax.random.uniform(arg_keys[13], (2, D, 3 * D), jnp.float32) ** levels(arg_keys[13], (2, D, 3 * D), ((1, 8), (2, 4)), -0.2, 0.2)), 8.830317553554234e-12, 3.532127021421694e-11),
        "v_output": jnp.clip(jnp.exp(math.log(3.5321270647897807e-12) - 1.3862944 * jax.random.uniform(arg_keys[14], (2, D, D), jnp.float32) ** levels(arg_keys[14], (2, D, D), ((1, 16), (2, 2)), -0.2, 0.2)), 8.830317661974452e-13, 3.5321270647897807e-12),
        "v_expand": jnp.clip(jnp.exp(math.log(3.532127021421694e-11) - 1.3862944 * jax.random.uniform(arg_keys[15], (2, D, FF), jnp.float32) ** levels(arg_keys[15], (2, D, FF), ((1, 8), (2, 4)), -0.2, 0.2)), 8.830317553554234e-12, 3.532127021421694e-11),
        "v_reduce": jnp.clip(jnp.exp(math.log(3.532127021421694e-11) - 1.3862944 * jax.random.uniform(arg_keys[16], (2, FF, D), jnp.float32) ** levels(arg_keys[16], (2, FF, D), ((1, 16), (2, 2)), -0.2, 0.2)), 8.830317553554234e-12, 3.532127021421694e-11),
    }


EPSILON = 1e-06
HIGH = lax.Precision.HIGHEST
BETA_ONE = 0.9
BETA_TWO = 0.999
RATE = 0.02
DECAY = 0.1

@jax.custom_vjp
def low(v):
    return lax.optimization_barrier(v.astype(jnp.bfloat16)).astype(jnp.float32)

@jax.custom_vjp
def low_back(v):
    return v

def low_keep(v):
    return (low(v), None)

def low_pass(kept, grad):
    return (grad,)

def back_keep(v):
    return (v, None)

def back_low(kept, grad):
    return (low(grad),)
low.defvjp(low_keep, low_pass)
low_back.defvjp(back_keep, back_low)

def matmul(operand, another):
    return jnp.dot(operand, another, precision=HIGH)

def layer_norm(values):
    center = lax.optimization_barrier(jnp.mean(values, axis=-1, keepdims=True))
    spread = lax.optimization_barrier(jnp.mean(values * values, axis=-1, keepdims=True)) - center * center
    return (values - center) * lax.rsqrt(spread + EPSILON)

def one_head(parts):
    scores = low_back(matmul(parts[0], parts[1].T) * HD ** (-0.5))
    shifted = jnp.exp(scores - lax.optimization_barrier(jnp.max(scores, axis=-1, keepdims=True)))
    soft_probs = shifted / lax.optimization_barrier(jnp.sum(shifted, axis=-1, keepdims=True))
    return matmul(low(soft_probs), parts[2])

def forward(w_att, w_out, w_exp, w_red, image_x, text_x):
    residual = [image_x, text_x]
    projected = [low(low_back(matmul(low(layer_norm(residual[branch])), w_att[branch]))) for branch in range(2)]
    joined = jnp.concatenate(projected, 0).reshape(-1, HEADS, 3, HD)
    by_head = jnp.transpose(joined, (1, 2, 0, 3))
    attended = lax.map(jax.checkpoint(one_head), by_head)
    attended = jnp.transpose(attended, (1, 0, 2)).reshape(-1, D)
    attended = low(low_back(attended))
    pieces = [attended[:IMG], attended[IMG:]]
    outputs = []
    for branch in range(2):
        middle = residual[branch] + low_back(matmul(pieces[branch], w_out[branch]))
        hidden = low_back(matmul(low(layer_norm(middle)), w_exp[branch]))
        activated = low(jax.nn.gelu(hidden, approximate=True))
        outputs.append(middle + low_back(matmul(activated, w_red[branch])))
    return (outputs[0], outputs[1])

def adamw(gradient, moment, square, weight, clip_factor):
    clipped = gradient * clip_factor
    moment_new = BETA_ONE * moment + (1.0 - BETA_ONE) * clipped
    square_new = BETA_TWO * square + (1.0 - BETA_TWO) * clipped * clipped
    corrected = moment_new / (1.0 - BETA_ONE ** STEP) / (jnp.sqrt(square_new / (1.0 - BETA_TWO ** STEP)) + 1e-08)
    return (moment_new, square_new, -RATE * (corrected + DECAY * weight))

def reference(image_input, text_input, image_cotan, text_cotan, seq_group, w_attend, w_output, w_expand, w_reduce, m_attend, m_output, m_expand, m_reduce, v_attend, v_output, v_expand, v_reduce):
    w_att = w_attend.astype(jnp.float32)
    w_out = w_output.astype(jnp.float32)
    w_exp = w_expand.astype(jnp.float32)
    w_red = w_reduce.astype(jnp.float32)
    slots = jnp.arange(N_BATCH, dtype=jnp.int32)
    present = jnp.any(seq_group[None, :] == slots[:, None], axis=1).astype(jnp.float32)

    def one_slot(totals, inputs):
        image_x, text_x, image_c, text_c, occupied = inputs
        results, pullback = jax.vjp(forward, w_att, w_out, w_exp, w_red, image_x.astype(jnp.float32), text_x.astype(jnp.float32))
        gradients = pullback((image_c.astype(jnp.float32) * occupied, text_c.astype(jnp.float32) * occupied))
        totals = tuple((running + fresh for running, fresh in zip(totals, gradients[:4])))
        return (totals, (results[0].astype(jnp.bfloat16), results[1].astype(jnp.bfloat16), gradients[4], gradients[5]))
    start = (jnp.zeros_like(w_att), jnp.zeros_like(w_out), jnp.zeros_like(w_exp), jnp.zeros_like(w_red))
    totals, emitted = lax.scan(one_slot, start, (image_input, text_input, image_cotan, text_cotan, present))
    squares = jnp.float32(0.0)
    for matrix in totals:
        squares = squares + jnp.sum(matrix * matrix)
    grad_norm = jnp.sqrt(squares)
    clip_factor = jnp.minimum(1.0, 1.0 / (grad_norm + 1e-06))
    attend_new = adamw(totals[0], m_attend, v_attend, w_att, clip_factor)
    output_new = adamw(totals[1], m_output, v_output, w_out, clip_factor)
    expand_new = adamw(totals[2], m_expand, v_expand, w_exp, clip_factor)
    reduce_new = adamw(totals[3], m_reduce, v_reduce, w_red, clip_factor)
    return (emitted[0], emitted[1], emitted[2], emitted[3], totals[0], totals[1], totals[2], totals[3], attend_new[0], output_new[0], expand_new[0], reduce_new[0], attend_new[1], output_new[1], expand_new[1], reduce_new[1], attend_new[2], output_new[2], expand_new[2], reduce_new[2], grad_norm)
```

```python
from functools import partial

import jax
import jax.numpy as jnp
from jax import lax
from jax.sharding import PartitionSpec as P

D = 1536
HD = 64
STEP = 10

EPSILON = 1e-06
BETA_ONE = 0.9
BETA_TWO = 0.999
RATE = 0.02
DECAY = 0.1

BF = jnp.bfloat16
F32 = jnp.float32


def dot(a, b):
    return lax.dot_general(a, b, (((a.ndim - 1,), (0,)), ((), ())), preferred_element_type=F32)


def dot_nt(a, b):
    return lax.dot_general(a, b, (((a.ndim - 1,), (1,)), ((), ())), preferred_element_type=F32)


def dot_tn(a, b):
    return lax.dot_general(a, b, (((0,), (0,)), ((), ())), preferred_element_type=F32)


def adamw(gradient, moment, square, weight, clip_factor):
    clipped = gradient * clip_factor
    moment_new = BETA_ONE * moment + (1.0 - BETA_ONE) * clipped
    square_new = BETA_TWO * square + (1.0 - BETA_TWO) * clipped * clipped
    corrected = (
        moment_new
        / (1.0 - BETA_ONE**STEP)
        / (jnp.sqrt(square_new / (1.0 - BETA_TWO**STEP)) + 1e-08)
    )
    return (moment_new, square_new, -RATE * (corrected + DECAY * weight))


def weight_shard(weight, group_index, shard_rows):
    return lax.dynamic_slice_in_dim(weight, group_index * shard_rows, shard_rows, 1).astype(F32)


class Layout:
    def __init__(self, n_row, img, txt):
        self.n_row = n_row
        self.img = img
        self.txt = txt
        self.txt_pad = -(-txt // 16) * 16
        self.rows = img + self.txt_pad
        self.real = img + txt

    def pack(self, image, text):
        return jnp.concatenate(
            [image, text, jnp.zeros((self.txt_pad - self.txt, image.shape[1]), image.dtype)], 0
        )

    def mm(self, full, w, f):
        full = full.reshape(self.n_row, self.rows, -1)
        one = f(full[:, : self.img], w[0])
        two = f(full[:, self.img :], w[1])
        return jnp.concatenate([one, two], 1).reshape(self.n_row * self.rows, -1)

    def grad(self, left, right):
        left = left.reshape(self.n_row, self.rows, -1)
        right = right.reshape(self.n_row, self.rows, -1)
        parts = []
        for part in (slice(0, self.img), slice(self.img, self.rows)):
            a = left[:, part].reshape(-1, left.shape[2])
            b = right[:, part].reshape(-1, right.shape[2])
            parts.append(dot_tn(a, b))
        return jnp.stack(parts)


def row_gather(x):
    return lax.all_gather(x, "row", axis=0, tiled=True)


def row_reduce(x):
    return lax.psum_scatter(x.astype(BF), "row", scatter_dimension=0, tiled=True).astype(F32)


def col_swap(x, n_col):
    return lax.ppermute(x, "col", [(i, (i + 1) % n_col) for i in range(n_col)])


def col_reduce(x, n_col):
    c = lax.axis_index("col")
    half = x.shape[1] // 2
    mine = lax.dynamic_slice_in_dim(x, c * half, half, 1)
    other = lax.dynamic_slice_in_dim(x, (1 - c) * half, half, 1).astype(BF)
    return mine + col_swap(other, n_col).astype(F32)


def col_gather(x, n_col):
    c = lax.axis_index("col")
    other = col_swap(x, n_col)
    both = jnp.where(c == 0, jnp.stack([x, other]), jnp.stack([other, x]))
    return jnp.concatenate([both[0], both[1]], 1)


def token_sums(a, b):
    return lax.psum(jnp.stack([jnp.sum(a, 1), jnp.sum(b, 1)]), "col")


def norm(x):
    sums = token_sums(x, x * x) / D
    center, square = sums[0], sums[1]
    inverse = lax.rsqrt(square - center * center + EPSILON)[:, None]
    return (x - center[:, None]) * inverse, inverse


def norm_back(normed, inverse, gradient):
    sums = token_sums(gradient, gradient * normed) / D
    return inverse * (gradient - sums[0][:, None] - normed * sums[1][:, None])


def attention_forward(qkv, heads, real, rows):
    t = qkv.shape[0]
    parts = qkv.reshape(t, heads, 3, HD)
    valid = (jnp.arange(t) % rows) < real
    s = jnp.einsum("qhd,khd->hqk", parts[:, :, 0], parts[:, :, 1], preferred_element_type=F32)
    s = jnp.where(valid[None, None], s * HD**-0.5, -1e30)
    peak = jnp.max(s, axis=2, keepdims=True)
    e = jnp.exp(s - peak)
    total = jnp.sum(e, axis=2, keepdims=True)
    p = (e / total).astype(BF)
    o = jnp.einsum("hqk,khd->qhd", p, parts[:, :, 2], preferred_element_type=F32)
    return o.astype(BF).reshape(t, heads * HD), peak + jnp.log(total)


def attention_backward(qkv, lse, do, heads, real, rows):
    t = qkv.shape[0]
    parts = qkv.reshape(t, heads, 3, HD)
    do = do.reshape(t, heads, HD)
    valid = (jnp.arange(t) % rows) < real
    q, k, v = parts[:, :, 0], parts[:, :, 1], parts[:, :, 2]
    s = jnp.einsum("qhd,khd->hqk", q, k, preferred_element_type=F32) * HD**-0.5
    p = jnp.where(valid[None, None], jnp.exp(s - lse), 0.0)
    dp = jnp.einsum("qhd,khd->hqk", do, v, preferred_element_type=F32)
    row_dot = jnp.sum(p * dp, axis=2, keepdims=True)
    ds = (p * (dp - row_dot)).astype(BF)
    dq = jnp.einsum("hqk,khd->qhd", ds, k, preferred_element_type=F32) * HD**-0.5
    dk = jnp.einsum("hqk,qhd->khd", ds, q, preferred_element_type=F32) * HD**-0.5
    dv = jnp.einsum("hqk,qhd->khd", p.astype(BF), do, preferred_element_type=F32)
    return jnp.stack([dq, dk, dv], 2).astype(BF).reshape(t, heads * 3 * HD)


def on_device(n_row, n_col, *args):
    (
        image_input,
        text_input,
        image_cotan,
        text_cotan,
        seq_group,
        w_attend,
        w_output,
        w_expand,
        w_reduce,
        m_attend,
        m_output,
        m_expand,
        m_reduce,
        v_attend,
        v_output,
        v_expand,
        v_reduce,
    ) = args
    img, txt = image_input.shape[1], text_input.shape[1]
    lay = Layout(n_row, img, txt)
    heads = w_attend.shape[2] // (3 * HD) // n_col
    group_index = lax.axis_index("batch")
    present = jnp.any(seq_group == group_index).astype(F32)

    x = lay.pack(image_input[0], text_input[0]).astype(F32)
    cot = lay.pack(image_cotan[0], text_cotan[0]).astype(F32) * present
    cb_all = row_gather(cot.astype(BF))

    normed_one, inverse_one = norm(x)
    a1_all = row_gather(normed_one.astype(BF))
    qkv = col_reduce(lay.mm(a1_all, w_attend, dot), n_col).astype(BF)
    o, lse = attention_forward(qkv, heads, lay.real, lay.rows)
    o_all = col_gather(o, n_col)
    middle = x + row_reduce(lay.mm(o_all, w_output, dot))
    normed_two, inverse_two = norm(middle)
    a2_all = row_gather(normed_two.astype(BF))
    dact = col_reduce(lay.mm(cb_all, w_reduce, dot_nt), n_col)
    hidden = col_reduce(lay.mm(a2_all, w_expand, dot), n_col)
    act, gelu_pull = jax.vjp(partial(jax.nn.gelu, approximate=True), hidden)
    dhidden = gelu_pull(dact)[0].astype(BF)
    dh_all = col_gather(dhidden, n_col)
    dn = row_reduce(lay.mm(dh_all, w_expand, dot_nt))
    g_all = col_gather(act.astype(BF), n_col)
    result = middle + row_reduce(lay.mm(g_all, w_reduce, dot))
    grad_mid = cot + norm_back(normed_two, inverse_two, dn)
    dy_all = row_gather(grad_mid.astype(BF))
    do = col_reduce(lay.mm(dy_all, w_output, dot_nt), n_col).astype(BF)

    g_red = lay.grad(g_all, cb_all)
    g_exp = lay.grad(a2_all, dh_all)
    g_out = lay.grad(o_all, dy_all)
    dqkv = attention_backward(qkv, lse, do, heads, lay.real, lay.rows)
    dqkv_all = col_gather(dqkv, n_col)
    g_att = lay.grad(a1_all, dqkv_all)
    da = row_reduce(lay.mm(dqkv_all, w_attend, dot_nt))
    grad_in = grad_mid + norm_back(normed_one, inverse_one, da)

    def batch_sum(g):
        return lax.psum_scatter(g.astype(BF), "batch", scatter_dimension=1, tiled=True).astype(F32)

    sums = [batch_sum(g) for g in (g_att, g_out, g_exp, g_red)]
    squares = sum(jnp.sum(g * g) for g in sums)
    grad_norm = jnp.sqrt(lax.psum(squares, ("batch", "row", "col")))
    clip_factor = jnp.minimum(1.0, 1.0 / (grad_norm + 1e-06))
    news = []
    for g, m, v, w in zip(
        sums,
        (m_attend, m_output, m_expand, m_reduce),
        (v_attend, v_output, v_expand, v_reduce),
        (w_attend, w_output, w_expand, w_reduce),
    ):
        news.append(adamw(g, m, v, weight_shard(w, group_index, g.shape[1]), clip_factor))
    return (
        result[:img].astype(BF)[None],
        result[img : lay.real].astype(BF)[None],
        grad_in[:img][None],
        grad_in[img : lay.real][None],
        *sums,
        *[n[0] for n in news],
        *[n[1] for n in news],
        *[n[2] for n in news],
        grad_norm,
    )


def solution(mesh):
    tokens = P("batch", "row", "col")
    wide = P(None, "col", "row")
    tall = P(None, "row", "col")
    wide_shard = P(None, ("col", "batch"), "row")
    tall_shard = P(None, ("row", "batch"), "col")
    shards = (wide_shard, tall_shard, wide_shard, tall_shard)
    return jax.shard_map(
        partial(on_device, mesh.shape["row"], mesh.shape["col"]),
        mesh=mesh,
        in_specs=(*[tokens] * 4, P(), wide, tall, wide, tall, *shards, *shards),
        out_specs=(*[tokens] * 4, *shards * 4, P()),
        check_vma=False,
    )
```

```python
import math
from functools import partial

import jax
import jax.numpy as jnp
from jax import lax
from jax.experimental import pallas as pl
from jax.experimental.pallas import tpu as pltpu
from jax.sharding import PartitionSpec as P

D = 1536
HD = 64
STEP = 10

EPSILON = 1e-06
BETA_ONE = 0.9
BETA_TWO = 0.999
RATE = 0.02
DECAY = 0.1

BF = jnp.bfloat16
F32 = jnp.float32


def dot(a, b):
    return lax.dot_general(a, b, (((a.ndim - 1,), (0,)), ((), ())), preferred_element_type=F32)


def dot_nt(a, b):
    return lax.dot_general(a, b, (((a.ndim - 1,), (1,)), ((), ())), preferred_element_type=F32)


def dot_tn(a, b):
    return lax.dot_general(a, b, (((0,), (0,)), ((), ())), preferred_element_type=F32)


MESH = pl.DeviceIdType.MESH
VMEM = pl.BlockSpec(memory_space=pltpu.VMEM)


def remote(src, dst, send, recv, **where):
    return pltpu.make_async_remote_copy(
        src_ref=src,
        dst_ref=dst,
        send_sem=send,
        recv_sem=recv,
        device_id=where,
        device_id_type=MESH,
    )


def near_first(z, n, j):
    alternate = jnp.where(j % 2 == 1, z - (j + 1) // 2, z + j // 2)
    reach = jnp.minimum(z, n - 1 - z)
    beyond = jnp.where(z <= n - 1 - z, j, n - 1 - j)
    return jnp.where(j <= 2 * reach, alternate, beyond)


def greet(n):
    z, c = lax.axis_index("row"), lax.axis_index("col")
    barrier = pltpu.get_barrier_semaphore()
    pl.semaphore_signal(barrier, inc=1, device_id={"col": 1 - c}, device_id_type=MESH)

    @pl.when(z > 0)
    def _():
        pl.semaphore_signal(barrier, inc=1, device_id={"row": z - 1}, device_id_type=MESH)

    @pl.when(z < n - 1)
    def _():
        pl.semaphore_signal(barrier, inc=1, device_id={"row": z + 1}, device_id_type=MESH)

    ends = jnp.where(z > 0, 1, 0) + jnp.where(z < n - 1, 1, 0)
    pl.semaphore_wait(barrier, 1 + ends)


class Gather:
    def __init__(self, full, send, recv, n):
        self.full, self.send, self.recv, self.n = full, send, recv, n
        self.z = lax.axis_index("row")

    def copy(self, k, step):
        there = (self.z + step + self.n) % self.n
        way = 0 if step > 0 else 1
        return remote(
            self.full.at[k], self.full.at[k], self.send.at[way, k], self.recv.at[k], row=there
        )

    def push(self, k):
        @pl.when((k <= self.z) & (self.z < self.n - 1))
        def _():
            self.copy(k, 1).start()

        @pl.when((k >= self.z) & (self.z > 0))
        def _():
            self.copy(k, -1).start()

    def arrive(self, k):
        @pl.when(k != self.z)
        def _():
            self.copy(k, 1).wait_recv()

        self.push(k)

    def arrive_after_own(self, k):
        @pl.when(k != self.z)
        def _():
            self.arrive(k)

    def finish(self):
        @pl.loop(0, self.n)
        def _(k):
            @pl.when((k <= self.z) & (self.z < self.n - 1))
            def _():
                self.copy(k, 1).wait_send()

            @pl.when((k >= self.z) & (self.z > 0))
            def _():
                self.copy(k, -1).wait_send()


class Reduce:
    def __init__(self, acc, out, inbox, send, recv, n):
        self.acc, self.out, self.inbox, self.send, self.recv, self.n = acc, out, inbox, send, recv, n
        self.z = lax.axis_index("row")

    def copy(self, o):
        way = jnp.where(o > self.z, 0, 1)
        there = (self.z + jnp.where(o > self.z, 1, -1) + self.n) % self.n
        return remote(
            self.out.at[o], self.inbox.at[way, o], self.send.at[o], self.recv.at[way, o], row=there
        )

    def wait_in(self, way, o):
        remote(
            self.out.at[o],
            self.inbox.at[way, o],
            self.send.at[o],
            self.recv.at[way, o],
            row=(self.z + 1) % self.n,
        ).wait_recv()

    def add(self, o):
        @pl.when((o >= self.z) & (self.z > 0))
        def _():
            self.wait_in(0, o)
            self.acc[...] += self.inbox[0, o].astype(F32)

        @pl.when((o <= self.z) & (self.z < self.n - 1))
        def _():
            self.wait_in(1, o)
            self.acc[...] += self.inbox[1, o].astype(F32)

        @pl.when(o != self.z)
        def _():
            self.out[o] = self.acc[...].astype(BF)
            self.copy(o).start()

    def finish(self):
        @pl.loop(0, self.n)
        def _(o):
            @pl.when(o != self.z)
            def _():
                self.copy(o).wait_send()


class Swap:
    def __init__(self, out, into, send, recv):
        self.out, self.into, self.send, self.recv = out, into, send, recv

    def copy(self, k):
        return remote(
            self.out.at[k],
            self.into.at[k],
            self.send.at[k],
            self.recv.at[k],
            col=1 - lax.axis_index("col"),
        )

    def start(self, k):
        self.copy(k).start()

    def arrive(self, k):
        self.copy(k).wait_recv()

    def finish(self, n):
        @pl.loop(0, n)
        def _(k):
            self.copy(k).wait_send()


def sums_of(a, b):
    lane = lax.broadcasted_iota(jnp.int32, (a.shape[0], 128), 1)
    one, two = jnp.sum(a, axis=1, keepdims=True), jnp.sum(b, axis=1, keepdims=True)
    return jnp.where(lane == 0, one, jnp.where(lane == 1, two, 0.0))


def moments(stat):
    mean = stat[0, :, 0:1] / D
    return mean, lax.rsqrt(stat[0, :, 1:2] / D - mean * mean + EPSILON)


def exchange(stat, stat_in, send, recv):
    swap = Swap(stat, stat_in, send, recv)
    swap.start(0)
    swap.arrive(0)
    swap.finish(1)
    stat[0] += stat_in[0]


def dma(*shape):
    return pltpu.SemaphoreType.DMA(shape)


def call(kernel, ident, outs, scratch, cost, *operands):
    return pl.pallas_call(
        kernel,
        out_shape=[jax.ShapeDtypeStruct(s, t) for s, t in outs],
        in_specs=[VMEM] * len(operands),
        out_specs=[VMEM] * len(outs),
        scratch_shapes=scratch,
        compiler_params=pltpu.CompilerParams(
            collective_id=ident, has_side_effects=True, vmem_limit_bytes=60 * 2**20
        ),
        cost_estimate=pl.CostEstimate(flops=cost, bytes_accessed=10**7, transcendentals=0),
    )(*operands)


def parts_of(lay):
    return ((0, slice(0, lay.img)), (1, slice(lay.img, lay.rows)))


def attend_kernel(lay, x_ref, w_ref, full_ref, qkv_ref, stat_ref, *scratch):
    own, out, into, stat_in, g_send, g_recv, s_send, s_recv, t_send, t_recv = scratch
    n = lay.n_row
    z, c = lax.axis_index("row"), lax.axis_index("col")
    half = qkv_ref.shape[2]
    greet(n)
    x = x_ref[...].astype(F32)
    stat_ref[0] = sums_of(x, x * x)
    exchange(stat_ref, stat_in, t_send, t_recv)
    mean, inverse = moments(stat_ref)
    full_ref[z] = ((x - mean) * inverse).astype(BF)
    gather = Gather(full_ref, g_send, g_recv, n)
    swap = Swap(out, into, s_send, s_recv)

    @pl.loop(0, n)
    def _(j):
        k = near_first(z, n, j)
        gather.arrive(k)
        for part, rows in parts_of(lay):
            p = dot(full_ref[k, rows], w_ref[part])
            low, high = p[:, :half], p[:, half:]
            own[k, rows] = jnp.where(c == 0, low, high)
            out[k, rows] = jnp.where(c == 0, high, low).astype(BF)
        swap.start(k)

    @pl.loop(0, n)
    def _(j):
        k = near_first(z, n, j)
        swap.arrive(k)
        qkv_ref[k] = (own[k] + into[k].astype(F32)).astype(BF)

    gather.finish()
    swap.finish(n)


def attend(lay, x, w):
    n, r, half, d = lay.n_row, lay.rows, w.shape[2] // 2, x.shape[1]
    return call(
        partial(attend_kernel, lay),
        1,
        [((n, r, d), BF), ((n, r, half), BF), ((1, r, 128), F32)],
        [
            pltpu.VMEM((n, r, half), F32),
            pltpu.VMEM((n, r, half), BF),
            pltpu.VMEM((n, r, half), BF),
            pltpu.VMEM((1, r, 128), F32),
            dma(2, n),
            dma(n),
            dma(n),
            dma(n),
            dma(1),
            dma(1),
        ],
        2 * n * r * w.shape[1] * w.shape[2],
        x,
        w,
    )


def split_heads(lay, qkv_ref, q_ref, k_ref, v_ref, fill):
    n, img, txt = lay.n_row, lay.img, lay.txt_pad
    heads = qkv_ref.shape[2] // (3 * HD)

    @pl.loop(0, n)
    def _(k):
        first = pl.ds(pl.multiple_of(k * img, 16), img)
        second = pl.ds(pl.multiple_of(n * img + k * txt, 16), txt)
        for h in range(heads):
            at = h * 3 * HD
            rows = qkv_ref[k, :, at : at + 3 * HD]
            q_ref[h, k] = rows[:, :HD] * jnp.asarray(HD**-0.5, BF)
            for ref, lo in ((k_ref, HD), (v_ref, 2 * HD)):
                value = rows[:, lo : lo + HD]
                if ref is v_ref and fill:
                    value = jnp.concatenate([value, jnp.ones_like(value)], 1)
                ref[h, first] = value[:img]
                ref[h, second] = value[img:]


def text_bias(lay):
    lane = lax.broadcasted_iota(jnp.int32, (1, lay.n_row * lay.txt_pad), 1)
    return jnp.where(lane % lay.txt_pad < lay.txt, 0.0, -1e30)


def middle_kernel(
    lay, qkv_ref, x_ref, cot_ref, wo_ref, wr_ref, o_ref, lse_ref, cb_ref, dg_ref, mid_ref, low_ref, stat_ref, *scratch
):
    (
        q_s, k_s, v_s, o_out, o_in, dg_out, dg_in, acc, r_out, inbox, stat_in,
        g_send, g_recv, o_send, o_recv, d_send, d_recv, r_send, r_recv, t_send, t_recv,
    ) = scratch
    n, far = lay.n_row, lay.n_row * lay.img
    z, c = lax.axis_index("row"), lax.axis_index("col")
    heads, hid = q_s.shape[0], dg_ref.shape[2]
    greet(n)
    gather = Gather(cb_ref, g_send, g_recv, n)
    cb_ref[z] = cot_ref[...]
    gather.push(z)
    swap_o = Swap(o_out, o_in, o_send, o_recv)
    swap_d = Swap(dg_out, dg_in, d_send, d_recv)
    reduce = Reduce(acc, r_out, inbox, r_send, r_recv, n)
    split_heads(lay, qkv_ref, q_s, k_s, v_s, True)
    bias = text_bias(lay)
    lane = lax.broadcasted_iota(jnp.int32, (lay.rows, 128), 1)

    def attention(k):
        outs, lse = [], jnp.zeros((lay.rows, 128), F32)
        for h in range(heads):
            q = q_s[h, k]
            s1 = dot_nt(q, k_s[h, :far])
            s2 = dot_nt(q, k_s[h, far:]) + bias
            peak = jnp.maximum(
                jnp.max(s1, axis=1, keepdims=True), jnp.max(s2, axis=1, keepdims=True)
            )
            e1, e2 = jnp.exp(s1 - peak).astype(BF), jnp.exp(s2 - peak).astype(BF)
            o = dot(e1, v_s[h, :far]) + dot(e2, v_s[h, far:])
            total = o[:, HD : HD + 1]
            outs.append((o[:, :HD] / total).astype(BF))
            lse = jnp.where(lane == h, peak + jnp.log(total), lse)
        lse_ref[k] = lse
        o_out[k] = jnp.concatenate(outs, 1)

    def project(k):
        swap_o.arrive(k)
        own, other = o_out[k], o_in[k]
        o_ref[k] = jnp.concatenate(
            [jnp.where(c == 0, own, other), jnp.where(c == 0, other, own)], 1
        )
        for part, rows in parts_of(lay):
            acc[rows] = dot(o_ref[k, rows], wo_ref[part])
        reduce.add(k)

    @pl.loop(0, n)
    def _(j):
        k = near_first(z, n, n - 1 - j)
        attention(k)
        swap_o.start(k)
        near = near_first(z, n, j)
        gather.arrive_after_own(near)
        for part, rows in parts_of(lay):
            dg_out[near, rows] = dot_nt(
                cb_ref[near, rows], wr_ref[part, pl.ds(pl.multiple_of((1 - c) * hid, 128), hid), :]
            ).astype(BF)
        swap_d.start(near)
        for part, rows in parts_of(lay):
            dg_ref[near, rows] = dot_nt(
                cb_ref[near, rows], wr_ref[part, pl.ds(pl.multiple_of(c * hid, 128), hid), :]
            )

        @pl.when(j > 0)
        def _():
            project(near_first(z, n, n - j))

    project(near_first(z, n, 0))
    mid = x_ref[...].astype(F32) + acc[...]
    mid_ref[...] = mid
    stat_ref[0] = sums_of(mid, mid * mid)
    exchange(stat_ref, stat_in, t_send, t_recv)
    mean, inverse = moments(stat_ref)
    low_ref[...] = ((mid - mean) * inverse).astype(BF)

    @pl.loop(0, n)
    def _(j):
        k = near_first(z, n, j)
        swap_d.arrive(k)
        dg_ref[k] += dg_in[k].astype(F32)

    gather.finish()
    swap_o.finish(n)
    swap_d.finish(n)
    reduce.finish()


def middle(lay, qkv, x, cot, wo, wr):
    n, r, d = lay.n_row, lay.rows, x.shape[1]
    heads, hid = qkv.shape[2] // (3 * HD), wr.shape[1] // 2
    keys = n * r
    return call(
        partial(middle_kernel, lay),
        2,
        [
            ((n, r, 2 * heads * HD), BF),
            ((n, r, 128), F32),
            ((n, r, d), BF),
            ((n, r, hid), F32),
            ((r, d), F32),
            ((r, d), BF),
            ((1, r, 128), F32),
        ],
        [
            pltpu.VMEM((heads, n, r, HD), BF),
            pltpu.VMEM((heads, keys, HD), BF),
            pltpu.VMEM((heads, keys, 2 * HD), BF),
            pltpu.VMEM((n, r, heads * HD), BF),
            pltpu.VMEM((n, r, heads * HD), BF),
            pltpu.VMEM((n, r, hid), BF),
            pltpu.VMEM((n, r, hid), BF),
            pltpu.VMEM((r, d), F32),
            pltpu.VMEM((n, r, d), BF),
            pltpu.VMEM((2, n, r, d), BF),
            pltpu.VMEM((1, r, 128), F32),
            dma(2, n),
            dma(n),
            dma(n),
            dma(n),
            dma(n),
            dma(n),
            dma(n),
            dma(2, n),
            dma(1),
            dma(1),
        ],
        10**10,
        qkv,
        x,
        cot,
        wo,
        wr,
    )


SLOPE = (2.0 / math.pi) ** 0.5
CUBIC = 0.044715


def gelu_pair(u):
    square = u * u
    t = jnp.tanh(SLOPE * u * (1.0 + CUBIC * square))
    half = 0.5 * (1.0 + t)
    slope = half + 0.5 * u * (1.0 - t * t) * (SLOPE * (1.0 + 3.0 * CUBIC * square))
    return u * half, slope


def hidden_kernel(
    lay, low_ref, dg_ref, mid_ref, cot_ref, stat_ref, we_ref, full_ref, act_ref, dh_ref, dmid_ref, dy_ref, *scratch
):
    (
        own, out, into, acc, r_out, inbox, stat_out, stat_in,
        g_send, g_recv, s_send, s_recv, d_send, d_recv, r_send, r_recv, t_send, t_recv,
    ) = scratch
    n = lay.n_row
    z, c = lax.axis_index("row"), lax.axis_index("col")
    hid = dg_ref.shape[2]
    mine = pl.ds(pl.multiple_of(c * hid, 128), hid)
    theirs = pl.ds(pl.multiple_of((1 - c) * hid, 128), hid)
    greet(n)
    gather = Gather(full_ref, g_send, g_recv, n)
    full_ref[z] = low_ref[...]
    gather.push(z)
    swap = Swap(out, into, s_send, s_recv)
    reduce = Reduce(acc, r_out, inbox, r_send, r_recv, n)

    def dh_copy(k):
        half = dh_ref.at[k, :, mine]
        return remote(half, half, d_send.at[k], d_recv.at[k], col=1 - c)

    @pl.loop(0, n)
    def _(j):
        k = near_first(z, n, j)
        gather.arrive_after_own(k)
        for part, rows in parts_of(lay):
            out[k, rows] = dot(full_ref[k, rows], we_ref[part, :, theirs]).astype(BF)
        swap.start(k)
        for part, rows in parts_of(lay):
            own[k, rows] = dot(full_ref[k, rows], we_ref[part, :, mine])

    def back(k):
        half = dh_ref.at[k, :, theirs]
        remote(half, half, d_send.at[k], d_recv.at[k], col=1 - c).wait_recv()
        for part, rows in parts_of(lay):
            acc[rows] = dot_nt(dh_ref[k, rows], we_ref[part])
        reduce.add(k)

    @pl.loop(0, n)
    def _(j):
        k = near_first(z, n, n - 1 - j)
        swap.arrive(k)
        act, slope = gelu_pair(own[k] + into[k].astype(F32))
        act_ref[k] = act.astype(BF)
        dh_ref[k, :, mine] = (dg_ref[k] * slope).astype(BF)
        dh_copy(k).start()

        @pl.when(j > 0)
        def _():
            back(near_first(z, n, n - j))

    back(near_first(z, n, 0))
    mean, inverse = moments(stat_ref)
    normed = (mid_ref[...] - mean) * inverse
    grad = acc[...]
    stat_out[0] = sums_of(grad, grad * normed)
    exchange(stat_out, stat_in, t_send, t_recv)
    back_one, back_two = stat_out[0, :, 0:1] / D, stat_out[0, :, 1:2] / D
    dmid = cot_ref[...].astype(F32) + inverse * (grad - back_one - normed * back_two)
    dmid_ref[...] = dmid
    dy_ref[...] = dmid.astype(BF)
    gather.finish()
    swap.finish(n)
    reduce.finish()

    @pl.loop(0, n)
    def _(k):
        dh_copy(k).wait_send()


def hidden(lay, low, dg, mid, cot, stat, we):
    n, r, d, hid = lay.n_row, lay.rows, low.shape[1], dg.shape[2]
    return call(
        partial(hidden_kernel, lay),
        3,
        [
            ((n, r, d), BF),
            ((n, r, hid), BF),
            ((n, r, 2 * hid), BF),
            ((r, d), F32),
            ((r, d), BF),
        ],
        [
            pltpu.VMEM((n, r, hid), F32),
            pltpu.VMEM((n, r, hid), BF),
            pltpu.VMEM((n, r, hid), BF),
            pltpu.VMEM((r, d), F32),
            pltpu.VMEM((n, r, d), BF),
            pltpu.VMEM((2, n, r, d), BF),
            pltpu.VMEM((1, r, 128), F32),
            pltpu.VMEM((1, r, 128), F32),
            dma(2, n),
            dma(n),
            dma(n),
            dma(n),
            dma(n),
            dma(n),
            dma(n),
            dma(2, n),
            dma(1),
            dma(1),
        ],
        10**10,
        low,
        dg,
        mid,
        cot,
        stat,
        we,
    )


def adamw(gradient, moment, square, weight, clip_factor):
    clipped = gradient * clip_factor
    moment_new = BETA_ONE * moment + (1.0 - BETA_ONE) * clipped
    square_new = BETA_TWO * square + (1.0 - BETA_TWO) * clipped * clipped
    corrected = (
        moment_new
        / (1.0 - BETA_ONE**STEP)
        / (jnp.sqrt(square_new / (1.0 - BETA_TWO**STEP)) + 1e-08)
    )
    return (moment_new, square_new, -RATE * (corrected + DECAY * weight))


def weight_shard(weight, group_index, shard_rows):
    return lax.dynamic_slice_in_dim(weight, group_index * shard_rows, shard_rows, 1).astype(F32)


class Layout:
    def __init__(self, n_row, img, txt):
        self.n_row = n_row
        self.img = img
        self.txt = txt
        self.txt_pad = -(-txt // 16) * 16
        self.rows = img + self.txt_pad
        self.real = img + txt

    def pack(self, image, text):
        return jnp.concatenate(
            [image, text, jnp.zeros((self.txt_pad - self.txt, image.shape[1]), image.dtype)], 0
        )

    def mm(self, full, w, f):
        full = full.reshape(self.n_row, self.rows, -1)
        one = f(full[:, : self.img], w[0])
        two = f(full[:, self.img :], w[1])
        return jnp.concatenate([one, two], 1).reshape(self.n_row * self.rows, -1)

    def grad(self, left, right):
        left = left.reshape(self.n_row, self.rows, -1)
        right = right.reshape(self.n_row, self.rows, -1)
        parts = []
        for part in (slice(0, self.img), slice(self.img, self.rows)):
            a = left[:, part].reshape(-1, left.shape[2])
            b = right[:, part].reshape(-1, right.shape[2])
            parts.append(dot_tn(a, b))
        return jnp.stack(parts)


def row_gather(x):
    return lax.all_gather(x, "row", axis=0, tiled=True)


def row_reduce(x):
    return lax.psum_scatter(x.astype(BF), "row", scatter_dimension=0, tiled=True).astype(F32)


def col_swap(x, n_col):
    return lax.ppermute(x, "col", [(i, (i + 1) % n_col) for i in range(n_col)])


def col_reduce(x, n_col):
    c = lax.axis_index("col")
    half = x.shape[1] // 2
    mine = lax.dynamic_slice_in_dim(x, c * half, half, 1)
    other = lax.dynamic_slice_in_dim(x, (1 - c) * half, half, 1).astype(BF)
    return mine + col_swap(other, n_col).astype(F32)


def col_gather(x, n_col):
    c = lax.axis_index("col")
    other = col_swap(x, n_col)
    both = jnp.where(c == 0, jnp.stack([x, other]), jnp.stack([other, x]))
    return jnp.concatenate([both[0], both[1]], 1)


def token_sums(a, b):
    return lax.psum(jnp.stack([jnp.sum(a, 1), jnp.sum(b, 1)]), "col")


def norm_back(normed, inverse, gradient):
    sums = token_sums(gradient, gradient * normed) / D
    return inverse * (gradient - sums[0][:, None] - normed * sums[1][:, None])


def attention_backward(qkv, lse, do, heads, real, rows):
    t = qkv.shape[0]
    parts = qkv.reshape(t, heads, 3, HD)
    do = do.reshape(t, heads, HD)
    valid = (jnp.arange(t) % rows) < real
    q, k, v = parts[:, :, 0], parts[:, :, 1], parts[:, :, 2]
    s = jnp.einsum("qhd,khd->hqk", q, k, preferred_element_type=F32) * HD**-0.5
    p = jnp.where(valid[None, None], jnp.exp(s - lse), 0.0)
    dp = jnp.einsum("qhd,khd->hqk", do, v, preferred_element_type=F32)
    row_dot = jnp.sum(p * dp, axis=2, keepdims=True)
    ds = (p * (dp - row_dot)).astype(BF)
    dq = jnp.einsum("hqk,khd->qhd", ds, k, preferred_element_type=F32) * HD**-0.5
    dk = jnp.einsum("hqk,qhd->khd", ds, q, preferred_element_type=F32) * HD**-0.5
    dv = jnp.einsum("hqk,qhd->khd", p.astype(BF), do, preferred_element_type=F32)
    return jnp.stack([dq, dk, dv], 2).astype(BF).reshape(t, heads * 3 * HD)


def on_device(n_row, n_col, *args):
    (
        image_input,
        text_input,
        image_cotan,
        text_cotan,
        seq_group,
        w_attend,
        w_output,
        w_expand,
        w_reduce,
        m_attend,
        m_output,
        m_expand,
        m_reduce,
        v_attend,
        v_output,
        v_expand,
        v_reduce,
    ) = args
    img, txt = image_input.shape[1], text_input.shape[1]
    lay = Layout(n_row, img, txt)
    heads = w_attend.shape[2] // (3 * HD) // n_col
    group_index = lax.axis_index("batch")
    present = jnp.any(seq_group == group_index).astype(F32)

    low_x = lay.pack(image_input[0], text_input[0])
    low_cot = (lay.pack(image_cotan[0], text_cotan[0]).astype(F32) * present).astype(BF)
    x, cot = low_x.astype(F32), low_cot.astype(F32)
    flat = n_row * lay.rows

    a1_all, qkv, stat_one = attend(lay, low_x, w_attend)
    o_all, lse, cb_all, dg, middle_x, low_two, stat_two = middle(
        lay, qkv, low_x, low_cot, w_output, w_reduce
    )
    a2_all, act, dh_all, grad_mid, low_mid = hidden(
        lay, low_two, dg, middle_x, low_cot, stat_two, w_expand
    )
    mean, inverse_one = moments(stat_one)
    normed_one = (x - mean) * inverse_one
    a1_all, qkv, o_all, cb_all, a2_all, act, dh_all = (
        t.reshape(flat, -1) for t in (a1_all, qkv, o_all, cb_all, a2_all, act, dh_all)
    )
    lse = jnp.transpose(lse.reshape(flat, -1)[:, :heads])[:, :, None]
    g_all = col_gather(act, n_col)
    result = middle_x + row_reduce(lay.mm(g_all, w_reduce, dot))
    dy_all = row_gather(low_mid)
    do = col_reduce(lay.mm(dy_all, w_output, dot_nt), n_col).astype(BF)

    g_red = lay.grad(g_all, cb_all)
    g_exp = lay.grad(a2_all, dh_all)
    g_out = lay.grad(o_all, dy_all)
    dqkv = attention_backward(qkv, lse, do, heads, lay.real, lay.rows)
    dqkv_all = col_gather(dqkv, n_col)
    g_att = lay.grad(a1_all, dqkv_all)
    da = row_reduce(lay.mm(dqkv_all, w_attend, dot_nt))
    grad_in = grad_mid + norm_back(normed_one, inverse_one, da)

    def batch_sum(g):
        return lax.psum_scatter(g.astype(BF), "batch", scatter_dimension=1, tiled=True).astype(F32)

    sums = [batch_sum(g) for g in (g_att, g_out, g_exp, g_red)]
    squares = sum(jnp.sum(g * g) for g in sums)
    grad_norm = jnp.sqrt(lax.psum(squares, ("batch", "row", "col")))
    clip_factor = jnp.minimum(1.0, 1.0 / (grad_norm + 1e-06))
    news = []
    for g, m, v, w in zip(
        sums,
        (m_attend, m_output, m_expand, m_reduce),
        (v_attend, v_output, v_expand, v_reduce),
        (w_attend, w_output, w_expand, w_reduce),
    ):
        news.append(adamw(g, m, v, weight_shard(w, group_index, g.shape[1]), clip_factor))
    return (
        result[:img].astype(BF)[None],
        result[img : lay.real].astype(BF)[None],
        grad_in[:img][None],
        grad_in[img : lay.real][None],
        *sums,
        *[n[0] for n in news],
        *[n[1] for n in news],
        *[n[2] for n in news],
        grad_norm,
    )


def solution(mesh):
    tokens = P("batch", "row", "col")
    wide = P(None, "col", "row")
    tall = P(None, "row", "col")
    wide_shard = P(None, ("col", "batch"), "row")
    tall_shard = P(None, ("row", "batch"), "col")
    shards = (wide_shard, tall_shard, wide_shard, tall_shard)
    return jax.shard_map(
        partial(on_device, mesh.shape["row"], mesh.shape["col"]),
        mesh=mesh,
        in_specs=(*[tokens] * 4, P(), wide, tall, wide, tall, *shards, *shards),
        out_specs=(*[tokens] * 4, *shards * 4, P()),
        check_vma=False,
    )
```

```python
import math
from functools import partial

import jax
import jax.numpy as jnp
from jax import lax
from jax.experimental import pallas as pl
from jax.experimental.pallas import tpu as pltpu
from jax.sharding import PartitionSpec as P

D = 1536
HD = 64
STEP = 10
STRIPE = 512

EPSILON = 1e-06
BETA_ONE = 0.9
BETA_TWO = 0.999
RATE = 0.02
DECAY = 0.1

BF = jnp.bfloat16
F32 = jnp.float32


def dot(a, b):
    return lax.dot_general(a, b, (((a.ndim - 1,), (0,)), ((), ())), preferred_element_type=F32)


def dot_nt(a, b):
    return lax.dot_general(a, b, (((a.ndim - 1,), (1,)), ((), ())), preferred_element_type=F32)


def dot_tn(a, b):
    return lax.dot_general(a, b, (((0,), (0,)), ((), ())), preferred_element_type=F32)


MESH = pl.DeviceIdType.MESH
VMEM = pl.BlockSpec(memory_space=pltpu.VMEM)


def remote(src, dst, send, recv, **where):
    return pltpu.make_async_remote_copy(
        src_ref=src,
        dst_ref=dst,
        send_sem=send,
        recv_sem=recv,
        device_id=where,
        device_id_type=MESH,
    )


def near_first(z, n, j):
    alternate = jnp.where(j % 2 == 1, z - (j + 1) // 2, z + j // 2)
    reach = jnp.minimum(z, n - 1 - z)
    beyond = jnp.where(z <= n - 1 - z, j, n - 1 - j)
    return jnp.where(j <= 2 * reach, alternate, beyond)


def greet(n, fused=False):
    z, c = lax.axis_index("row"), lax.axis_index("col")
    barrier = pltpu.get_barrier_semaphore()
    pl.semaphore_signal(barrier, inc=1, device_id={"col": 1 - c}, device_id_type=MESH)

    @pl.when(z > 0)
    def _():
        pl.semaphore_signal(barrier, inc=1, device_id={"row": z - 1}, device_id_type=MESH)

    @pl.when(z < n - 1)
    def _():
        pl.semaphore_signal(barrier, inc=1, device_id={"row": z + 1}, device_id_type=MESH)

    if fused:
        b = lax.axis_index("batch")
        for other in (b + 1 - 2 * (b % 2), (b + 2) % 4):
            pl.semaphore_signal(barrier, inc=1, device_id={"batch": other}, device_id_type=MESH)
    ends = jnp.where(z > 0, 1, 0) + jnp.where(z < n - 1, 1, 0)
    pl.semaphore_wait(barrier, ends + (3 if fused else 1))


class Gather:
    def __init__(self, full, send, recv, n):
        self.full, self.send, self.recv, self.n = full, send, recv, n
        self.z = lax.axis_index("row")

    def copy(self, k, step):
        there = (self.z + step + self.n) % self.n
        way = 0 if step > 0 else 1
        return remote(
            self.full.at[k], self.full.at[k], self.send.at[way, k], self.recv.at[k], row=there
        )

    def push(self, k):
        @pl.when((k <= self.z) & (self.z < self.n - 1))
        def _():
            self.copy(k, 1).start()

        @pl.when((k >= self.z) & (self.z > 0))
        def _():
            self.copy(k, -1).start()

    def arrive(self, k):
        @pl.when(k != self.z)
        def _():
            self.copy(k, 1).wait_recv()

        self.push(k)

    def arrive_after_own(self, k):
        @pl.when(k != self.z)
        def _():
            self.arrive(k)

    def finish(self):
        @pl.loop(0, self.n)
        def _(k):
            @pl.when((k <= self.z) & (self.z < self.n - 1))
            def _():
                self.copy(k, 1).wait_send()

            @pl.when((k >= self.z) & (self.z > 0))
            def _():
                self.copy(k, -1).wait_send()


class Reduce:
    def __init__(self, acc, out, inbox, send, recv, n):
        self.acc, self.out, self.inbox, self.send, self.recv, self.n = acc, out, inbox, send, recv, n
        self.z = lax.axis_index("row")

    def copy(self, o):
        slot = jnp.where(o > self.z, o + 1, o)
        there = (self.z + jnp.where(o > self.z, 1, -1) + self.n) % self.n
        return remote(
            self.out.at[o], self.inbox.at[slot], self.send.at[o], self.recv.at[slot], row=there
        )

    def take(self, slot):
        remote(
            self.out.at[0],
            self.inbox.at[slot],
            self.send.at[0],
            self.recv.at[slot],
            row=(self.z + 1) % self.n,
        ).wait_recv()
        self.acc[...] += self.inbox[slot].astype(F32)

    def add(self, o):
        @pl.when((o >= self.z) & (self.z > 0))
        def _():
            self.take(o + 1)

        @pl.when((o <= self.z) & (self.z < self.n - 1))
        def _():
            self.take(o)

        @pl.when(o != self.z)
        def _():
            self.out[o] = self.acc[...].astype(BF)
            self.copy(o).start()

    def finish(self):
        @pl.loop(0, self.n)
        def _(o):
            @pl.when(o != self.z)
            def _():
                self.copy(o).wait_send()


class Swap:
    def __init__(self, out, into, send, recv):
        self.out, self.into, self.send, self.recv = out, into, send, recv

    def copy(self, k):
        return remote(
            self.out.at[k],
            self.into.at[k],
            self.send.at[k],
            self.recv.at[k],
            col=1 - lax.axis_index("col"),
        )

    def start(self, k):
        self.copy(k).start()

    def arrive(self, k):
        self.copy(k).wait_recv()

    def finish(self, n):
        @pl.loop(0, n)
        def _(k):
            self.copy(k).wait_send()


def sums_of(a, b):
    lane = lax.broadcasted_iota(jnp.int32, (a.shape[0], 128), 1)
    one, two = jnp.sum(a, axis=1, keepdims=True), jnp.sum(b, axis=1, keepdims=True)
    return jnp.where(lane == 0, one, jnp.where(lane == 1, two, 0.0))


def moments(stat):
    mean = stat[0, :, 0:1] / D
    return mean, lax.rsqrt(stat[0, :, 1:2] / D - mean * mean + EPSILON)


def exchange(stat, stat_in, send, recv):
    swap = Swap(stat, stat_in, send, recv)
    swap.start(0)
    swap.arrive(0)
    swap.finish(1)
    stat[0] += stat_in[0]


def dma(*shape):
    return pltpu.SemaphoreType.DMA(shape)


def call(kernel, ident, outs, scratch, cost, *operands):
    return pl.pallas_call(
        kernel,
        out_shape=[jax.ShapeDtypeStruct(s, t) for s, t in outs],
        in_specs=[VMEM] * len(operands),
        out_specs=[VMEM] * len(outs),
        scratch_shapes=scratch,
        compiler_params=pltpu.CompilerParams(
            collective_id=ident, has_side_effects=True, vmem_limit_bytes=60 * 2**20
        ),
        cost_estimate=pl.CostEstimate(flops=cost, bytes_accessed=10**7, transcendentals=0),
    )(*operands)


def parts_of(lay):
    return ((0, slice(0, lay.img)), (1, slice(lay.img, lay.rows)))


def attend_kernel(lay, x_ref, w_ref, full_ref, qkv_ref, stat_ref, *scratch):
    own, out, into, stat_in, g_send, g_recv, s_send, s_recv, t_send, t_recv = scratch
    n = lay.n_row
    z, c = lax.axis_index("row"), lax.axis_index("col")
    half = qkv_ref.shape[2]
    greet(n)
    x = x_ref[...].astype(F32)
    stat_ref[0] = sums_of(x, x * x)
    exchange(stat_ref, stat_in, t_send, t_recv)
    mean, inverse = moments(stat_ref)
    full_ref[z] = ((x - mean) * inverse).astype(BF)
    gather = Gather(full_ref, g_send, g_recv, n)
    swap = Swap(out, into, s_send, s_recv)

    @pl.loop(0, n)
    def _(j):
        k = near_first(z, n, j)
        gather.arrive(k)
        for part, rows in parts_of(lay):
            p = dot(full_ref[k, rows], w_ref[part])
            low, high = p[:, :half], p[:, half:]
            own[k, rows] = jnp.where(c == 0, low, high)
            out[k, rows] = jnp.where(c == 0, high, low).astype(BF)
        swap.start(k)

    @pl.loop(0, n)
    def _(j):
        k = near_first(z, n, j)
        swap.arrive(k)
        qkv_ref[k] = (own[k] + into[k].astype(F32)).astype(BF)

    gather.finish()
    swap.finish(n)


def attend(lay, x, w):
    n, r, half, d = lay.n_row, lay.rows, w.shape[2] // 2, x.shape[1]
    return call(
        partial(attend_kernel, lay),
        1,
        [((n, r, d), BF), ((n, r, half), BF), ((1, r, 128), F32)],
        [
            pltpu.VMEM((n, r, half), F32),
            pltpu.VMEM((n, r, half), BF),
            pltpu.VMEM((n, r, half), BF),
            pltpu.VMEM((1, r, 128), F32),
            dma(2, n),
            dma(n),
            dma(n),
            dma(n),
            dma(1),
            dma(1),
        ],
        2 * n * r * w.shape[1] * w.shape[2],
        x,
        w,
    )


def split_heads(lay, qkv_ref, q_ref, k_ref, v_ref, fill):
    n, img, txt = lay.n_row, lay.img, lay.txt_pad
    heads = qkv_ref.shape[2] // (3 * HD)

    @pl.loop(0, n)
    def _(k):
        first = pl.ds(pl.multiple_of(k * img, 16), img)
        second = pl.ds(pl.multiple_of(n * img + k * txt, 16), txt)
        for h in range(heads):
            at = h * 3 * HD
            rows = qkv_ref[k, :, at : at + 3 * HD]
            q_ref[h, k] = rows[:, :HD] * jnp.asarray(HD**-0.5, BF)
            for ref, lo in ((k_ref, HD), (v_ref, 2 * HD)):
                value = rows[:, lo : lo + HD]
                if ref is v_ref and fill:
                    value = jnp.concatenate([value, jnp.ones_like(value)], 1)
                ref[h, first] = value[:img]
                ref[h, second] = value[img:]


def text_bias(lay):
    lane = lax.broadcasted_iota(jnp.int32, (1, lay.n_row * lay.txt_pad), 1)
    return jnp.where(lane % lay.txt_pad < lay.txt, 0.0, -1e30)


def middle_kernel(
    lay, qkv_ref, x_ref, cot_ref, wo_ref, wr_ref, o_ref, lse_ref, cb_ref, dg_ref, mid_ref, low_ref, stat_ref, *scratch
):
    (
        q_s, k_s, v_s, o_out, o_in, dg_out, dg_in, acc, r_out, inbox, stat_in,
        g_send, g_recv, o_send, o_recv, d_send, d_recv, r_send, r_recv, t_send, t_recv,
    ) = scratch
    n, far = lay.n_row, lay.n_row * lay.img
    z, c = lax.axis_index("row"), lax.axis_index("col")
    heads, hid = q_s.shape[0], dg_ref.shape[2]
    greet(n)
    gather = Gather(cb_ref, g_send, g_recv, n)
    cb_ref[z] = cot_ref[...]
    gather.push(z)
    swap_o = Swap(o_out, o_in, o_send, o_recv)
    swap_d = Swap(dg_out, dg_in, d_send, d_recv)
    reduce = Reduce(acc, r_out, inbox, r_send, r_recv, n)
    split_heads(lay, qkv_ref, q_s, k_s, v_s, True)
    bias = text_bias(lay)
    lane = lax.broadcasted_iota(jnp.int32, (lay.rows, 128), 1)

    def attention(k):
        outs, lse = [], jnp.zeros((lay.rows, 128), F32)
        for h in range(heads):
            q = q_s[h, k]
            s1 = dot_nt(q, k_s[h, :far])
            s2 = dot_nt(q, k_s[h, far:]) + bias
            peak = jnp.maximum(
                jnp.max(s1, axis=1, keepdims=True), jnp.max(s2, axis=1, keepdims=True)
            )
            e1, e2 = jnp.exp(s1 - peak).astype(BF), jnp.exp(s2 - peak).astype(BF)
            o = dot(e1, v_s[h, :far]) + dot(e2, v_s[h, far:])
            total = o[:, HD : HD + 1]
            outs.append((o[:, :HD] / total).astype(BF))
            lse = jnp.where(lane == h, peak + jnp.log(total), lse)
        lse_ref[k] = lse
        o_out[k] = jnp.concatenate(outs, 1)

    def project(k):
        swap_o.arrive(k)
        own, other = o_out[k], o_in[k]
        o_ref[k] = jnp.concatenate(
            [jnp.where(c == 0, own, other), jnp.where(c == 0, other, own)], 1
        )
        for part, rows in parts_of(lay):
            acc[rows] = dot(o_ref[k, rows], wo_ref[part])
        reduce.add(k)

    @pl.loop(0, n)
    def _(j):
        k = near_first(z, n, n - 1 - j)
        attention(k)
        swap_o.start(k)
        near = near_first(z, n, j)
        gather.arrive_after_own(near)
        for part, rows in parts_of(lay):
            dg_out[near, rows] = dot_nt(
                cb_ref[near, rows], wr_ref[part, pl.ds(pl.multiple_of((1 - c) * hid, 128), hid), :]
            ).astype(BF)
        swap_d.start(near)
        for part, rows in parts_of(lay):
            dg_ref[near, rows] = dot_nt(
                cb_ref[near, rows], wr_ref[part, pl.ds(pl.multiple_of(c * hid, 128), hid), :]
            )

        @pl.when(j > 0)
        def _():
            project(near_first(z, n, n - j))

    project(near_first(z, n, 0))
    mid = x_ref[...].astype(F32) + acc[...]
    mid_ref[...] = mid
    stat_ref[0] = sums_of(mid, mid * mid)
    exchange(stat_ref, stat_in, t_send, t_recv)
    mean, inverse = moments(stat_ref)
    low_ref[...] = ((mid - mean) * inverse).astype(BF)

    @pl.loop(0, n)
    def _(j):
        k = near_first(z, n, j)
        swap_d.arrive(k)
        dg_ref[k] += dg_in[k].astype(F32)

    gather.finish()
    swap_o.finish(n)
    swap_d.finish(n)
    reduce.finish()


def middle(lay, qkv, x, cot, wo, wr):
    n, r, d = lay.n_row, lay.rows, x.shape[1]
    heads, hid = qkv.shape[2] // (3 * HD), wr.shape[1] // 2
    keys = n * r
    return call(
        partial(middle_kernel, lay),
        2,
        [
            ((n, r, 2 * heads * HD), BF),
            ((n, r, 128), F32),
            ((n, r, d), BF),
            ((n, r, hid), F32),
            ((r, d), F32),
            ((r, d), BF),
            ((1, r, 128), F32),
        ],
        [
            pltpu.VMEM((heads, n, r, HD), BF),
            pltpu.VMEM((heads, keys, HD), BF),
            pltpu.VMEM((heads, keys, 2 * HD), BF),
            pltpu.VMEM((n, r, heads * HD), BF),
            pltpu.VMEM((n, r, heads * HD), BF),
            pltpu.VMEM((n, r, hid), BF),
            pltpu.VMEM((n, r, hid), BF),
            pltpu.VMEM((r, d), F32),
            pltpu.VMEM((n, r, d), BF),
            pltpu.VMEM((n + 1, r, d), BF),
            pltpu.VMEM((1, r, 128), F32),
            dma(2, n),
            dma(n),
            dma(n),
            dma(n),
            dma(n),
            dma(n),
            dma(n),
            dma(n + 1),
            dma(1),
            dma(1),
        ],
        10**10,
        qkv,
        x,
        cot,
        wo,
        wr,
    )


SLOPE = (2.0 / math.pi) ** 0.5
CUBIC = 0.044715


def gelu_pair(u):
    square = u * u
    t = jnp.tanh(SLOPE * u * (1.0 + CUBIC * square))
    half = 0.5 * (1.0 + t)
    slope = half + 0.5 * u * (1.0 - t * t) * (SLOPE * (1.0 + 3.0 * CUBIC * square))
    return u * half, slope


def hidden_kernel(
    lay, low_ref, dg_ref, mid_ref, cot_ref, stat_ref, we_ref, full_ref, act_ref, dh_ref, dmid_ref, dy_ref, *scratch
):
    (
        own, out, into, acc, r_out, inbox, stat_out, stat_in,
        g_send, g_recv, s_send, s_recv, d_send, d_recv, r_send, r_recv, t_send, t_recv,
    ) = scratch
    n = lay.n_row
    z, c = lax.axis_index("row"), lax.axis_index("col")
    hid = dg_ref.shape[2]
    mine = pl.ds(pl.multiple_of(c * hid, 128), hid)
    theirs = pl.ds(pl.multiple_of((1 - c) * hid, 128), hid)
    greet(n)
    gather = Gather(full_ref, g_send, g_recv, n)
    full_ref[z] = low_ref[...]
    gather.push(z)
    swap = Swap(out, into, s_send, s_recv)
    reduce = Reduce(acc, r_out, inbox, r_send, r_recv, n)

    def dh_copy(k):
        half = dh_ref.at[k, :, mine]
        return remote(half, half, d_send.at[k], d_recv.at[k], col=1 - c)

    @pl.loop(0, n)
    def _(j):
        k = near_first(z, n, j)
        gather.arrive_after_own(k)
        for part, rows in parts_of(lay):
            out[k, rows] = dot(full_ref[k, rows], we_ref[part, :, theirs]).astype(BF)
        swap.start(k)
        for part, rows in parts_of(lay):
            own[k, rows] = dot(full_ref[k, rows], we_ref[part, :, mine])

    def back(k):
        half = dh_ref.at[k, :, theirs]
        remote(half, half, d_send.at[k], d_recv.at[k], col=1 - c).wait_recv()
        for part, rows in parts_of(lay):
            acc[rows] = dot_nt(dh_ref[k, rows], we_ref[part])
        reduce.add(k)

    @pl.loop(0, n)
    def _(j):
        k = near_first(z, n, n - 1 - j)
        swap.arrive(k)
        act, slope = gelu_pair(own[k] + into[k].astype(F32))
        act_ref[k] = act.astype(BF)
        dh_ref[k, :, mine] = (dg_ref[k] * slope).astype(BF)
        dh_copy(k).start()

        @pl.when(j > 0)
        def _():
            back(near_first(z, n, n - j))

    back(near_first(z, n, 0))
    mean, inverse = moments(stat_ref)
    normed = (mid_ref[...] - mean) * inverse
    grad = acc[...]
    stat_out[0] = sums_of(grad, grad * normed)
    exchange(stat_out, stat_in, t_send, t_recv)
    back_one, back_two = stat_out[0, :, 0:1] / D, stat_out[0, :, 1:2] / D
    dmid = cot_ref[...].astype(F32) + inverse * (grad - back_one - normed * back_two)
    dmid_ref[...] = dmid
    dy_ref[...] = dmid.astype(BF)
    gather.finish()
    swap.finish(n)
    reduce.finish()

    @pl.loop(0, n)
    def _(k):
        dh_copy(k).wait_send()


def hidden(lay, low, dg, mid, cot, stat, we):
    n, r, d, hid = lay.n_row, lay.rows, low.shape[1], dg.shape[2]
    return call(
        partial(hidden_kernel, lay),
        3,
        [
            ((n, r, d), BF),
            ((n, r, hid), BF),
            ((n, r, 2 * hid), BF),
            ((r, d), F32),
            ((r, d), BF),
        ],
        [
            pltpu.VMEM((n, r, hid), F32),
            pltpu.VMEM((n, r, hid), BF),
            pltpu.VMEM((n, r, hid), BF),
            pltpu.VMEM((r, d), F32),
            pltpu.VMEM((n, r, d), BF),
            pltpu.VMEM((n + 1, r, d), BF),
            pltpu.VMEM((1, r, 128), F32),
            pltpu.VMEM((1, r, 128), F32),
            dma(2, n),
            dma(n),
            dma(n),
            dma(n),
            dma(n),
            dma(n),
            dma(n),
            dma(n + 1),
            dma(1),
            dma(1),
        ],
        10**10,
        low,
        dg,
        mid,
        cot,
        stat,
        we,
    )


class BatchSum:
    def __init__(self, local, first, out, second, sems):
        self.local, self.first, self.out, self.second = local, first, out, second
        self.f_send, self.f_recv, self.s_send, self.s_recv = sems
        b = lax.axis_index("batch")
        self.x, self.core = b // 2, b % 2
        self.to_core, self.to_x = 2 * self.x + 1 - self.core, 2 * (1 - self.x) + self.core
        self.s = out.shape[1]

    def rows(self, block):
        return pl.ds(pl.multiple_of(block * self.s, 16), self.s)

    def core_copy(self, q):
        block = 2 * q + 1 - self.core
        return remote(
            self.local.at[:, self.rows(block), :],
            self.first.at[q],
            self.f_send.at[q],
            self.f_recv.at[q],
            batch=self.to_core,
        )

    def x_copy(self):
        return remote(self.out, self.second, self.s_send.at[0], self.s_recv.at[0], batch=self.to_x)

    def start(self):
        self.core_copy(1 - self.x).start()
        self.core_copy(self.x).start()

    def block(self, q):
        self.core_copy(q).wait_recv()
        mine = self.local[:, self.rows(2 * q + self.core), :].astype(F32)
        return mine + self.first[q].astype(F32)

    def pass_on(self):
        self.out[...] = self.block(1 - self.x).astype(BF)
        self.x_copy().start()

    def total(self):
        near = self.block(self.x)
        self.x_copy().wait_recv()
        return near + self.second[...].astype(F32)

    def finish(self):
        self.core_copy(0).wait_send()
        self.core_copy(1).wait_send()
        self.x_copy().wait_send()


def batch_scratch(rows, cols):
    s = rows // 4
    return [
        pltpu.VMEM((2, rows, cols), BF),
        pltpu.VMEM((2, 2, s, cols), BF),
        pltpu.VMEM((2, s, cols), BF),
        pltpu.VMEM((2, s, cols), BF),
        dma(2),
        dma(2),
        dma(1),
        dma(1),
    ]


def batch_of(scratch):
    return BatchSum(*scratch[:4], scratch[4:])


def transpose_rows(lay, left, turned):
    n, img, far = lay.n_row, lay.img, lay.n_row * lay.img
    for k in range(n):
        turned[:, k * img : (k + 1) * img] = left[k, :img, :].T
    turned[:, far:] = jnp.concatenate([left[k, img:, :] for k in range(n)], 0).T


def weight_gradient(lay, turned, right, local, part, cols):
    n, img, far = lay.n_row, lay.img, lay.n_row * lay.img
    if part == 0:
        total = dot(turned[:, :img], right[0, :img, cols])
        for k in range(1, n):
            total += dot(turned[:, k * img : (k + 1) * img], right[k, :img, cols])
    else:
        text = jnp.concatenate([right[k, img:, cols] for k in range(n)], 0)
        total = dot(turned[:, far:], text)
    local[part, :, cols] = total.astype(BF)


def pull_kernel(
    lay, fused, low_ref, qkv_ref, lse_ref, wo_ref, act_ref, wr_ref, mid_ref, a2_ref, dh_ref, full_ref, dqkv_ref, g_ref, res_ref, exp_ref, *scratch
):
    (
        q_s, k_s, v_s, do_own, do_out, do_in, do_s, dq_s, dk_s, dv_s, acc, r_out, inbox, turned,
        g_send, g_recv, s_send, s_recv, a_send, a_recv, r_send, r_recv,
    ) = scratch[:22]
    n, img, txt, far = lay.n_row, lay.img, lay.txt_pad, lay.n_row * lay.img
    z, c = lax.axis_index("row"), lax.axis_index("col")
    heads, half, hid = q_s.shape[0], do_own.shape[2], act_ref.shape[2]
    mine = pl.ds(pl.multiple_of(c * half, 16), half)
    theirs = pl.ds(pl.multiple_of((1 - c) * half, 16), half)
    my_act = pl.ds(pl.multiple_of(c * hid, 128), hid)
    their_act = pl.ds(pl.multiple_of((1 - c) * hid, 128), hid)
    greet(n, fused)
    gather = Gather(full_ref, g_send, g_recv, n)
    full_ref[z] = low_ref[...]
    gather.push(z)
    swap = Swap(do_out, do_in, s_send, s_recv)
    reduce = Reduce(acc, r_out, inbox, r_send, r_recv, n)
    local = exp_ref
    if fused:
        batch = batch_of(scratch[22:])
        local = batch.local
    split_heads(lay, qkv_ref, q_s, k_s, v_s, False)
    bias = text_bias(lay)
    dk_s[...] = jnp.zeros_like(dk_s)
    dv_s[...] = jnp.zeros_like(dv_s)
    lag = jnp.minimum(z, n - 1 - z)

    def act_copy(k, where):
        return remote(act_ref.at[k], g_ref.at[k, :, where], a_send.at[k], a_recv.at[k], col=1 - c)

    def arrive(k):
        gather.arrive_after_own(k)
        for part, rows in parts_of(lay):
            do_out[k, rows] = dot_nt(full_ref[k, rows], wo_ref[part, theirs, :]).astype(BF)
        swap.start(k)
        for part, rows in parts_of(lay):
            do_own[k, rows] = dot_nt(full_ref[k, rows], wo_ref[part, mine, :])

    def expand_gradient():
        transpose_rows(lay, a2_ref, turned)

        @pl.loop(0, 2 * hid // STRIPE)
        def _(i):
            cols = pl.ds(pl.multiple_of(i * STRIPE, 128), STRIPE)
            for part in range(2):
                weight_gradient(lay, turned, dh_ref, local, part, cols)

    def attention(k):
        swap.arrive(k)
        do_s[...] = (do_own[k] + do_in[k].astype(F32)).astype(BF)
        for h in range(heads):
            q, do = q_s[h, k], do_s[:, h * HD : (h + 1) * HD]
            lse = lse_ref[k, :, h : h + 1]
            p1 = jnp.exp(dot_nt(q, k_s[h, :far]) - lse)
            p2 = jnp.exp(dot_nt(q, k_s[h, far:]) + bias - lse)
            dp1 = dot_nt(do, v_s[h, :far])
            dp2 = dot_nt(do, v_s[h, far:])
            row = jnp.sum(p1 * dp1, axis=1, keepdims=True) + jnp.sum(
                p2 * dp2, axis=1, keepdims=True
            )
            ds1 = (p1 * (dp1 - row)).astype(BF)
            ds2 = (p2 * (dp2 - row)).astype(BF)
            dq_s[h, k] = dot(ds1, k_s[h, :far]) + dot(ds2, k_s[h, far:])
            dk_s[h, :, :far] += dot_tn(q, ds1)
            dk_s[h, :, far:] += dot_tn(q, ds2)
            dv_s[h, :, :far] += dot_tn(do, p1.astype(BF))
            dv_s[h, :, far:] += dot_tn(do, p2.astype(BF))

    def down(k):
        act_copy(k, their_act).wait_recv()
        g_ref[k, :, my_act] = act_ref[k]
        for part, rows in parts_of(lay):
            acc[rows] = dot(g_ref[k, rows], wr_ref[part])
        reduce.add(k)

    @pl.loop(0, n + 1 + (n - 1) // 2)
    def _(j):
        @pl.when(j < n)
        def _():
            arrive(near_first(z, n, j))
            act_copy(near_first(z, n, n - 1 - j), my_act).start()

        @pl.when(j == 0)
        def _():
            expand_gradient()
            if fused:
                batch.start()

        if fused:

            @pl.when(j == 1)
            def _():
                batch.pass_on()

        @pl.when((j > 0) & (j <= n))
        def _():
            attention(near_first(z, n, j - 1))

        i = j - 1 - lag

        @pl.when((i >= 0) & (i < n))
        def _():
            down(near_first(z, n, n - 1 - i))

    res_ref[...] = (mid_ref[...] + acc[...]).astype(BF)
    for k in range(n):
        for h in range(heads):
            at = h * 3 * HD
            for rows, first, count in (
                (slice(0, img), k * img, img),
                (slice(img, lay.rows), far + k * txt, txt),
            ):
                dk = dk_s[h, :, first : first + count].T
                dv = dv_s[h, :, first : first + count].T
                dq = dq_s[h, k, rows] * HD**-0.5
                dqkv_ref[k, rows, at : at + 3 * HD] = jnp.concatenate([dq, dk, dv], 1).astype(BF)
    if fused:
        exp_ref[...] = batch.total()
        batch.finish()
    gather.finish()
    swap.finish(n)
    reduce.finish()

    @pl.loop(0, n)
    def _(k):
        act_copy(k, my_act).wait_send()


def pull(lay, fused, low, qkv, lse, wo, act, wr, mid, a2, dh):
    n, r, d, hid = lay.n_row, lay.rows, low.shape[1], act.shape[2]
    heads = qkv.shape[2] // (3 * HD)
    keys = n * r
    return call(
        partial(pull_kernel, lay, fused),
        4,
        [
            ((n, r, d), BF),
            ((n, r, 3 * heads * HD), BF),
            ((n, r, 2 * hid), BF),
            ((r, d), BF),
            ((2, d // 4, 2 * hid), F32) if fused else ((2, d, 2 * hid), BF),
        ],
        [
            pltpu.VMEM((heads, n, r, HD), BF),
            pltpu.VMEM((heads, keys, HD), BF),
            pltpu.VMEM((heads, keys, HD), BF),
            pltpu.VMEM((n, r, heads * HD), F32),
            pltpu.VMEM((n, r, heads * HD), BF),
            pltpu.VMEM((n, r, heads * HD), BF),
            pltpu.VMEM((r, heads * HD), BF),
            pltpu.VMEM((heads, n, r, HD), F32),
            pltpu.VMEM((heads, HD, keys), F32),
            pltpu.VMEM((heads, HD, keys), F32),
            pltpu.VMEM((r, d), F32),
            pltpu.VMEM((n, r, d), BF),
            pltpu.VMEM((n + 1, r, d), BF),
            pltpu.VMEM((d, keys), BF),
            dma(2, n),
            dma(n),
            dma(n),
            dma(n),
            dma(n),
            dma(n),
            dma(n),
            dma(n + 1),
            *(batch_scratch(d, 2 * hid) if fused else []),
        ],
        10**10,
        low,
        qkv,
        lse,
        wo,
        act,
        wr,
        mid,
        a2,
        dh,
    )


def input_kernel(
    lay, fused, dqkv_ref, x_ref, dmid_ref, stat_ref, wa_ref, a1_ref, o_ref, dy_ref, g_ref, cb_ref, dx_ref, att_ref, out_ref, red_ref, *scratch
):
    (
        full, into, acc, r_out, inbox, stat_out, stat_in, turned, turned_g,
        s_send, s_recv, r_send, r_recv, t_send, t_recv,
    ) = scratch[:15]
    n = lay.n_row
    z, c = lax.axis_index("row"), lax.axis_index("col")
    half, d = dqkv_ref.shape[2], x_ref.shape[1]
    greet(n, fused)
    swap = Swap(dqkv_ref, into, s_send, s_recv)
    reduce = Reduce(acc, r_out, inbox, r_send, r_recv, n)
    own, other, red, out = (scratch[15 + 8 * i : 23 + 8 * i] for i in range(4)) if fused else (
        scratch[15:16], scratch[16:17], (red_ref,), (out_ref,)
    )
    sums = [batch_of(s) for s in (own, other, red, out)] if fused else []

    @pl.loop(0, n)
    def _(j):
        swap.start(near_first(z, n, n - 1 - j))

    def gradient(turned, right, local, stripe):
        if stripe == right.shape[2]:
            for part in range(2):
                weight_gradient(lay, turned, right, local, part, slice(0, stripe))
            return

        @pl.loop(0, right.shape[2] // stripe)
        def _(i):
            cols = pl.ds(pl.multiple_of(i * stripe, 128), stripe)
            for part in range(2):
                weight_gradient(lay, turned, right, local, part, cols)

    transpose_rows(lay, a1_ref, turned)
    gradient(turned, dqkv_ref, own[0], half)
    if fused:
        sums[0].start()
    transpose_rows(lay, g_ref, turned_g)
    gradient(turned_g, cb_ref, red[0], STRIPE // 2)
    if fused:
        sums[2].start()
        sums[0].pass_on()
    lag = jnp.minimum(z, n - 1 - z)

    @pl.loop(0, n + (n - 1) // 2)
    def _(j):
        i = j - lag

        @pl.when((i >= 0) & (i < n))
        def _():
            k = near_first(z, n, n - 1 - i)
            swap.arrive(k)
            mine, theirs = dqkv_ref[k], into[k]
            full[...] = jnp.concatenate(
                [jnp.where(c == 0, mine, theirs), jnp.where(c == 0, theirs, mine)], 1
            )
            for part, rows in parts_of(lay):
                acc[rows] = dot_nt(full[rows], wa_ref[part])
            reduce.add(k)

        if fused:

            @pl.when(j == 0)
            def _():
                sums[2].pass_on()

        @pl.when(j == 2)
        def _():
            turned_o = turned_g.at[: o_ref.shape[2]]
            transpose_rows(lay, o_ref, turned_o)
            gradient(turned_o, dy_ref, out[0], d)
            if fused:
                sums[3].start()

    gradient(turned, into, other[0], half)
    if fused:
        sums[1].start()
        sums[3].pass_on()
    mean, inverse = moments(stat_ref)
    normed = (x_ref[...].astype(F32) - mean) * inverse
    grad = acc[...]
    stat_out[0] = sums_of(grad, grad * normed)
    exchange(stat_out, stat_in, t_send, t_recv)
    back_one, back_two = stat_out[0, :, 0:1] / D, stat_out[0, :, 1:2] / D
    dx_ref[...] = dmid_ref[...] + inverse * (grad - back_one - normed * back_two)
    if fused:
        sums[1].pass_on()
        red_ref[...] = sums[2].total()
        out_ref[...] = sums[3].total()
        mine, theirs = sums[0].total(), sums[1].total()
    else:
        mine, theirs = own[0][...], other[0][...]
    att_ref[...] = jnp.concatenate(
        [jnp.where(c == 0, mine, theirs), jnp.where(c == 0, theirs, mine)], 2
    )
    for total in sums:
        total.finish()
    swap.finish(n)
    reduce.finish()


def inputs_back(lay, fused, dqkv, x, dmid, stat, wa, a1, o, dy, g, cb):
    n, r, d, half = lay.n_row, lay.rows, x.shape[1], dqkv.shape[2]
    keys = n * r
    shapes = [(d, 2 * half), (o.shape[2], d), (g.shape[2], d)]
    return call(
        partial(input_kernel, lay, fused),
        5,
        [
            ((r, d), F32),
            *[((2, s[0] // 4, s[1]), F32) if fused else ((2, *s), BF) for s in shapes],
        ],
        [
            pltpu.VMEM((r, 2 * half), BF),
            pltpu.VMEM((n, r, half), BF),
            pltpu.VMEM((r, d), F32),
            pltpu.VMEM((n, r, d), BF),
            pltpu.VMEM((n + 1, r, d), BF),
            pltpu.VMEM((1, r, 128), F32),
            pltpu.VMEM((1, r, 128), F32),
            pltpu.VMEM((d, keys), BF),
            pltpu.VMEM((g.shape[2], keys), BF),
            dma(n),
            dma(n),
            dma(n),
            dma(n + 1),
            dma(1),
            dma(1),
            *(
                [
                    *batch_scratch(d, half),
                    *batch_scratch(d, half),
                    *batch_scratch(g.shape[2], d),
                    *batch_scratch(o.shape[2], d),
                ]
                if fused
                else [pltpu.VMEM((2, d, half), BF)] * 2
            ),
        ],
        10**10,
        dqkv,
        x,
        dmid,
        stat,
        wa,
        a1,
        o,
        dy,
        g,
        cb,
    )


def adamw(gradient, moment, square, weight, clip_factor):
    clipped = gradient * clip_factor
    moment_new = BETA_ONE * moment + (1.0 - BETA_ONE) * clipped
    square_new = BETA_TWO * square + (1.0 - BETA_TWO) * clipped * clipped
    corrected = (
        moment_new
        / (1.0 - BETA_ONE**STEP)
        / (jnp.sqrt(square_new / (1.0 - BETA_TWO**STEP)) + 1e-08)
    )
    return (moment_new, square_new, -RATE * (corrected + DECAY * weight))


def weight_shard(weight, group_index, shard_rows):
    return lax.dynamic_slice_in_dim(weight, group_index * shard_rows, shard_rows, 1).astype(F32)


class Layout:
    def __init__(self, n_row, img, txt):
        self.n_row = n_row
        self.img = img
        self.txt = txt
        self.txt_pad = -(-txt // 16) * 16
        self.rows = img + self.txt_pad
        self.real = img + txt

    def pack(self, image, text):
        return jnp.concatenate(
            [image, text, jnp.zeros((self.txt_pad - self.txt, image.shape[1]), image.dtype)], 0
        )


def on_device(n_batch, n_row, *args):
    (
        image_input,
        text_input,
        image_cotan,
        text_cotan,
        seq_group,
        w_attend,
        w_output,
        w_expand,
        w_reduce,
        m_attend,
        m_output,
        m_expand,
        m_reduce,
        v_attend,
        v_output,
        v_expand,
        v_reduce,
    ) = args
    img, txt = image_input.shape[1], text_input.shape[1]
    lay = Layout(n_row, img, txt)
    group_index = lax.axis_index("batch")
    present = jnp.any(seq_group == group_index).astype(F32)

    low_x = lay.pack(image_input[0], text_input[0])
    low_cot = (lay.pack(image_cotan[0], text_cotan[0]).astype(F32) * present).astype(BF)
    fused = n_batch == 4

    a1_all, qkv, stat_one = attend(lay, low_x, w_attend)
    o_all, lse, cb_all, dg, middle_x, low_two, stat_two = middle(
        lay, qkv, low_x, low_cot, w_output, w_reduce
    )
    a2_all, act, dh_all, grad_mid, low_mid = hidden(
        lay, low_two, dg, middle_x, low_cot, stat_two, w_expand
    )
    dy_all, dqkv, g_all, result, g_exp = pull(
        lay, fused, low_mid, qkv, lse, w_output, act, w_reduce, middle_x, a2_all, dh_all
    )
    grad_in, g_att, g_out, g_red = inputs_back(
        lay, fused, dqkv, low_x, grad_mid, stat_one, w_attend, a1_all, o_all, dy_all, g_all, cb_all
    )
    sums = [g_att, g_out, g_exp, g_red]
    if not fused:
        sums = [
            lax.psum_scatter(g, "batch", scatter_dimension=1, tiled=True).astype(F32) for g in sums
        ]
    squares = sum(jnp.sum(g * g) for g in sums)
    grad_norm = jnp.sqrt(lax.psum(lax.psum(lax.psum(squares, "batch"), "row"), "col"))
    clip_factor = jnp.minimum(1.0, 1.0 / (grad_norm + 1e-06))
    news = []
    for g, m, v, w in zip(
        sums,
        (m_attend, m_output, m_expand, m_reduce),
        (v_attend, v_output, v_expand, v_reduce),
        (w_attend, w_output, w_expand, w_reduce),
    ):
        news.append(adamw(g, m, v, weight_shard(w, group_index, g.shape[1]), clip_factor))
    return (
        result[:img][None],
        result[img : lay.real][None],
        grad_in[:img][None],
        grad_in[img : lay.real][None],
        *sums,
        *[n[0] for n in news],
        *[n[1] for n in news],
        *[n[2] for n in news],
        grad_norm,
    )


def solution(mesh):
    tokens = P("batch", "row", "col")
    wide = P(None, "col", "row")
    tall = P(None, "row", "col")
    wide_shard = P(None, ("col", "batch"), "row")
    tall_shard = P(None, ("row", "batch"), "col")
    shards = (wide_shard, tall_shard, wide_shard, tall_shard)
    return jax.shard_map(
        partial(on_device, mesh.shape["batch"], mesh.shape["row"]),
        mesh=mesh,
        in_specs=(*[tokens] * 4, P(), wide, tall, wide, tall, *shards, *shards),
        out_specs=(*[tokens] * 4, *shards * 4, P()),
        check_vma=False,
    )
```

```python
import math
from functools import partial

import jax
import jax.numpy as jnp
from jax import lax
from jax.experimental import pallas as pl
from jax.experimental.pallas import tpu as pltpu
from jax.sharding import PartitionSpec as P

D = 1536
HD = 64
STEP = 10
STRIPE = 512

EPSILON = 1e-06
BETA_ONE = 0.9
BETA_TWO = 0.999
RATE = 0.02
DECAY = 0.1

BF = jnp.bfloat16
F32 = jnp.float32


def dot(a, b):
    return lax.dot_general(a, b, (((a.ndim - 1,), (0,)), ((), ())), preferred_element_type=F32)


def dot_nt(a, b):
    return lax.dot_general(a, b, (((a.ndim - 1,), (1,)), ((), ())), preferred_element_type=F32)


def dot_tn(a, b):
    return lax.dot_general(a, b, (((0,), (0,)), ((), ())), preferred_element_type=F32)


MESH = pl.DeviceIdType.MESH
VMEM = pl.BlockSpec(memory_space=pltpu.VMEM)
ANY = pl.BlockSpec(memory_space=pl.ANY)


def remote(src, dst, send, recv, **where):
    return pltpu.make_async_remote_copy(
        src_ref=src,
        dst_ref=dst,
        send_sem=send,
        recv_sem=recv,
        device_id=where,
        device_id_type=MESH,
    )


def near_first(z, n, j):
    alternate = jnp.where(j % 2 == 1, z - (j + 1) // 2, z + j // 2)
    reach = jnp.minimum(z, n - 1 - z)
    beyond = jnp.where(z <= n - 1 - z, j, n - 1 - j)
    return jnp.where(j <= 2 * reach, alternate, beyond)


def greet(n, fused=False, more=()):
    z, c = lax.axis_index("row"), lax.axis_index("col")
    barrier = pltpu.get_barrier_semaphore()
    pl.semaphore_signal(barrier, inc=1, device_id={"col": 1 - c}, device_id_type=MESH)

    @pl.when(z > 0)
    def _():
        pl.semaphore_signal(barrier, inc=1, device_id={"row": z - 1}, device_id_type=MESH)

    @pl.when(z < n - 1)
    def _():
        pl.semaphore_signal(barrier, inc=1, device_id={"row": z + 1}, device_id_type=MESH)

    if fused:
        b = lax.axis_index("batch")
        for other in (b + 1 - 2 * (b % 2), (b + 2) % 4):
            pl.semaphore_signal(barrier, inc=1, device_id={"batch": other}, device_id_type=MESH)
    ends = jnp.where(z > 0, 1, 0) + jnp.where(z < n - 1, 1, 0)
    for where in more:
        pl.semaphore_signal(barrier, inc=1, device_id=where, device_id_type=MESH)
    pl.semaphore_wait(barrier, ends + (3 if fused else 1) + len(more))


class Gather:
    def __init__(self, full, send, recv, n):
        self.full, self.send, self.recv, self.n = full, send, recv, n
        self.z = lax.axis_index("row")

    def copy(self, k, step):
        there = (self.z + step + self.n) % self.n
        way = 0 if step > 0 else 1
        return remote(
            self.full.at[k], self.full.at[k], self.send.at[way, k], self.recv.at[k], row=there
        )

    def push(self, k):
        @pl.when((k <= self.z) & (self.z < self.n - 1))
        def _():
            self.copy(k, 1).start()

        @pl.when((k >= self.z) & (self.z > 0))
        def _():
            self.copy(k, -1).start()

    def arrive(self, k):
        @pl.when(k != self.z)
        def _():
            self.copy(k, 1).wait_recv()

        self.push(k)

    def arrive_after_own(self, k):
        @pl.when(k != self.z)
        def _():
            self.arrive(k)

    def finish(self):
        @pl.loop(0, self.n)
        def _(k):
            @pl.when((k <= self.z) & (self.z < self.n - 1))
            def _():
                self.copy(k, 1).wait_send()

            @pl.when((k >= self.z) & (self.z > 0))
            def _():
                self.copy(k, -1).wait_send()


class Reduce:
    def __init__(self, acc, out, inbox, send, recv, n):
        self.acc, self.out, self.inbox, self.send, self.recv, self.n = acc, out, inbox, send, recv, n
        self.z = lax.axis_index("row")

    def copy(self, o):
        slot = jnp.where(o > self.z, o + 1, o)
        there = (self.z + jnp.where(o > self.z, 1, -1) + self.n) % self.n
        return remote(
            self.out.at[o], self.inbox.at[slot], self.send.at[o], self.recv.at[slot], row=there
        )

    def take(self, slot):
        remote(
            self.out.at[0],
            self.inbox.at[slot],
            self.send.at[0],
            self.recv.at[slot],
            row=(self.z + 1) % self.n,
        ).wait_recv()
        self.acc[...] += self.inbox[slot].astype(F32)

    def add(self, o):
        @pl.when((o >= self.z) & (self.z > 0))
        def _():
            self.take(o + 1)

        @pl.when((o <= self.z) & (self.z < self.n - 1))
        def _():
            self.take(o)

        @pl.when(o != self.z)
        def _():
            self.out[o] = self.acc[...].astype(BF)
            self.copy(o).start()

    def finish(self):
        @pl.loop(0, self.n)
        def _(o):
            @pl.when(o != self.z)
            def _():
                self.copy(o).wait_send()


class Swap:
    def __init__(self, out, into, send, recv):
        self.out, self.into, self.send, self.recv = out, into, send, recv

    def copy(self, k):
        return remote(
            self.out.at[k],
            self.into.at[k],
            self.send.at[k],
            self.recv.at[k],
            col=1 - lax.axis_index("col"),
        )

    def start(self, k):
        self.copy(k).start()

    def arrive(self, k):
        self.copy(k).wait_recv()

    def finish(self, n):
        @pl.loop(0, n)
        def _(k):
            self.copy(k).wait_send()


def sums_of(a, b):
    lane = lax.broadcasted_iota(jnp.int32, (a.shape[0], 128), 1)
    one, two = jnp.sum(a, axis=1, keepdims=True), jnp.sum(b, axis=1, keepdims=True)
    return jnp.where(lane == 0, one, jnp.where(lane == 1, two, 0.0)).T[:8]


def columns(stat):
    rows = stat[0]
    turned = jnp.concatenate([rows, jnp.zeros((120, rows.shape[1]), F32)], 0).T
    return turned[:, 0:1] / D, turned[:, 1:2] / D


def moments(stat):
    mean, square = columns(stat)
    return mean, lax.rsqrt(square - mean * mean + EPSILON)


def exchange(stat, stat_in, send, recv):
    swap = Swap(stat, stat_in, send, recv)
    swap.start(0)
    swap.arrive(0)
    swap.finish(1)
    stat[0] += stat_in[0]


def dma(*shape):
    return pltpu.SemaphoreType.DMA(shape)


def call(kernel, ident, outs, scratch, cost, *operands, far=()):
    return pl.pallas_call(
        kernel,
        out_shape=[jax.ShapeDtypeStruct(s, t) for s, t in outs],
        in_specs=[ANY if i in far else VMEM for i in range(len(operands))],
        out_specs=[VMEM] * len(outs),
        scratch_shapes=scratch,
        compiler_params=pltpu.CompilerParams(
            collective_id=ident, has_side_effects=True, vmem_limit_bytes=60 * 2**20
        ),
        cost_estimate=pl.CostEstimate(flops=cost, bytes_accessed=10**7, transcendentals=0),
    )(*operands)


def parts_of(lay):
    return ((0, slice(0, lay.img)), (1, slice(lay.img, lay.rows)))


def attend_kernel(lay, x_ref, w_ref, full_ref, qkv_ref, stat_ref, *scratch):
    own, out, into, stat_in, g_send, g_recv, s_send, s_recv, t_send, t_recv = scratch
    n = lay.n_row
    z, c = lax.axis_index("row"), lax.axis_index("col")
    half = qkv_ref.shape[2]
    greet(n)
    x = x_ref[...].astype(F32)
    stat_ref[0] = sums_of(x, x * x)
    exchange(stat_ref, stat_in, t_send, t_recv)
    mean, inverse = moments(stat_ref)
    full_ref[z] = ((x - mean) * inverse).astype(BF)
    gather = Gather(full_ref, g_send, g_recv, n)
    swap = Swap(out, into, s_send, s_recv)

    @pl.loop(0, n)
    def _(j):
        k = near_first(z, n, j)
        gather.arrive(k)
        for part, rows in parts_of(lay):
            p = dot(full_ref[k, rows], w_ref[part])
            low, high = p[:, :half], p[:, half:]
            own[k, rows] = jnp.where(c == 0, low, high)
            out[k, rows] = jnp.where(c == 0, high, low).astype(BF)
        swap.start(k)

    @pl.loop(0, n)
    def _(j):
        k = near_first(z, n, j)
        swap.arrive(k)
        qkv_ref[k] = (own[k] + into[k].astype(F32)).astype(BF)

    gather.finish()
    swap.finish(n)


def attend(lay, x, w):
    n, r, half, d = lay.n_row, lay.rows, w.shape[2] // 2, x.shape[1]
    return call(
        partial(attend_kernel, lay),
        1,
        [((n, r, d), BF), ((n, r, half), BF), ((1, 8, r), F32)],
        [
            pltpu.VMEM((n, r, half), F32),
            pltpu.VMEM((n, r, half), BF),
            pltpu.VMEM((n, r, half), BF),
            pltpu.VMEM((1, 8, r), F32),
            dma(2, n),
            dma(n),
            dma(n),
            dma(n),
            dma(1),
            dma(1),
        ],
        2 * n * r * w.shape[1] * w.shape[2],
        x,
        w,
    )


def split_heads(lay, qkv_ref, q_ref, k_ref, v_ref, fill):
    n, img, txt = lay.n_row, lay.img, lay.txt_pad
    heads = qkv_ref.shape[2] // (3 * HD)

    @pl.loop(0, n)
    def _(k):
        first = pl.ds(pl.multiple_of(k * img, 16), img)
        second = pl.ds(pl.multiple_of(n * img + k * txt, 16), txt)
        for h in range(heads):
            at = h * 3 * HD
            rows = qkv_ref[k, :, at : at + 3 * HD]
            q_ref[h, k] = rows[:, :HD] * jnp.asarray(HD**-0.5, BF)
            for ref, lo in ((k_ref, HD), (v_ref, 2 * HD)):
                value = rows[:, lo : lo + HD]
                if ref is v_ref and fill:
                    value = jnp.concatenate([value, jnp.ones_like(value)], 1)
                ref[h, first] = value[:img]
                ref[h, second] = value[img:]


def text_bias(lay):
    lane = lax.broadcasted_iota(jnp.int32, (1, lay.n_row * lay.txt_pad), 1)
    return jnp.where(lane % lay.txt_pad < lay.txt, 0.0, -1e30)


def middle_kernel(
    lay, qkv_ref, x_ref, cot_ref, wo_ref, wr_ref, o_ref, lse_ref, cb_ref, dg_ref, mid_ref, low_ref, stat_ref, *scratch
):
    (
        q_s, k_s, v_s, o_out, o_in, dg_out, dg_in, acc, r_out, inbox, stat_in,
        g_send, g_recv, o_send, o_recv, d_send, d_recv, r_send, r_recv, t_send, t_recv,
    ) = scratch
    n, far = lay.n_row, lay.n_row * lay.img
    z, c = lax.axis_index("row"), lax.axis_index("col")
    heads, hid = q_s.shape[0], dg_ref.shape[2]
    greet(n)
    gather = Gather(cb_ref, g_send, g_recv, n)
    cb_ref[z] = cot_ref[...]
    gather.push(z)
    swap_o = Swap(o_out, o_in, o_send, o_recv)
    swap_d = Swap(dg_out, dg_in, d_send, d_recv)
    reduce = Reduce(acc, r_out, inbox, r_send, r_recv, n)
    split_heads(lay, qkv_ref, q_s, k_s, v_s, True)
    bias = text_bias(lay)
    lane = lax.broadcasted_iota(jnp.int32, (lay.rows, 128), 1)

    def attention(k):
        outs, lse = [], jnp.zeros((lay.rows, 128), F32)
        for h in range(heads):
            q = q_s[h, k]
            s1 = dot_nt(q, k_s[h, :far])
            s2 = dot_nt(q, k_s[h, far:]) + bias
            peak = jnp.maximum(
                jnp.max(s1, axis=1, keepdims=True), jnp.max(s2, axis=1, keepdims=True)
            )
            e1, e2 = jnp.exp(s1 - peak).astype(BF), jnp.exp(s2 - peak).astype(BF)
            o = dot(e1, v_s[h, :far]) + dot(e2, v_s[h, far:])
            total = o[:, HD : HD + 1]
            outs.append((o[:, :HD] / total).astype(BF))
            lse = jnp.where(lane == h, peak + jnp.log(total), lse)
        lse_ref[k] = lse
        o_out[k] = jnp.concatenate(outs, 1)

    def project(k):
        swap_o.arrive(k)
        own, other = o_out[k], o_in[k]
        o_ref[k] = jnp.concatenate(
            [jnp.where(c == 0, own, other), jnp.where(c == 0, other, own)], 1
        )
        for part, rows in parts_of(lay):
            acc[rows] = dot(o_ref[k, rows], wo_ref[part])
        reduce.add(k)

    @pl.loop(0, n)
    def _(j):
        k = near_first(z, n, n - 1 - j)
        attention(k)
        swap_o.start(k)
        near = near_first(z, n, j)
        gather.arrive_after_own(near)
        for part, rows in parts_of(lay):
            dg_out[near, rows] = dot_nt(
                cb_ref[near, rows], wr_ref[part, pl.ds(pl.multiple_of((1 - c) * hid, 128), hid), :]
            ).astype(BF)
        swap_d.start(near)
        for part, rows in parts_of(lay):
            dg_ref[near, rows] = dot_nt(
                cb_ref[near, rows], wr_ref[part, pl.ds(pl.multiple_of(c * hid, 128), hid), :]
            )

        @pl.when(j > 0)
        def _():
            project(near_first(z, n, n - j))

    project(near_first(z, n, 0))
    mid = x_ref[...].astype(F32) + acc[...]
    mid_ref[...] = mid
    stat_ref[0] = sums_of(mid, mid * mid)
    exchange(stat_ref, stat_in, t_send, t_recv)
    mean, inverse = moments(stat_ref)
    low_ref[...] = ((mid - mean) * inverse).astype(BF)

    @pl.loop(0, n)
    def _(j):
        k = near_first(z, n, j)
        swap_d.arrive(k)
        dg_ref[k] += dg_in[k].astype(F32)

    gather.finish()
    swap_o.finish(n)
    swap_d.finish(n)
    reduce.finish()


def middle(lay, qkv, x, cot, wo, wr):
    n, r, d = lay.n_row, lay.rows, x.shape[1]
    heads, hid = qkv.shape[2] // (3 * HD), wr.shape[1] // 2
    keys = n * r
    return call(
        partial(middle_kernel, lay),
        2,
        [
            ((n, r, 2 * heads * HD), BF),
            ((n, r, 128), F32),
            ((n, r, d), BF),
            ((n, r, hid), F32),
            ((r, d), F32),
            ((r, d), BF),
            ((1, 8, r), F32),
        ],
        [
            pltpu.VMEM((heads, n, r, HD), BF),
            pltpu.VMEM((heads, keys, HD), BF),
            pltpu.VMEM((heads, keys, 2 * HD), BF),
            pltpu.VMEM((n, r, heads * HD), BF),
            pltpu.VMEM((n, r, heads * HD), BF),
            pltpu.VMEM((n, r, hid), BF),
            pltpu.VMEM((n, r, hid), BF),
            pltpu.VMEM((r, d), F32),
            pltpu.VMEM((n, r, d), BF),
            pltpu.VMEM((n + 1, r, d), BF),
            pltpu.VMEM((1, 8, r), F32),
            dma(2, n),
            dma(n),
            dma(n),
            dma(n),
            dma(n),
            dma(n),
            dma(n),
            dma(n + 1),
            dma(1),
            dma(1),
        ],
        10**10,
        qkv,
        x,
        cot,
        wo,
        wr,
    )


SLOPE = (2.0 / math.pi) ** 0.5
CUBIC = 0.044715


def gelu_pair(u):
    square = u * u
    t = jnp.tanh(SLOPE * u * (1.0 + CUBIC * square))
    half = 0.5 * (1.0 + t)
    slope = half + 0.5 * u * (1.0 - t * t) * (SLOPE * (1.0 + 3.0 * CUBIC * square))
    return u * half, slope


def hidden_kernel(
    lay, low_ref, dg_ref, mid_ref, cot_ref, stat_ref, we_ref, full_ref, act_ref, dh_ref, dmid_ref, dy_ref, *scratch
):
    (
        own, out, into, acc, r_out, inbox, stat_out, stat_in,
        g_send, g_recv, s_send, s_recv, d_send, d_recv, r_send, r_recv, t_send, t_recv,
    ) = scratch
    n = lay.n_row
    z, c = lax.axis_index("row"), lax.axis_index("col")
    hid = dg_ref.shape[2]
    mine = pl.ds(pl.multiple_of(c * hid, 128), hid)
    theirs = pl.ds(pl.multiple_of((1 - c) * hid, 128), hid)
    greet(n)
    gather = Gather(full_ref, g_send, g_recv, n)
    full_ref[z] = low_ref[...]
    gather.push(z)
    swap = Swap(out, into, s_send, s_recv)
    reduce = Reduce(acc, r_out, inbox, r_send, r_recv, n)

    def dh_copy(k):
        half = dh_ref.at[k, :, mine]
        return remote(half, half, d_send.at[k], d_recv.at[k], col=1 - c)

    @pl.loop(0, n)
    def _(j):
        k = near_first(z, n, j)
        gather.arrive_after_own(k)
        for part, rows in parts_of(lay):
            out[k, rows] = dot(full_ref[k, rows], we_ref[part, :, theirs]).astype(BF)
        swap.start(k)
        for part, rows in parts_of(lay):
            own[k, rows] = dot(full_ref[k, rows], we_ref[part, :, mine])

    def back(k):
        half = dh_ref.at[k, :, theirs]
        remote(half, half, d_send.at[k], d_recv.at[k], col=1 - c).wait_recv()
        for part, rows in parts_of(lay):
            acc[rows] = dot_nt(dh_ref[k, rows], we_ref[part])
        reduce.add(k)

    @pl.loop(0, n)
    def _(j):
        k = near_first(z, n, n - 1 - j)
        swap.arrive(k)
        act, slope = gelu_pair(own[k] + into[k].astype(F32))
        act_ref[k] = act.astype(BF)
        dh_ref[k, :, mine] = (dg_ref[k] * slope).astype(BF)
        dh_copy(k).start()

        @pl.when(j > 0)
        def _():
            back(near_first(z, n, n - j))

    back(near_first(z, n, 0))
    mean, inverse = moments(stat_ref)
    normed = (mid_ref[...] - mean) * inverse
    grad = acc[...]
    stat_out[0] = sums_of(grad, grad * normed)
    exchange(stat_out, stat_in, t_send, t_recv)
    back_one, back_two = columns(stat_out)
    dmid = cot_ref[...].astype(F32) + inverse * (grad - back_one - normed * back_two)
    dmid_ref[...] = dmid
    dy_ref[...] = dmid.astype(BF)
    gather.finish()
    swap.finish(n)
    reduce.finish()

    @pl.loop(0, n)
    def _(k):
        dh_copy(k).wait_send()


def hidden(lay, low, dg, mid, cot, stat, we):
    n, r, d, hid = lay.n_row, lay.rows, low.shape[1], dg.shape[2]
    return call(
        partial(hidden_kernel, lay),
        3,
        [
            ((n, r, d), BF),
            ((n, r, hid), BF),
            ((n, r, 2 * hid), BF),
            ((r, d), F32),
            ((r, d), BF),
        ],
        [
            pltpu.VMEM((n, r, hid), F32),
            pltpu.VMEM((n, r, hid), BF),
            pltpu.VMEM((n, r, hid), BF),
            pltpu.VMEM((r, d), F32),
            pltpu.VMEM((n, r, d), BF),
            pltpu.VMEM((n + 1, r, d), BF),
            pltpu.VMEM((1, 8, r), F32),
            pltpu.VMEM((1, 8, r), F32),
            dma(2, n),
            dma(n),
            dma(n),
            dma(n),
            dma(n),
            dma(n),
            dma(n),
            dma(n + 1),
            dma(1),
            dma(1),
        ],
        10**10,
        low,
        dg,
        mid,
        cot,
        stat,
        we,
    )


class BatchSum:
    def __init__(self, local, first, out, second, sems):
        self.local, self.first, self.out, self.second = local, first, out, second
        self.f_send, self.f_recv, self.s_send, self.s_recv = sems
        b = lax.axis_index("batch")
        self.x, self.core = b // 2, b % 2
        self.to_core, self.to_x = 2 * self.x + 1 - self.core, 2 * (1 - self.x) + self.core
        self.s = out.shape[1]

    def rows(self, block):
        return pl.ds(pl.multiple_of(block * self.s, 16), self.s)

    def core_copy(self, q):
        block = 2 * q + 1 - self.core
        return remote(
            self.local.at[:, self.rows(block), :],
            self.first.at[q],
            self.f_send.at[q],
            self.f_recv.at[q],
            batch=self.to_core,
        )

    def x_copy(self):
        return remote(self.out, self.second, self.s_send.at[0], self.s_recv.at[0], batch=self.to_x)

    def start(self):
        self.core_copy(1 - self.x).start()
        self.core_copy(self.x).start()

    def block(self, q):
        self.core_copy(q).wait_recv()
        mine = self.local[:, self.rows(2 * q + self.core), :].astype(F32)
        return mine + self.first[q].astype(F32)

    def pass_on(self):
        self.out[...] = self.block(1 - self.x).astype(BF)
        self.x_copy().start()

    def total(self):
        near = self.block(self.x)
        self.x_copy().wait_recv()
        return near + self.second[...].astype(F32)

    def finish(self):
        self.core_copy(0).wait_send()
        self.core_copy(1).wait_send()
        self.x_copy().wait_send()


def batch_scratch(rows, cols):
    s = rows // 4
    return [
        pltpu.VMEM((2, rows, cols), BF),
        pltpu.VMEM((2, 2, s, cols), BF),
        pltpu.VMEM((2, s, cols), BF),
        pltpu.VMEM((2, s, cols), BF),
        dma(2),
        dma(2),
        dma(1),
        dma(1),
    ]


def batch_of(scratch):
    return BatchSum(*scratch[:4], scratch[4:])


def squares_of(ref):
    total = jnp.zeros((1, 1), F32)
    for m in range(2):
        lanes = jnp.sum(ref[m] * ref[m], axis=0, keepdims=True)
        total += jnp.sum(lanes, axis=1, keepdims=True)
    return jnp.broadcast_to(total, (8, 128))


class Norm:
    def __init__(self, n_batch, n_row, plane, line, p_send, p_recv, b_send, b_recv):
        self.n_batch, self.plane, self.line = n_batch, plane, line
        self.p_send, self.p_recv, self.b_send, self.b_recv = p_send, p_recv, b_send, b_recv
        self.b, z, c = lax.axis_index("batch"), lax.axis_index("row"), lax.axis_index("col")
        self.me = z * 2 + c
        self.peers = [((z + i) % n_row, (c + j) % 2) for i in range(n_row) for j in range(2)][1:]

    def where(self):
        return [{"row": row, "col": col} for row, col in self.peers] + [
            {"batch": (self.b + i) % self.n_batch} for i in range(1, self.n_batch)
        ]

    def to_plane(self, i, slot):
        row, col = self.peers[i]
        block = self.plane.at[slot]
        return remote(block, block, self.p_send.at[i], self.p_recv.at[slot], row=row, col=col)

    def to_line(self, i, slot):
        block = self.line.at[slot]
        other = (self.b + i) % self.n_batch
        return remote(block, block, self.b_send.at[i], self.b_recv.at[slot], batch=other)

    def total(self, tile):
        b, n_batch = self.b, self.n_batch
        self.plane[self.me] = tile
        for i in range(len(self.peers)):
            self.to_plane(i, self.me).start()
        for i, (row, col) in enumerate(self.peers):
            self.to_plane(i, row * 2 + col).wait_recv()
        self.line[b] = jnp.sum(self.plane[...], axis=0)
        for i in range(1, n_batch):
            self.to_line(i, b).start()
        for i in range(1, n_batch):
            self.to_line(i, (b + i) % n_batch).wait_recv()
        for i in range(len(self.peers)):
            self.to_plane(i, self.me).wait_send()
        for i in range(1, n_batch):
            self.to_line(i, b).wait_send()
        return jnp.sum(self.line[...], axis=0)


def norm_scratch(n_batch, n_row):
    return [
        pltpu.VMEM((2 * n_row, 8, 128), F32),
        pltpu.VMEM((n_batch, 8, 128), F32),
        dma(2 * n_row - 1),
        dma(2 * n_row),
        dma(n_batch),
        dma(n_batch),
    ]


def transpose_rows(lay, left, turned):
    n, img, far = lay.n_row, lay.img, lay.n_row * lay.img
    for k in range(n):
        turned[:, k * img : (k + 1) * img] = left[k, :img, :].T
    turned[:, far:] = jnp.concatenate([left[k, img:, :] for k in range(n)], 0).T


def weight_gradient(lay, turned, right, local, part, cols):
    n, img, far = lay.n_row, lay.img, lay.n_row * lay.img
    if part == 0:
        total = dot(turned[:, :img], right[0, :img, cols])
        for k in range(1, n):
            total += dot(turned[:, k * img : (k + 1) * img], right[k, :img, cols])
    else:
        text = jnp.concatenate([right[k, img:, cols] for k in range(n)], 0)
        total = dot(turned[:, far:], text)
    local[part, :, cols] = total.astype(BF)


def pull_kernel(
    lay, fused, low_ref, qkv_ref, lse_ref, wo_ref, act_ref, wr_any, mid_ref, a2_ref, dh_ref, o_ref,
    full_ref, dqkv_ref, g_ref, res_ref, exp_ref, out_ref, square_ref, *scratch
):
    (
        q_s, k_s, v_s, do_own, do_out, do_in, do_s, dq_s, dk_s, dv_s, acc, r_out, inbox, turned, wr_ref, a_load, w_load,
        g_send, g_recv, s_send, s_recv, a_send, a_recv, r_send, r_recv,
    ) = scratch[:25]
    n, img, txt, far = lay.n_row, lay.img, lay.txt_pad, lay.n_row * lay.img
    z, c = lax.axis_index("row"), lax.axis_index("col")
    heads, half, hid = q_s.shape[0], do_own.shape[2], act_ref.shape[2]
    mine = pl.ds(pl.multiple_of(c * half, 16), half)
    theirs = pl.ds(pl.multiple_of((1 - c) * half, 16), half)
    my_act = pl.ds(pl.multiple_of(c * hid, 128), hid)
    their_act = pl.ds(pl.multiple_of((1 - c) * hid, 128), hid)
    greet(n, fused)
    gather = Gather(full_ref, g_send, g_recv, n)
    full_ref[z] = low_ref[...]
    gather.push(z)
    swap = Swap(do_out, do_in, s_send, s_recv)
    reduce = Reduce(acc, r_out, inbox, r_send, r_recv, n)
    local, local_out = exp_ref, out_ref
    if fused:
        batch, batch_out = batch_of(scratch[25:33]), batch_of(scratch[33:41])
        local, local_out = batch.local, batch_out.local
    split_heads(lay, qkv_ref, q_s, k_s, v_s, False)
    bias = text_bias(lay)
    dk_s[...] = jnp.zeros_like(dk_s)
    dv_s[...] = jnp.zeros_like(dv_s)
    lag = jnp.minimum(z, n - 1 - z)

    def act_copy(k, where):
        block = g_ref.at[k, :, where]
        return remote(block, block, a_send.at[k], a_recv.at[k], col=1 - c)

    def load(k):
        return pltpu.make_async_copy(act_ref.at[k], g_ref.at[k, :, my_act], a_load.at[k])

    def wr_load():
        return pltpu.make_async_copy(wr_any, wr_ref, w_load.at[0])

    wr_load().start()
    for k in range(n):
        load(k).start()

    def arrive(k):
        gather.arrive_after_own(k)
        for part, rows in parts_of(lay):
            do_out[k, rows] = dot_nt(full_ref[k, rows], wo_ref[part, theirs, :]).astype(BF)
        swap.start(k)
        for part, rows in parts_of(lay):
            do_own[k, rows] = dot_nt(full_ref[k, rows], wo_ref[part, mine, :])

    def expand_gradient():
        transpose_rows(lay, a2_ref, turned)

        @pl.loop(0, 2 * hid // STRIPE)
        def _(i):
            cols = pl.ds(pl.multiple_of(i * STRIPE, 128), STRIPE)
            for part in range(2):
                weight_gradient(lay, turned, dh_ref, local, part, cols)

    def attention(k):
        swap.arrive(k)
        do_s[...] = (do_own[k] + do_in[k].astype(F32)).astype(BF)
        for h in range(heads):
            q, do = q_s[h, k], do_s[:, h * HD : (h + 1) * HD]
            lse = lse_ref[k, :, h : h + 1]
            p1 = jnp.exp(dot_nt(q, k_s[h, :far]) - lse)
            p2 = jnp.exp(dot_nt(q, k_s[h, far:]) + bias - lse)
            dp1 = dot_nt(do, v_s[h, :far])
            dp2 = dot_nt(do, v_s[h, far:])
            row = jnp.sum(p1 * dp1, axis=1, keepdims=True) + jnp.sum(
                p2 * dp2, axis=1, keepdims=True
            )
            ds1 = (p1 * (dp1 - row)).astype(BF)
            ds2 = (p2 * (dp2 - row)).astype(BF)
            dq = (dot(ds1, k_s[h, :far]) + dot(ds2, k_s[h, far:])) * HD**-0.5
            dq_s[h, k] = dq.astype(BF)
            dk_s[h, :, :far] += dot_tn(q, ds1)
            dk_s[h, :, far:] += dot_tn(q, ds2)
            dv_s[h, :, :far] += dot_tn(do, p1.astype(BF))
            dv_s[h, :, far:] += dot_tn(do, p2.astype(BF))

    def down(k):
        act_copy(k, their_act).wait_recv()
        for part, rows in parts_of(lay):
            acc[rows] = dot(g_ref[k, rows], wr_ref[part])
        reduce.add(k)

    @pl.loop(0, n + 1)
    def _(j):
        @pl.when(j < n)
        def _():
            arrive(near_first(z, n, j))

        @pl.when(j < 2)
        def _():
            load(near_first(z, n, n - 1 - j)).wait()
            act_copy(near_first(z, n, n - 1 - j), my_act).start()

        @pl.when(j == n - 1)
        def _():
            for i in range(2, n):
                load(near_first(z, n, n - 1 - i)).wait()
                act_copy(near_first(z, n, n - 1 - i), my_act).start()

        @pl.when(j == 0)
        def _():
            expand_gradient()
            wr_load().wait()
            if fused:
                batch.start()

        if fused:

            @pl.when(j == 2)
            def _():
                batch.pass_on()

        @pl.when((j > 0) & (j <= n))
        def _():
            attention(near_first(z, n, j - 1))

        i = j - 1 - lag

        @pl.when((i >= 0) & (i < 2))
        def _():
            down(near_first(z, n, n - 1 - i))

    turned_o = turned.at[: o_ref.shape[2]]
    transpose_rows(lay, o_ref, turned_o)
    for part in range(2):
        weight_gradient(lay, turned_o, full_ref, local_out, part, slice(0, full_ref.shape[2]))
    if fused:
        batch_out.start()
    for k in range(n):
        for h in range(heads):
            at = h * 3 * HD
            for rows, first, count in (
                (slice(0, img), k * img, img),
                (slice(img, lay.rows), far + k * txt, txt),
            ):
                dk = dk_s[h, :, first : first + count].T.astype(BF)
                dv = dv_s[h, :, first : first + count].T.astype(BF)
                dqkv_ref[k, rows, at : at + 3 * HD] = jnp.concatenate(
                    [dq_s[h, k, rows], dk, dv], 1
                )
    if fused:
        batch_out.pass_on()
    for i in range(2, n):
        down(near_first(z, n, n - 1 - i))
    res_ref[...] = (mid_ref[...] + acc[...]).astype(BF)
    if fused:
        exp_ref[...] = batch.total()
        out_ref[...] = batch_out.total()
        batch.finish()
        batch_out.finish()
        square_ref[...] = squares_of(exp_ref) + squares_of(out_ref)
    gather.finish()
    swap.finish(n)
    reduce.finish()

    @pl.loop(0, n)
    def _(k):
        act_copy(k, my_act).wait_send()


def pull(lay, fused, low, qkv, lse, wo, act, wr, mid, a2, dh, o):
    n, r, d, hid = lay.n_row, lay.rows, low.shape[1], act.shape[2]
    heads = qkv.shape[2] // (3 * HD)
    keys = n * r
    shapes = [(d, 2 * hid), (o.shape[2], d)]
    return call(
        partial(pull_kernel, lay, fused),
        4,
        [
            ((n, r, d), BF),
            ((n, r, 3 * heads * HD), BF),
            ((n, r, 2 * hid), BF),
            ((r, d), BF),
            *[((2, s[0] // 4, s[1]), F32) if fused else ((2, *s), BF) for s in shapes],
            ((8, 128), F32),
        ],
        [
            pltpu.VMEM((heads, n, r, HD), BF),
            pltpu.VMEM((heads, keys, HD), BF),
            pltpu.VMEM((heads, keys, HD), BF),
            pltpu.VMEM((n, r, heads * HD), F32),
            pltpu.VMEM((n, r, heads * HD), BF),
            pltpu.VMEM((n, r, heads * HD), BF),
            pltpu.VMEM((r, heads * HD), BF),
            pltpu.VMEM((heads, n, r, HD), BF),
            pltpu.VMEM((heads, HD, keys), F32),
            pltpu.VMEM((heads, HD, keys), F32),
            pltpu.VMEM((r, d), F32),
            pltpu.VMEM((n, r, d), BF),
            pltpu.VMEM((n + 1, r, d), BF),
            pltpu.VMEM((d, keys), BF),
            pltpu.VMEM(wr.shape, BF),
            dma(n),
            dma(1),
            dma(2, n),
            dma(n),
            dma(n),
            dma(n),
            dma(n),
            dma(n),
            dma(n),
            dma(n + 1),
            *([t for s in shapes for t in batch_scratch(*s)] if fused else []),
        ],
        10**10,
        low,
        qkv,
        lse,
        wo,
        act,
        wr,
        mid,
        a2,
        dh,
        o,
        far=(4, 5),
    )


def input_kernel(
    lay, fused, dqkv_ref, x_ref, dmid_ref, stat_ref, wa_ref, a1_ref, g_ref, cb_ref, square_ref,
    dx_ref, att_ref, red_ref, norm_ref, *scratch
):
    (
        full, into, acc, r_out, inbox, stat_out, stat_in, turned, turned_g,
        s_send, s_recv, r_send, r_recv, t_send, t_recv,
    ) = scratch[:15]
    n = lay.n_row
    z, c = lax.axis_index("row"), lax.axis_index("col")
    half, d = dqkv_ref.shape[2], x_ref.shape[1]
    more = ()
    if fused:
        norm = Norm(4, n, *scratch[39:])
        more = norm.where()
    greet(n, False, more)
    swap = Swap(dqkv_ref, into, s_send, s_recv)
    reduce = Reduce(acc, r_out, inbox, r_send, r_recv, n)
    own, other, red = (scratch[15 + 8 * i : 23 + 8 * i] for i in range(3)) if fused else (
        scratch[15:16], scratch[16:17], (red_ref,)
    )
    sums = [batch_of(s) for s in (own, other, red)] if fused else []

    @pl.loop(0, n)
    def _(j):
        swap.start(near_first(z, n, n - 1 - j))

    def gradient(turned, right, local, stripe):
        if stripe == right.shape[2]:
            for part in range(2):
                weight_gradient(lay, turned, right, local, part, slice(0, stripe))
            return

        @pl.loop(0, right.shape[2] // stripe)
        def _(i):
            cols = pl.ds(pl.multiple_of(i * stripe, 128), stripe)
            for part in range(2):
                weight_gradient(lay, turned, right, local, part, cols)

    transpose_rows(lay, a1_ref, turned)
    gradient(turned, dqkv_ref, own[0], half)
    if fused:
        sums[0].start()
    transpose_rows(lay, g_ref, turned_g)
    gradient(turned_g, cb_ref, red[0], STRIPE // 2)
    if fused:
        sums[2].start()
        sums[0].pass_on()
    lag = jnp.minimum(z, n - 1 - z)

    @pl.loop(0, n + (n - 1) // 2)
    def _(j):
        i = j - lag

        @pl.when((i >= 0) & (i < n))
        def _():
            k = near_first(z, n, n - 1 - i)
            swap.arrive(k)
            mine, theirs = dqkv_ref[k], into[k]
            full[...] = jnp.concatenate(
                [jnp.where(c == 0, mine, theirs), jnp.where(c == 0, theirs, mine)], 1
            )
            for part, rows in parts_of(lay):
                acc[rows] = dot_nt(full[rows], wa_ref[part])
            reduce.add(k)

        if fused:

            @pl.when(j == 0)
            def _():
                sums[2].pass_on()

    gradient(turned, into, other[0], half)
    if fused:
        sums[1].start()
    mean, inverse = moments(stat_ref)
    normed = (x_ref[...].astype(F32) - mean) * inverse
    grad = acc[...]
    stat_out[0] = sums_of(grad, grad * normed)
    exchange(stat_out, stat_in, t_send, t_recv)
    back_one, back_two = columns(stat_out)
    dx_ref[...] = dmid_ref[...] + inverse * (grad - back_one - normed * back_two)
    if fused:
        sums[1].pass_on()
        red_ref[...] = sums[2].total()
        mine, theirs = sums[0].total(), sums[1].total()
    else:
        mine, theirs = own[0][...], other[0][...]
    att_ref[...] = jnp.concatenate(
        [jnp.where(c == 0, mine, theirs), jnp.where(c == 0, theirs, mine)], 2
    )
    if fused:
        squares = square_ref[...] + squares_of(att_ref) + squares_of(red_ref)
        norm_ref[...] = jnp.sqrt(norm.total(squares))
    for total in sums:
        total.finish()
    swap.finish(n)
    reduce.finish()


def inputs_back(lay, fused, dqkv, x, dmid, stat, wa, a1, g, cb, square):
    n, r, d, half = lay.n_row, lay.rows, x.shape[1], dqkv.shape[2]
    keys = n * r
    shapes = [(d, 2 * half), (g.shape[2], d)]
    return call(
        partial(input_kernel, lay, fused),
        5,
        [
            ((r, d), F32),
            *[((2, s[0] // 4, s[1]), F32) if fused else ((2, *s), BF) for s in shapes],
            ((8, 128), F32),
        ],
        [
            pltpu.VMEM((r, 2 * half), BF),
            pltpu.VMEM((n, r, half), BF),
            pltpu.VMEM((r, d), F32),
            pltpu.VMEM((n, r, d), BF),
            pltpu.VMEM((n + 1, r, d), BF),
            pltpu.VMEM((1, 8, r), F32),
            pltpu.VMEM((1, 8, r), F32),
            pltpu.VMEM((d, keys), BF),
            pltpu.VMEM((g.shape[2], keys), BF),
            dma(n),
            dma(n),
            dma(n),
            dma(n + 1),
            dma(1),
            dma(1),
            *(
                [
                    *batch_scratch(d, half),
                    *batch_scratch(d, half),
                    *batch_scratch(g.shape[2], d),
                    *norm_scratch(4, n),
                ]
                if fused
                else [pltpu.VMEM((2, d, half), BF)] * 2
            ),
        ],
        10**10,
        dqkv,
        x,
        dmid,
        stat,
        wa,
        a1,
        g,
        cb,
        square,
    )


def adamw(gradient, moment, square, weight, clip_factor):
    clipped = gradient * clip_factor
    moment_new = BETA_ONE * moment + (1.0 - BETA_ONE) * clipped
    square_new = BETA_TWO * square + (1.0 - BETA_TWO) * clipped * clipped
    corrected = (
        moment_new
        / (1.0 - BETA_ONE**STEP)
        / (jnp.sqrt(square_new / (1.0 - BETA_TWO**STEP)) + 1e-08)
    )
    return (moment_new, square_new, -RATE * (corrected + DECAY * weight))


def update_kernel(norm_ref, *refs):
    grads, moments_in, squares_in, weights = refs[0:4], refs[4:8], refs[8:12], refs[12:16]
    m_out, v_out, s_out, g_out = refs[16:20], refs[20:24], refs[24:28], refs[28:32]
    g_s, m_s, v_s, w_s, t_s = (refs[32 + 4 * i : 36 + 4 * i] for i in range(5))
    load, store = refs[52:]
    b = lax.axis_index("batch")
    loads = []
    for i in range(4):
        rows = grads[i].shape[1]
        part = pl.ds(pl.multiple_of(b * rows, 16), rows)
        for m in range(2):
            for q, (src, dst) in enumerate(
                (
                    (grads[i].at[m], g_s[i]),
                    (moments_in[i].at[m], m_s[i]),
                    (squares_in[i].at[m], v_s[i]),
                    (weights[i].at[m, part, :], w_s[i]),
                )
            ):
                loads.append(pltpu.make_async_copy(src, dst.at[m], load.at[i, m, q]))
                loads[-1].start()
    clip = jnp.minimum(1.0, 1.0 / (norm_ref[0:1, 0:1] + 1e-06))
    stores = []
    for i in range(4):
        for m in range(2):
            for q in range(4):
                loads[8 * i + 4 * m + q].wait()
            stores.append(pltpu.make_async_copy(g_s[i].at[m], g_out[i].at[m], store.at[i, m, 3]))
            stores[-1].start()

            @pl.loop(0, grads[i].shape[1] // TILE)
            def _(r):
                part = pl.ds(pl.multiple_of(r * TILE, TILE), TILE)
                new_m, new_v, step = adamw(
                    g_s[i][m, part, :],
                    m_s[i][m, part, :],
                    v_s[i][m, part, :],
                    w_s[i][m, part, :].astype(F32),
                    clip,
                )
                m_s[i][m, part, :] = new_m
                v_s[i][m, part, :] = new_v
                t_s[i][m, part, :] = step

            for q, (src, dst) in enumerate(
                ((m_s[i], m_out[i]), (v_s[i], v_out[i]), (t_s[i], s_out[i]))
            ):
                stores.append(pltpu.make_async_copy(src.at[m], dst.at[m], store.at[i, m, q]))
                stores[-1].start()
    for each in stores:
        each.wait()


TILE = 16


def update(norm, grads, ms, vs, ws):
    shapes = [g.shape for g in grads]
    outs = pl.pallas_call(
        update_kernel,
        out_shape=[jax.ShapeDtypeStruct(s, F32) for _ in range(4) for s in shapes],
        in_specs=[VMEM] + [ANY] * 16,
        out_specs=[ANY] * 16,
        scratch_shapes=[
            *[pltpu.VMEM(s, t) for t in (F32, F32, F32, BF, F32) for s in shapes],
            dma(4, 2, 4),
            dma(4, 2, 4),
        ],
        compiler_params=pltpu.CompilerParams(vmem_limit_bytes=60 * 2**20),
        cost_estimate=pl.CostEstimate(flops=10**8, bytes_accessed=5 * 10**7, transcendentals=0),
    )(norm, *grads, *ms, *vs, *ws)
    return outs[0:4], outs[4:8], outs[8:12], outs[12:16]


def weight_shard(weight, group_index, shard_rows):
    return lax.dynamic_slice_in_dim(weight, group_index * shard_rows, shard_rows, 1).astype(F32)


class Layout:
    def __init__(self, n_row, img, txt):
        self.n_row = n_row
        self.img = img
        self.txt = txt
        self.txt_pad = -(-txt // 16) * 16
        self.rows = img + self.txt_pad
        self.real = img + txt

    def pack(self, image, text):
        return jnp.concatenate(
            [image, text, jnp.zeros((self.txt_pad - self.txt, image.shape[1]), image.dtype)], 0
        )


def on_device(n_batch, n_row, *args):
    (
        image_input,
        text_input,
        image_cotan,
        text_cotan,
        seq_group,
        w_attend,
        w_output,
        w_expand,
        w_reduce,
        m_attend,
        m_output,
        m_expand,
        m_reduce,
        v_attend,
        v_output,
        v_expand,
        v_reduce,
    ) = args
    img, txt = image_input.shape[1], text_input.shape[1]
    lay = Layout(n_row, img, txt)
    group_index = lax.axis_index("batch")
    present = jnp.any(seq_group == group_index).astype(F32)

    low_x = lay.pack(image_input[0], text_input[0])
    low_cot = (lay.pack(image_cotan[0], text_cotan[0]).astype(F32) * present).astype(BF)
    fused = n_batch == 4

    a1_all, qkv, stat_one = attend(lay, low_x, w_attend)
    o_all, lse, cb_all, dg, middle_x, low_two, stat_two = middle(
        lay, qkv, low_x, low_cot, w_output, w_reduce
    )
    a2_all, act, dh_all, grad_mid, low_mid = hidden(
        lay, low_two, dg, middle_x, low_cot, stat_two, w_expand
    )
    _, dqkv, g_all, result, g_exp, g_out, square = pull(
        lay, fused, low_mid, qkv, lse, w_output, act, w_reduce, middle_x, a2_all, dh_all, o_all
    )
    grad_in, g_att, g_red, norm = inputs_back(
        lay, fused, dqkv, low_x, grad_mid, stat_one, w_attend, a1_all, g_all, cb_all, square
    )
    sums = [g_att, g_out, g_exp, g_red]
    if not fused:
        sums = [
            lax.psum_scatter(g, "batch", scatter_dimension=1, tiled=True).astype(F32) for g in sums
        ]
    ms = (m_attend, m_output, m_expand, m_reduce)
    vs = (v_attend, v_output, v_expand, v_reduce)
    ws = (w_attend, w_output, w_expand, w_reduce)
    if fused:
        grad_norm = norm[0, 0]
        new_m, new_v, steps, sums = update(norm, sums, ms, vs, ws)
    else:
        squares = sum(jnp.sum(g * g) for g in sums)
        grad_norm = jnp.sqrt(lax.psum(lax.psum(lax.psum(squares, "batch"), "row"), "col"))
        clip_factor = jnp.minimum(1.0, 1.0 / (grad_norm + 1e-06))
        new_m, new_v, steps = zip(
            *[
                adamw(g, m, v, weight_shard(w, group_index, g.shape[1]), clip_factor)
                for g, m, v, w in zip(sums, ms, vs, ws)
            ]
        )
    return (
        result[:img][None],
        result[img : lay.real][None],
        grad_in[:img][None],
        grad_in[img : lay.real][None],
        *sums,
        *new_m,
        *new_v,
        *steps,
        grad_norm,
    )


def solution(mesh):
    tokens = P("batch", "row", "col")
    wide = P(None, "col", "row")
    tall = P(None, "row", "col")
    wide_shard = P(None, ("col", "batch"), "row")
    tall_shard = P(None, ("row", "batch"), "col")
    shards = (wide_shard, tall_shard, wide_shard, tall_shard)
    return jax.shard_map(
        partial(on_device, mesh.shape["batch"], mesh.shape["row"]),
        mesh=mesh,
        in_specs=(*[tokens] * 4, P(), wide, tall, wide, tall, *shards, *shards),
        out_specs=(*[tokens] * 4, *shards * 4, P()),
        check_vma=False,
    )
```

```python
import math
from functools import partial

import jax
import jax.numpy as jnp
from jax import lax
from jax.experimental import pallas as pl
from jax.experimental.pallas import tpu as pltpu
from jax.sharding import PartitionSpec as P

D = 1536
HD = 64
STEP = 10
STRIPE = 512

EPSILON = 1e-06
BETA_ONE = 0.9
BETA_TWO = 0.999
RATE = 0.02
DECAY = 0.1

BF = jnp.bfloat16
F32 = jnp.float32


def dot(a, b):
    return lax.dot_general(a, b, (((a.ndim - 1,), (0,)), ((), ())), preferred_element_type=F32)


def dot_nt(a, b):
    return lax.dot_general(a, b, (((a.ndim - 1,), (1,)), ((), ())), preferred_element_type=F32)


def dot_tn(a, b):
    return lax.dot_general(a, b, (((0,), (0,)), ((), ())), preferred_element_type=F32)


MESH = pl.DeviceIdType.MESH
VMEM = pl.BlockSpec(memory_space=pltpu.VMEM)
ANY = pl.BlockSpec(memory_space=pl.ANY)


def remote(src, dst, send, recv, **where):
    return pltpu.make_async_remote_copy(
        src_ref=src,
        dst_ref=dst,
        send_sem=send,
        recv_sem=recv,
        device_id=where,
        device_id_type=MESH,
    )


def near_first(z, n, j):
    alternate = jnp.where(j % 2 == 1, z - (j + 1) // 2, z + j // 2)
    reach = jnp.minimum(z, n - 1 - z)
    beyond = jnp.where(z <= n - 1 - z, j, n - 1 - j)
    return jnp.where(j <= 2 * reach, alternate, beyond)


def greet(n, fused=False, more=()):
    z, c = lax.axis_index("row"), lax.axis_index("col")
    barrier = pltpu.get_barrier_semaphore()
    pl.semaphore_signal(barrier, inc=1, device_id={"col": 1 - c}, device_id_type=MESH)

    @pl.when(z > 0)
    def _():
        pl.semaphore_signal(barrier, inc=1, device_id={"row": z - 1}, device_id_type=MESH)

    @pl.when(z < n - 1)
    def _():
        pl.semaphore_signal(barrier, inc=1, device_id={"row": z + 1}, device_id_type=MESH)

    if fused:
        b = lax.axis_index("batch")
        for other in (b + 1 - 2 * (b % 2), (b + 2) % 4):
            pl.semaphore_signal(barrier, inc=1, device_id={"batch": other}, device_id_type=MESH)
    ends = jnp.where(z > 0, 1, 0) + jnp.where(z < n - 1, 1, 0)
    for where in more:
        pl.semaphore_signal(barrier, inc=1, device_id=where, device_id_type=MESH)
    pl.semaphore_wait(barrier, ends + (3 if fused else 1) + len(more))


class Gather:
    def __init__(self, full, send, recv, n):
        self.full, self.send, self.recv, self.n = full, send, recv, n
        self.z = lax.axis_index("row")

    def copy(self, k, step):
        there = (self.z + step + self.n) % self.n
        way = 0 if step > 0 else 1
        return remote(
            self.full.at[k], self.full.at[k], self.send.at[way, k], self.recv.at[k], row=there
        )

    def push(self, k):
        @pl.when((k <= self.z) & (self.z < self.n - 1))
        def _():
            self.copy(k, 1).start()

        @pl.when((k >= self.z) & (self.z > 0))
        def _():
            self.copy(k, -1).start()

    def arrive(self, k):
        @pl.when(k != self.z)
        def _():
            self.copy(k, 1).wait_recv()

        self.push(k)

    def arrive_after_own(self, k):
        @pl.when(k != self.z)
        def _():
            self.arrive(k)

    def finish(self):
        @pl.loop(0, self.n)
        def _(k):
            @pl.when((k <= self.z) & (self.z < self.n - 1))
            def _():
                self.copy(k, 1).wait_send()

            @pl.when((k >= self.z) & (self.z > 0))
            def _():
                self.copy(k, -1).wait_send()


class Reduce:
    def __init__(self, acc, out, inbox, send, recv, n):
        self.acc, self.out, self.inbox, self.send, self.recv, self.n = acc, out, inbox, send, recv, n
        self.z = lax.axis_index("row")

    def copy(self, o):
        slot = jnp.where(o > self.z, o + 1, o)
        there = (self.z + jnp.where(o > self.z, 1, -1) + self.n) % self.n
        return remote(
            self.out.at[o], self.inbox.at[slot], self.send.at[o], self.recv.at[slot], row=there
        )

    def take(self, slot):
        remote(
            self.out.at[0],
            self.inbox.at[slot],
            self.send.at[0],
            self.recv.at[slot],
            row=(self.z + 1) % self.n,
        ).wait_recv()
        self.acc[...] += self.inbox[slot].astype(F32)

    def add(self, o):
        @pl.when((o >= self.z) & (self.z > 0))
        def _():
            self.take(o + 1)

        @pl.when((o <= self.z) & (self.z < self.n - 1))
        def _():
            self.take(o)

        @pl.when(o != self.z)
        def _():
            self.out[o] = self.acc[...].astype(BF)
            self.copy(o).start()

    def finish(self):
        @pl.loop(0, self.n)
        def _(o):
            @pl.when(o != self.z)
            def _():
                self.copy(o).wait_send()


class Swap:
    def __init__(self, out, into, send, recv):
        self.out, self.into, self.send, self.recv = out, into, send, recv

    def copy(self, k):
        return remote(
            self.out.at[k],
            self.into.at[k],
            self.send.at[k],
            self.recv.at[k],
            col=1 - lax.axis_index("col"),
        )

    def start(self, k):
        self.copy(k).start()

    def arrive(self, k):
        self.copy(k).wait_recv()

    def finish(self, n):
        @pl.loop(0, n)
        def _(k):
            self.copy(k).wait_send()


def sums_of(a, b):
    lane = lax.broadcasted_iota(jnp.int32, (a.shape[0], 128), 1)
    one, two = jnp.sum(a, axis=1, keepdims=True), jnp.sum(b, axis=1, keepdims=True)
    return jnp.where(lane == 0, one, jnp.where(lane == 1, two, 0.0)).T[:8]


def columns(stat):
    rows = stat[0]
    turned = jnp.concatenate([rows, jnp.zeros((120, rows.shape[1]), F32)], 0).T
    return turned[:, 0:1] / D, turned[:, 1:2] / D


def moments(stat):
    mean, square = columns(stat)
    return mean, lax.rsqrt(square - mean * mean + EPSILON)


def exchange(stat, stat_in, send, recv):
    swap = Swap(stat, stat_in, send, recv)
    swap.start(0)
    swap.arrive(0)
    swap.finish(1)
    stat[0] += stat_in[0]


def dma(*shape):
    return pltpu.SemaphoreType.DMA(shape)


def call(kernel, ident, outs, scratch, cost, *operands, far=()):
    return pl.pallas_call(
        kernel,
        out_shape=[jax.ShapeDtypeStruct(s, t) for s, t in outs],
        in_specs=[ANY if i in far else VMEM for i in range(len(operands))],
        out_specs=[VMEM] * len(outs),
        scratch_shapes=scratch,
        compiler_params=pltpu.CompilerParams(
            collective_id=ident, has_side_effects=True, vmem_limit_bytes=60 * 2**20
        ),
        cost_estimate=pl.CostEstimate(flops=cost, bytes_accessed=10**7, transcendentals=0),
    )(*operands)


def parts_of(lay):
    return ((0, slice(0, lay.img)), (1, slice(lay.img, lay.rows)))


def attend_kernel(lay, x_ref, w_ref, full_ref, qkv_ref, stat_ref, *scratch):
    own, out, into, stat_in, g_send, g_recv, s_send, s_recv, t_send, t_recv = scratch
    n = lay.n_row
    z, c = lax.axis_index("row"), lax.axis_index("col")
    half = qkv_ref.shape[2]
    greet(n)
    x = x_ref[...].astype(F32)
    stat_ref[0] = sums_of(x, x * x)
    exchange(stat_ref, stat_in, t_send, t_recv)
    mean, inverse = moments(stat_ref)
    full_ref[z] = ((x - mean) * inverse).astype(BF)
    gather = Gather(full_ref, g_send, g_recv, n)
    swap = Swap(out, into, s_send, s_recv)

    @pl.loop(0, n)
    def _(j):
        k = near_first(z, n, j)
        gather.arrive(k)
        for part, rows in parts_of(lay):
            p = dot(full_ref[k, rows], w_ref[part])
            low, high = p[:, :half], p[:, half:]
            own[k, rows] = jnp.where(c == 0, low, high)
            out[k, rows] = jnp.where(c == 0, high, low).astype(BF)
        swap.start(k)

    @pl.loop(0, n)
    def _(j):
        k = near_first(z, n, j)
        swap.arrive(k)
        qkv_ref[k] = (own[k] + into[k].astype(F32)).astype(BF)

    gather.finish()
    swap.finish(n)


def attend(lay, x, w):
    n, r, half, d = lay.n_row, lay.rows, w.shape[2] // 2, x.shape[1]
    return call(
        partial(attend_kernel, lay),
        1,
        [((n, r, d), BF), ((n, r, half), BF), ((1, 8, r), F32)],
        [
            pltpu.VMEM((n, r, half), F32),
            pltpu.VMEM((n, r, half), BF),
            pltpu.VMEM((n, r, half), BF),
            pltpu.VMEM((1, 8, r), F32),
            dma(2, n),
            dma(n),
            dma(n),
            dma(n),
            dma(1),
            dma(1),
        ],
        2 * n * r * w.shape[1] * w.shape[2],
        x,
        w,
    )


def split_heads(lay, qkv_ref, q_ref, k_ref, v_ref, fill):
    n, img, txt = lay.n_row, lay.img, lay.txt_pad
    heads = qkv_ref.shape[2] // (3 * HD)

    @pl.loop(0, n)
    def _(k):
        first = pl.ds(pl.multiple_of(k * img, 16), img)
        second = pl.ds(pl.multiple_of(n * img + k * txt, 16), txt)
        for h in range(heads):
            at = h * 3 * HD
            rows = qkv_ref[k, :, at : at + 3 * HD]
            q_ref[h, k] = rows[:, :HD] * jnp.asarray(HD**-0.5, BF)
            for ref, lo in ((k_ref, HD), (v_ref, 2 * HD)):
                value = rows[:, lo : lo + HD]
                if ref is v_ref and fill:
                    value = jnp.concatenate([value, jnp.ones_like(value)], 1)
                ref[h, first] = value[:img]
                ref[h, second] = value[img:]


def text_bias(lay):
    lane = lax.broadcasted_iota(jnp.int32, (1, lay.n_row * lay.txt_pad), 1)
    return jnp.where(lane % lay.txt_pad < lay.txt, 0.0, -1e30)


def middle_kernel(
    lay, loads, qkv_ref, x_ref, cot_ref, wo_ref, wr_ref, o_ref, lse_ref, cb_ref, dg_ref, mid_ref, low_ref, stat_ref, *scratch
):
    (
        q_s, k_s, v_s, o_out, o_in, dg_out, dg_in, acc, r_out, inbox, stat_in,
        g_send, g_recv, o_send, o_recv, d_send, d_recv, r_send, r_recv, t_send, t_recv,
    ) = scratch
    n, far = lay.n_row, lay.n_row * lay.img
    z, c = lax.axis_index("row"), lax.axis_index("col")
    heads, hid = q_s.shape[0], dg_ref.shape[2]
    greet(n)
    gather = Gather(cb_ref, g_send, g_recv, n)
    cb_ref[z] = cot_ref[...]
    gather.push(z)
    swap_o = Swap(o_out, o_in, o_send, o_recv)
    swap_d = Swap(dg_out, dg_in, d_send, d_recv)
    reduce = Reduce(acc, r_out, inbox, r_send, r_recv, n)
    split_heads(lay, qkv_ref, q_s, k_s, v_s, True)
    bias = text_bias(lay)
    lane = lax.broadcasted_iota(jnp.int32, (lay.rows, 128), 1)

    def attention(k):
        outs, lse = [], jnp.zeros((lay.rows, 128), F32)
        for h in range(heads):
            q = q_s[h, k]
            s1 = dot_nt(q, k_s[h, :far])
            s2 = dot_nt(q, k_s[h, far:]) + bias
            peak = jnp.maximum(
                jnp.max(s1, axis=1, keepdims=True), jnp.max(s2, axis=1, keepdims=True)
            )
            e1, e2 = jnp.exp(s1 - peak).astype(BF), jnp.exp(s2 - peak).astype(BF)
            o = dot(e1, v_s[h, :far]) + dot(e2, v_s[h, far:])
            total = o[:, HD : HD + 1]
            outs.append((o[:, :HD] / total).astype(BF))
            lse = jnp.where(lane == h, peak + jnp.log(total), lse)
        lse_ref[k] = lse
        o_out[k] = jnp.concatenate(outs, 1)

    def project(k):
        swap_o.arrive(k)
        own, other = o_out[k], o_in[k]
        o_ref[k] = jnp.concatenate(
            [jnp.where(c == 0, own, other), jnp.where(c == 0, other, own)], 1
        )
        for part, rows in parts_of(lay):
            acc[rows] = dot(o_ref[k, rows], wo_ref[part])
        reduce.add(k)

    @pl.loop(0, n)
    def _(j):
        k = near_first(z, n, n - 1 - j)
        attention(k)
        swap_o.start(k)

        @pl.when(j == 0)
        def _():
            loads[0].wait()
            loads[1].wait()

        near = near_first(z, n, j)
        gather.arrive_after_own(near)
        for part, rows in parts_of(lay):
            dg_out[near, rows] = dot_nt(
                cb_ref[near, rows], wr_ref[part, pl.ds(pl.multiple_of((1 - c) * hid, 128), hid), :]
            ).astype(BF)
        swap_d.start(near)
        for part, rows in parts_of(lay):
            dg_ref[near, rows] = dot_nt(
                cb_ref[near, rows], wr_ref[part, pl.ds(pl.multiple_of(c * hid, 128), hid), :]
            )

        @pl.when(j > 0)
        def _():
            project(near_first(z, n, n - j))

    project(near_first(z, n, 0))
    mid = x_ref[...].astype(F32) + acc[...]
    mid_ref[...] = mid
    stat_ref[0] = sums_of(mid, mid * mid)
    exchange(stat_ref, stat_in, t_send, t_recv)
    mean, inverse = moments(stat_ref)
    low_ref[...] = ((mid - mean) * inverse).astype(BF)

    @pl.loop(0, n)
    def _(j):
        k = near_first(z, n, j)
        swap_d.arrive(k)
        dg_ref[k] += dg_in[k].astype(F32)

    gather.finish()
    swap_o.finish(n)
    swap_d.finish(n)
    reduce.finish()


SLOPE = (2.0 / math.pi) ** 0.5
CUBIC = 0.044715


def gelu_pair(u):
    square = u * u
    t = jnp.tanh(SLOPE * u * (1.0 + CUBIC * square))
    half = 0.5 * (1.0 + t)
    slope = half + 0.5 * u * (1.0 - t * t) * (SLOPE * (1.0 + 3.0 * CUBIC * square))
    return u * half, slope


def hidden_kernel(
    lay, low_ref, dg_ref, mid_ref, cot_ref, stat_ref, we_ref, full_ref, act_ref, dh_ref, dmid_ref, dy_ref, *scratch
):
    (
        own, out, into, acc, r_out, inbox, stat_out, stat_in,
        g_send, g_recv, s_send, s_recv, d_send, d_recv, r_send, r_recv, t_send, t_recv,
    ) = scratch
    n = lay.n_row
    z, c = lax.axis_index("row"), lax.axis_index("col")
    hid = dg_ref.shape[2]
    mine = pl.ds(pl.multiple_of(c * hid, 128), hid)
    theirs = pl.ds(pl.multiple_of((1 - c) * hid, 128), hid)
    gather = Gather(full_ref, g_send, g_recv, n)
    full_ref[z] = low_ref[...]
    gather.push(z)
    swap = Swap(out, into, s_send, s_recv)
    reduce = Reduce(acc, r_out, inbox, r_send, r_recv, n)

    def dh_copy(k):
        half = dh_ref.at[k, :, mine]
        return remote(half, half, d_send.at[k], d_recv.at[k], col=1 - c)

    @pl.loop(0, n)
    def _(j):
        k = near_first(z, n, j)
        gather.arrive_after_own(k)
        for part, rows in parts_of(lay):
            out[k, rows] = dot(full_ref[k, rows], we_ref[part, :, theirs]).astype(BF)
        swap.start(k)
        for part, rows in parts_of(lay):
            own[k, rows] = dot(full_ref[k, rows], we_ref[part, :, mine])

    def back(k):
        half = dh_ref.at[k, :, theirs]
        remote(half, half, d_send.at[k], d_recv.at[k], col=1 - c).wait_recv()
        for part, rows in parts_of(lay):
            acc[rows] = dot_nt(dh_ref[k, rows], we_ref[part])
        reduce.add(k)

    @pl.loop(0, n)
    def _(j):
        k = near_first(z, n, n - 1 - j)
        swap.arrive(k)
        act, slope = gelu_pair(own[k] + into[k].astype(F32))
        act_ref[k] = act.astype(BF)
        dh_ref[k, :, mine] = (dg_ref[k] * slope).astype(BF)
        dh_copy(k).start()

        @pl.when(j > 0)
        def _():
            back(near_first(z, n, n - j))

    back(near_first(z, n, 0))
    mean, inverse = moments(stat_ref)
    normed = (mid_ref[...] - mean) * inverse
    grad = acc[...]
    stat_out[0] = sums_of(grad, grad * normed)
    exchange(stat_out, stat_in, t_send, t_recv)
    back_one, back_two = columns(stat_out)
    dmid = cot_ref[...].astype(F32) + inverse * (grad - back_one - normed * back_two)
    dmid_ref[...] = dmid
    dy_ref[...] = dmid.astype(BF)
    gather.finish()
    swap.finish(n)
    reduce.finish()

    @pl.loop(0, n)
    def _(k):
        dh_copy(k).wait_send()


def forward_kernel(
    lay, qkv_ref, x_ref, cot_ref, wo_ref, wr_any, we_any,
    o_ref, lse_ref, cb_ref, mid_ref, a2_ref, act_ref, dh_ref, dmid_ref, dy_ref, *scratch
):
    dg_ref, low_ref, stat_ref, wr_ref, we_ref, w_load = scratch[:6]
    loads = [
        pltpu.make_async_copy(wr_any, wr_ref, w_load.at[0]),
        pltpu.make_async_copy(we_any, we_ref, w_load.at[1]),
    ]
    for each in loads:
        each.start()
    middle_kernel(
        lay, loads, qkv_ref, x_ref, cot_ref, wo_ref, wr_ref, o_ref, lse_ref, cb_ref, dg_ref, mid_ref, low_ref, stat_ref, *scratch[6:27]
    )
    hidden_kernel(
        lay, low_ref, dg_ref, mid_ref, cot_ref, stat_ref, we_ref, a2_ref, act_ref, dh_ref, dmid_ref, dy_ref, *scratch[27:]
    )


def forward(lay, qkv, x, cot, wo, wr, we):
    n, r, d = lay.n_row, lay.rows, x.shape[1]
    heads, hid = qkv.shape[2] // (3 * HD), wr.shape[1] // 2
    keys = n * r
    return call(
        partial(forward_kernel, lay),
        2,
        [
            ((n, r, 2 * heads * HD), BF),
            ((n, r, 128), F32),
            ((n, r, d), BF),
            ((r, d), F32),
            ((n, r, d), BF),
            ((n, r, hid), BF),
            ((n, r, 2 * hid), BF),
            ((r, d), F32),
            ((r, d), BF),
        ],
        [
            pltpu.VMEM((n, r, hid), F32),
            pltpu.VMEM((r, d), BF),
            pltpu.VMEM((1, 8, r), F32),
            pltpu.VMEM(wr.shape, BF),
            pltpu.VMEM(we.shape, BF),
            dma(2),
            pltpu.VMEM((heads, n, r, HD), BF),
            pltpu.VMEM((heads, keys, HD), BF),
            pltpu.VMEM((heads, keys, 2 * HD), BF),
            pltpu.VMEM((n, r, heads * HD), BF),
            pltpu.VMEM((n, r, heads * HD), BF),
            pltpu.VMEM((n, r, hid), BF),
            pltpu.VMEM((n, r, hid), BF),
            pltpu.VMEM((r, d), F32),
            pltpu.VMEM((n, r, d), BF),
            pltpu.VMEM((n + 1, r, d), BF),
            pltpu.VMEM((1, 8, r), F32),
            dma(2, n),
            dma(n),
            dma(n),
            dma(n),
            dma(n),
            dma(n),
            dma(n),
            dma(n + 1),
            dma(1),
            dma(1),
            pltpu.VMEM((n, r, hid), F32),
            pltpu.VMEM((n, r, hid), BF),
            pltpu.VMEM((n, r, hid), BF),
            pltpu.VMEM((r, d), F32),
            pltpu.VMEM((n, r, d), BF),
            pltpu.VMEM((n + 1, r, d), BF),
            pltpu.VMEM((1, 8, r), F32),
            pltpu.VMEM((1, 8, r), F32),
            dma(2, n),
            dma(n),
            dma(n),
            dma(n),
            dma(n),
            dma(n),
            dma(n),
            dma(n + 1),
            dma(1),
            dma(1),
        ],
        10**10,
        qkv,
        x,
        cot,
        wo,
        wr,
        we,
        far=(4, 5),
    )


class BatchSum:
    def __init__(self, local, first, out, second, sems):
        self.local, self.first, self.out, self.second = local, first, out, second
        self.f_send, self.f_recv, self.s_send, self.s_recv = sems
        b = lax.axis_index("batch")
        self.x, self.core = b // 2, b % 2
        self.to_core, self.to_x = 2 * self.x + 1 - self.core, 2 * (1 - self.x) + self.core
        self.s = out.shape[1]

    def rows(self, block):
        return pl.ds(pl.multiple_of(block * self.s, 16), self.s)

    def core_copy(self, q):
        block = 2 * q + 1 - self.core
        return remote(
            self.local.at[:, self.rows(block), :],
            self.first.at[q],
            self.f_send.at[q],
            self.f_recv.at[q],
            batch=self.to_core,
        )

    def x_copy(self):
        return remote(self.out, self.second, self.s_send.at[0], self.s_recv.at[0], batch=self.to_x)

    def start(self):
        self.core_copy(1 - self.x).start()
        self.core_copy(self.x).start()

    def block(self, q):
        self.core_copy(q).wait_recv()
        mine = self.local[:, self.rows(2 * q + self.core), :].astype(F32)
        return mine + self.first[q].astype(F32)

    def pass_on(self):
        self.out[...] = self.block(1 - self.x).astype(BF)
        self.x_copy().start()

    def total(self):
        near = self.block(self.x)
        self.x_copy().wait_recv()
        return near + self.second[...].astype(F32)

    def finish(self):
        self.core_copy(0).wait_send()
        self.core_copy(1).wait_send()
        self.x_copy().wait_send()


def batch_scratch(rows, cols):
    s = rows // 4
    return [
        pltpu.VMEM((2, rows, cols), BF),
        pltpu.VMEM((2, 2, s, cols), BF),
        pltpu.VMEM((2, s, cols), BF),
        pltpu.VMEM((2, s, cols), BF),
        dma(2),
        dma(2),
        dma(1),
        dma(1),
    ]


def batch_of(scratch):
    return BatchSum(*scratch[:4], scratch[4:])


def squares_of(ref):
    total = jnp.zeros((1, 1), F32)
    for m in range(2):
        lanes = jnp.sum(ref[m] * ref[m], axis=0, keepdims=True)
        total += jnp.sum(lanes, axis=1, keepdims=True)
    return jnp.broadcast_to(total, (8, 128))


class Norm:
    def __init__(self, n_batch, n_row, plane, line, p_send, p_recv, b_send, b_recv):
        self.n_batch, self.plane, self.line = n_batch, plane, line
        self.p_send, self.p_recv, self.b_send, self.b_recv = p_send, p_recv, b_send, b_recv
        self.b, z, c = lax.axis_index("batch"), lax.axis_index("row"), lax.axis_index("col")
        self.me = z * 2 + c
        self.peers = [((z + i) % n_row, (c + j) % 2) for i in range(n_row) for j in range(2)][1:]

    def where(self):
        return [{"row": row, "col": col} for row, col in self.peers] + [
            {"batch": (self.b + i) % self.n_batch} for i in range(1, self.n_batch)
        ]

    def to_plane(self, i, slot):
        row, col = self.peers[i]
        block = self.plane.at[slot]
        return remote(block, block, self.p_send.at[i], self.p_recv.at[slot], row=row, col=col)

    def to_line(self, i, slot):
        block = self.line.at[slot]
        other = (self.b + i) % self.n_batch
        return remote(block, block, self.b_send.at[i], self.b_recv.at[slot], batch=other)

    def total(self, tile):
        b, n_batch = self.b, self.n_batch
        self.plane[self.me] = tile
        for i in range(len(self.peers)):
            self.to_plane(i, self.me).start()
        for i, (row, col) in enumerate(self.peers):
            self.to_plane(i, row * 2 + col).wait_recv()
        self.line[b] = jnp.sum(self.plane[...], axis=0)
        for i in range(1, n_batch):
            self.to_line(i, b).start()
        for i in range(1, n_batch):
            self.to_line(i, (b + i) % n_batch).wait_recv()
        for i in range(len(self.peers)):
            self.to_plane(i, self.me).wait_send()
        for i in range(1, n_batch):
            self.to_line(i, b).wait_send()
        return jnp.sum(self.line[...], axis=0)


def norm_scratch(n_batch, n_row):
    return [
        pltpu.VMEM((2 * n_row, 8, 128), F32),
        pltpu.VMEM((n_batch, 8, 128), F32),
        dma(2 * n_row - 1),
        dma(2 * n_row),
        dma(n_batch),
        dma(n_batch),
    ]


def transpose_rows(lay, left, turned):
    n, img, far = lay.n_row, lay.img, lay.n_row * lay.img
    for k in range(n):
        turned[:, k * img : (k + 1) * img] = left[k, :img, :].T
    turned[:, far:] = jnp.concatenate([left[k, img:, :] for k in range(n)], 0).T


def weight_gradient(lay, turned, right, local, part, cols):
    n, img, far = lay.n_row, lay.img, lay.n_row * lay.img
    if part == 0:
        total = dot(turned[:, :img], right[0, :img, cols])
        for k in range(1, n):
            total += dot(turned[:, k * img : (k + 1) * img], right[k, :img, cols])
    else:
        text = jnp.concatenate([right[k, img:, cols] for k in range(n)], 0)
        total = dot(turned[:, far:], text)
    local[part, :, cols] = total.astype(BF)


def pull_kernel(
    lay, fused, low_ref, qkv_ref, lse_ref, wo_ref, act_ref, wr_any, mid_ref, a2_ref, dh_ref, o_ref,
    dqkv_ref, g_ref, res_ref, exp_ref, out_ref, square_ref, *scratch
):
    (
        q_s, k_s, v_s, do_own, do_out, do_in, do_s, dq_s, dk_s, dv_s, acc, r_out, inbox, turned, wr_ref, full_ref, a_load, w_load,
        g_send, g_recv, s_send, s_recv, a_send, a_recv, r_send, r_recv,
    ) = scratch[:26]
    n, img, txt, far = lay.n_row, lay.img, lay.txt_pad, lay.n_row * lay.img
    z, c = lax.axis_index("row"), lax.axis_index("col")
    heads, half, hid = q_s.shape[0], do_own.shape[2], act_ref.shape[2]
    mine = pl.ds(pl.multiple_of(c * half, 16), half)
    theirs = pl.ds(pl.multiple_of((1 - c) * half, 16), half)
    my_act = pl.ds(pl.multiple_of(c * hid, 128), hid)
    their_act = pl.ds(pl.multiple_of((1 - c) * hid, 128), hid)
    greet(n, fused)
    gather = Gather(full_ref, g_send, g_recv, n)
    full_ref[z] = low_ref[...]
    gather.push(z)
    swap = Swap(do_out, do_in, s_send, s_recv)
    reduce = Reduce(acc, r_out, inbox, r_send, r_recv, n)
    local, local_out = exp_ref, out_ref
    if fused:
        batch, batch_out = batch_of(scratch[26:34]), batch_of(scratch[34:42])
        local, local_out = batch.local, batch_out.local
    split_heads(lay, qkv_ref, q_s, k_s, v_s, False)
    bias = text_bias(lay)
    dk_s[...] = jnp.zeros_like(dk_s)
    dv_s[...] = jnp.zeros_like(dv_s)
    lag = jnp.minimum(z, n - 1 - z)

    def act_copy(k, where):
        block = g_ref.at[k, :, where]
        return remote(block, block, a_send.at[k], a_recv.at[k], col=1 - c)

    def load(k):
        return pltpu.make_async_copy(act_ref.at[k], g_ref.at[k, :, my_act], a_load.at[k])

    def wr_load():
        return pltpu.make_async_copy(wr_any, wr_ref, w_load.at[0])

    wr_load().start()
    for k in range(n):
        load(k).start()

    def arrive(k):
        gather.arrive_after_own(k)
        for part, rows in parts_of(lay):
            do_out[k, rows] = dot_nt(full_ref[k, rows], wo_ref[part, theirs, :]).astype(BF)
        swap.start(k)
        for part, rows in parts_of(lay):
            do_own[k, rows] = dot_nt(full_ref[k, rows], wo_ref[part, mine, :])

    def expand_gradient():
        transpose_rows(lay, a2_ref, turned)

        @pl.loop(0, 2 * hid // STRIPE)
        def _(i):
            cols = pl.ds(pl.multiple_of(i * STRIPE, 128), STRIPE)
            for part in range(2):
                weight_gradient(lay, turned, dh_ref, local, part, cols)

    def attention(k):
        swap.arrive(k)
        do_s[...] = (do_own[k] + do_in[k].astype(F32)).astype(BF)
        for h in range(heads):
            q, do = q_s[h, k], do_s[:, h * HD : (h + 1) * HD]
            lse = lse_ref[k, :, h : h + 1]
            p1 = jnp.exp(dot_nt(q, k_s[h, :far]) - lse)
            p2 = jnp.exp(dot_nt(q, k_s[h, far:]) + bias - lse)
            dp1 = dot_nt(do, v_s[h, :far])
            dp2 = dot_nt(do, v_s[h, far:])
            row = jnp.sum(p1 * dp1, axis=1, keepdims=True) + jnp.sum(
                p2 * dp2, axis=1, keepdims=True
            )
            ds1 = (p1 * (dp1 - row)).astype(BF)
            ds2 = (p2 * (dp2 - row)).astype(BF)
            dq = (dot(ds1, k_s[h, :far]) + dot(ds2, k_s[h, far:])) * HD**-0.5
            dq_s[h, k] = dq.astype(BF)
            dk_s[h, :, :far] += dot_tn(q, ds1)
            dk_s[h, :, far:] += dot_tn(q, ds2)
            dv_s[h, :, :far] += dot_tn(do, p1.astype(BF))
            dv_s[h, :, far:] += dot_tn(do, p2.astype(BF))

    def down(k):
        act_copy(k, their_act).wait_recv()
        for part, rows in parts_of(lay):
            acc[rows] = dot(g_ref[k, rows], wr_ref[part])
        reduce.add(k)

    @pl.loop(0, n + 1)
    def _(j):
        @pl.when(j < n)
        def _():
            arrive(near_first(z, n, j))

        @pl.when(j < 2)
        def _():
            load(near_first(z, n, n - 1 - j)).wait()
            act_copy(near_first(z, n, n - 1 - j), my_act).start()

        @pl.when(j == n - 1)
        def _():
            for i in range(2, n):
                load(near_first(z, n, n - 1 - i)).wait()
                act_copy(near_first(z, n, n - 1 - i), my_act).start()

        @pl.when(j == 0)
        def _():
            expand_gradient()
            wr_load().wait()
            if fused:
                batch.start()

        if fused:

            @pl.when(j == 2)
            def _():
                batch.pass_on()

        @pl.when((j > 0) & (j <= n))
        def _():
            attention(near_first(z, n, j - 1))

        i = j - 1 - lag

        @pl.when((i >= 0) & (i < 2))
        def _():
            down(near_first(z, n, n - 1 - i))

    turned_o = turned.at[: o_ref.shape[2]]
    transpose_rows(lay, o_ref, turned_o)
    for part in range(2):
        weight_gradient(lay, turned_o, full_ref, local_out, part, slice(0, full_ref.shape[2]))
    if fused:
        batch_out.start()
    for k in range(n):
        for h in range(heads):
            at = h * 3 * HD
            for rows, first, count in (
                (slice(0, img), k * img, img),
                (slice(img, lay.rows), far + k * txt, txt),
            ):
                dk = dk_s[h, :, first : first + count].T.astype(BF)
                dv = dv_s[h, :, first : first + count].T.astype(BF)
                dqkv_ref[k, rows, at : at + 3 * HD] = jnp.concatenate(
                    [dq_s[h, k, rows], dk, dv], 1
                )
    if fused:
        batch_out.pass_on()
    for i in range(2, n):
        down(near_first(z, n, n - 1 - i))
    res_ref[...] = (mid_ref[...] + acc[...]).astype(BF)
    if fused:
        exp_ref[...] = batch.total()
        out_ref[...] = batch_out.total()
        batch.finish()
        batch_out.finish()
        square_ref[...] = squares_of(exp_ref) + squares_of(out_ref)
    gather.finish()
    swap.finish(n)
    reduce.finish()

    @pl.loop(0, n)
    def _(k):
        act_copy(k, my_act).wait_send()


def pull(lay, fused, low, qkv, lse, wo, act, wr, mid, a2, dh, o):
    n, r, d, hid = lay.n_row, lay.rows, low.shape[1], act.shape[2]
    heads = qkv.shape[2] // (3 * HD)
    keys = n * r
    shapes = [(d, 2 * hid), (o.shape[2], d)]
    return call(
        partial(pull_kernel, lay, fused),
        4,
        [
            ((n, r, 3 * heads * HD), BF),
            ((n, r, 2 * hid), BF),
            ((r, d), BF),
            *[((2, s[0] // 4, s[1]), F32) if fused else ((2, *s), BF) for s in shapes],
            ((8, 128), F32),
        ],
        [
            pltpu.VMEM((heads, n, r, HD), BF),
            pltpu.VMEM((heads, keys, HD), BF),
            pltpu.VMEM((heads, keys, HD), BF),
            pltpu.VMEM((n, r, heads * HD), F32),
            pltpu.VMEM((n, r, heads * HD), BF),
            pltpu.VMEM((n, r, heads * HD), BF),
            pltpu.VMEM((r, heads * HD), BF),
            pltpu.VMEM((heads, n, r, HD), BF),
            pltpu.VMEM((heads, HD, keys), F32),
            pltpu.VMEM((heads, HD, keys), F32),
            pltpu.VMEM((r, d), F32),
            pltpu.VMEM((n, r, d), BF),
            pltpu.VMEM((n + 1, r, d), BF),
            pltpu.VMEM((d, keys), BF),
            pltpu.VMEM(wr.shape, BF),
            pltpu.VMEM((n, r, d), BF),
            dma(n),
            dma(1),
            dma(2, n),
            dma(n),
            dma(n),
            dma(n),
            dma(n),
            dma(n),
            dma(n),
            dma(n + 1),
            *([t for s in shapes for t in batch_scratch(*s)] if fused else []),
        ],
        10**10,
        low,
        qkv,
        lse,
        wo,
        act,
        wr,
        mid,
        a2,
        dh,
        o,
        far=(4, 5),
    )


def input_kernel(
    lay, fused, dqkv_ref, x_ref, dmid_ref, stat_ref, wa_any, a1_ref, g_ref, cb_ref, square_ref,
    dx_ref, att_ref, red_ref, norm_ref, *scratch
):
    (
        full, into, acc, r_out, inbox, stat_out, stat_in, turned, turned_g, wa_ref, w_load,
        s_send, s_recv, r_send, r_recv, t_send, t_recv,
    ) = scratch[:17]
    n = lay.n_row
    z, c = lax.axis_index("row"), lax.axis_index("col")
    half, d = dqkv_ref.shape[2], x_ref.shape[1]
    more = ()
    if fused:
        norm = Norm(4, n, *scratch[41:])
        more = norm.where()
    load = pltpu.make_async_copy(wa_any, wa_ref, w_load.at[0])
    load.start()
    greet(n, False, more)
    swap = Swap(dqkv_ref, into, s_send, s_recv)
    reduce = Reduce(acc, r_out, inbox, r_send, r_recv, n)
    own, other, red = (scratch[17 + 8 * i : 25 + 8 * i] for i in range(3)) if fused else (
        scratch[17:18], scratch[18:19], (red_ref,)
    )
    sums = [batch_of(s) for s in (own, other, red)] if fused else []

    @pl.loop(0, n)
    def _(j):
        swap.start(near_first(z, n, n - 1 - j))

    def gradient(turned, right, local, stripe):
        if stripe == right.shape[2]:
            for part in range(2):
                weight_gradient(lay, turned, right, local, part, slice(0, stripe))
            return

        @pl.loop(0, right.shape[2] // stripe)
        def _(i):
            cols = pl.ds(pl.multiple_of(i * stripe, 128), stripe)
            for part in range(2):
                weight_gradient(lay, turned, right, local, part, cols)

    transpose_rows(lay, a1_ref, turned)
    gradient(turned, dqkv_ref, own[0], half)
    if fused:
        sums[0].start()
    transpose_rows(lay, g_ref, turned_g)
    if fused:
        sums[0].pass_on()
    gradient(turned_g, cb_ref, red[0], STRIPE // 2)
    if fused:
        sums[2].start()
    lag = jnp.minimum(z, n - 1 - z)
    load.wait()

    @pl.loop(0, n + (n - 1) // 2)
    def _(j):
        i = j - lag

        @pl.when((i >= 0) & (i < n))
        def _():
            k = near_first(z, n, n - 1 - i)
            swap.arrive(k)
            mine, theirs = dqkv_ref[k], into[k]
            full[...] = jnp.concatenate(
                [jnp.where(c == 0, mine, theirs), jnp.where(c == 0, theirs, mine)], 1
            )
            for part, rows in parts_of(lay):
                acc[rows] = dot_nt(full[rows], wa_ref[part])

            @pl.when(i == n - 1)
            def _():
                gradient(turned, into, other[0], half)
                if fused:
                    sums[1].start()
                    sums[1].pass_on()

            reduce.add(k)

        if fused:

            @pl.when(j == 0)
            def _():
                sums[2].pass_on()

    mean, inverse = moments(stat_ref)
    normed = (x_ref[...].astype(F32) - mean) * inverse
    grad = acc[...]
    stat_out[0] = sums_of(grad, grad * normed)
    exchange(stat_out, stat_in, t_send, t_recv)
    back_one, back_two = columns(stat_out)
    dx_ref[...] = dmid_ref[...] + inverse * (grad - back_one - normed * back_two)
    if fused:
        red_ref[...] = sums[2].total()
        mine, theirs = sums[0].total(), sums[1].total()
    else:
        mine, theirs = own[0][...], other[0][...]
    att_ref[...] = jnp.concatenate(
        [jnp.where(c == 0, mine, theirs), jnp.where(c == 0, theirs, mine)], 2
    )
    if fused:
        squares = square_ref[...] + squares_of(att_ref) + squares_of(red_ref)
        norm_ref[...] = jnp.sqrt(norm.total(squares))
    for total in sums:
        total.finish()
    swap.finish(n)
    reduce.finish()


def inputs_back(lay, fused, dqkv, x, dmid, stat, wa, a1, g, cb, square):
    n, r, d, half = lay.n_row, lay.rows, x.shape[1], dqkv.shape[2]
    keys = n * r
    shapes = [(d, 2 * half), (g.shape[2], d)]
    return call(
        partial(input_kernel, lay, fused),
        5,
        [
            ((r, d), F32),
            *[((2, s[0] // 4, s[1]), F32) if fused else ((2, *s), BF) for s in shapes],
            ((8, 128), F32),
        ],
        [
            pltpu.VMEM((r, 2 * half), BF),
            pltpu.VMEM((n, r, half), BF),
            pltpu.VMEM((r, d), F32),
            pltpu.VMEM((n, r, d), BF),
            pltpu.VMEM((n + 1, r, d), BF),
            pltpu.VMEM((1, 8, r), F32),
            pltpu.VMEM((1, 8, r), F32),
            pltpu.VMEM((d, keys), BF),
            pltpu.VMEM((g.shape[2], keys), BF),
            pltpu.VMEM(wa.shape, BF),
            dma(1),
            dma(n),
            dma(n),
            dma(n),
            dma(n + 1),
            dma(1),
            dma(1),
            *(
                [
                    *batch_scratch(d, half),
                    *batch_scratch(d, half),
                    *batch_scratch(g.shape[2], d),
                    *norm_scratch(4, n),
                ]
                if fused
                else [pltpu.VMEM((2, d, half), BF)] * 2
            ),
        ],
        10**10,
        dqkv,
        x,
        dmid,
        stat,
        wa,
        a1,
        g,
        cb,
        square,
        far=(4,),
    )


def adamw(gradient, moment, square, weight, clip_factor):
    clipped = gradient * clip_factor
    moment_new = BETA_ONE * moment + (1.0 - BETA_ONE) * clipped
    square_new = BETA_TWO * square + (1.0 - BETA_TWO) * clipped * clipped
    corrected = (
        moment_new
        / (1.0 - BETA_ONE**STEP)
        / (jnp.sqrt(square_new / (1.0 - BETA_TWO**STEP)) + 1e-08)
    )
    return (moment_new, square_new, -RATE * (corrected + DECAY * weight))


def update_kernel(norm_ref, *refs):
    grads, moments_in, squares_in, weights = refs[0:4], refs[4:8], refs[8:12], refs[12:16]
    m_out, v_out, s_out, g_out = refs[16:20], refs[20:24], refs[24:28], refs[28:32]
    g_s, m_s, v_s, w_s, t_s = (refs[32 + 4 * i : 36 + 4 * i] for i in range(5))
    load, store = refs[52:]
    b = lax.axis_index("batch")
    loads = []
    for i in range(4):
        rows = grads[i].shape[1]
        part = pl.ds(pl.multiple_of(b * rows, 16), rows)
        for m in range(2):
            for q, (src, dst) in enumerate(
                (
                    (grads[i].at[m], g_s[i]),
                    (moments_in[i].at[m], m_s[i]),
                    (squares_in[i].at[m], v_s[i]),
                    (weights[i].at[m, part, :], w_s[i]),
                )
            ):
                loads.append(pltpu.make_async_copy(src, dst.at[m], load.at[i, m, q]))
                loads[-1].start()
    clip = jnp.minimum(1.0, 1.0 / (norm_ref[0:1, 0:1] + 1e-06))
    stores = []
    for i in range(4):
        for m in range(2):
            for q in range(4):
                loads[8 * i + 4 * m + q].wait()
            stores.append(pltpu.make_async_copy(g_s[i].at[m], g_out[i].at[m], store.at[i, m, 3]))
            stores[-1].start()

            @pl.loop(0, grads[i].shape[1] // TILE)
            def _(r):
                part = pl.ds(pl.multiple_of(r * TILE, TILE), TILE)
                new_m, new_v, step = adamw(
                    g_s[i][m, part, :],
                    m_s[i][m, part, :],
                    v_s[i][m, part, :],
                    w_s[i][m, part, :].astype(F32),
                    clip,
                )
                m_s[i][m, part, :] = new_m
                v_s[i][m, part, :] = new_v
                t_s[i][m, part, :] = step

            for q, (src, dst) in enumerate(
                ((m_s[i], m_out[i]), (v_s[i], v_out[i]), (t_s[i], s_out[i]))
            ):
                stores.append(pltpu.make_async_copy(src.at[m], dst.at[m], store.at[i, m, q]))
                stores[-1].start()
    for each in stores:
        each.wait()


TILE = 16


def update(norm, grads, ms, vs, ws):
    shapes = [g.shape for g in grads]
    outs = pl.pallas_call(
        update_kernel,
        out_shape=[jax.ShapeDtypeStruct(s, F32) for _ in range(4) for s in shapes],
        in_specs=[VMEM] + [ANY] * 16,
        out_specs=[ANY] * 16,
        scratch_shapes=[
            *[pltpu.VMEM(s, t) for t in (F32, F32, F32, BF, F32) for s in shapes],
            dma(4, 2, 4),
            dma(4, 2, 4),
        ],
        compiler_params=pltpu.CompilerParams(vmem_limit_bytes=60 * 2**20),
        cost_estimate=pl.CostEstimate(flops=10**8, bytes_accessed=5 * 10**7, transcendentals=0),
    )(norm, *grads, *ms, *vs, *ws)
    return outs[0:4], outs[4:8], outs[8:12], outs[12:16]


def weight_shard(weight, group_index, shard_rows):
    return lax.dynamic_slice_in_dim(weight, group_index * shard_rows, shard_rows, 1).astype(F32)


class Layout:
    def __init__(self, n_row, img, txt):
        self.n_row = n_row
        self.img = img
        self.txt = txt
        self.txt_pad = -(-txt // 16) * 16
        self.rows = img + self.txt_pad
        self.real = img + txt

    def pack(self, image, text):
        return jnp.concatenate(
            [image, text, jnp.zeros((self.txt_pad - self.txt, image.shape[1]), image.dtype)], 0
        )


def on_device(n_batch, n_row, *args):
    (
        image_input,
        text_input,
        image_cotan,
        text_cotan,
        seq_group,
        w_attend,
        w_output,
        w_expand,
        w_reduce,
        m_attend,
        m_output,
        m_expand,
        m_reduce,
        v_attend,
        v_output,
        v_expand,
        v_reduce,
    ) = args
    img, txt = image_input.shape[1], text_input.shape[1]
    lay = Layout(n_row, img, txt)
    group_index = lax.axis_index("batch")
    present = jnp.any(seq_group == group_index).astype(F32)

    low_x = lay.pack(image_input[0], text_input[0])
    low_cot = (lay.pack(image_cotan[0], text_cotan[0]).astype(F32) * present).astype(BF)
    fused = n_batch == 4

    a1_all, qkv, stat_one = attend(lay, low_x, w_attend)
    o_all, lse, cb_all, middle_x, a2_all, act, dh_all, grad_mid, low_mid = forward(
        lay, qkv, low_x, low_cot, w_output, w_reduce, w_expand
    )
    dqkv, g_all, result, g_exp, g_out, square = pull(
        lay, fused, low_mid, qkv, lse, w_output, act, w_reduce, middle_x, a2_all, dh_all, o_all
    )
    grad_in, g_att, g_red, norm = inputs_back(
        lay, fused, dqkv, low_x, grad_mid, stat_one, w_attend, a1_all, g_all, cb_all, square
    )
    sums = [g_att, g_out, g_exp, g_red]
    if not fused:
        sums = [
            lax.psum_scatter(g, "batch", scatter_dimension=1, tiled=True).astype(F32) for g in sums
        ]
    ms = (m_attend, m_output, m_expand, m_reduce)
    vs = (v_attend, v_output, v_expand, v_reduce)
    ws = (w_attend, w_output, w_expand, w_reduce)
    if fused:
        grad_norm = norm[0, 0]
        new_m, new_v, steps, sums = update(norm, sums, ms, vs, ws)
    else:
        squares = sum(jnp.sum(g * g) for g in sums)
        grad_norm = jnp.sqrt(lax.psum(lax.psum(lax.psum(squares, "batch"), "row"), "col"))
        clip_factor = jnp.minimum(1.0, 1.0 / (grad_norm + 1e-06))
        new_m, new_v, steps = zip(
            *[
                adamw(g, m, v, weight_shard(w, group_index, g.shape[1]), clip_factor)
                for g, m, v, w in zip(sums, ms, vs, ws)
            ]
        )
    return (
        result[:img][None],
        result[img : lay.real][None],
        grad_in[:img][None],
        grad_in[img : lay.real][None],
        *sums,
        *new_m,
        *new_v,
        *steps,
        grad_norm,
    )


def solution(mesh):
    tokens = P("batch", "row", "col")
    wide = P(None, "col", "row")
    tall = P(None, "row", "col")
    wide_shard = P(None, ("col", "batch"), "row")
    tall_shard = P(None, ("row", "batch"), "col")
    shards = (wide_shard, tall_shard, wide_shard, tall_shard)
    return jax.shard_map(
        partial(on_device, mesh.shape["batch"], mesh.shape["row"]),
        mesh=mesh,
        in_specs=(*[tokens] * 4, P(), wide, tall, wide, tall, *shards, *shards),
        out_specs=(*[tokens] * 4, *shards * 4, P()),
        check_vma=False,
    )
```

```python
import math
from functools import partial

import jax
import jax.numpy as jnp
from jax import lax
from jax.experimental import pallas as pl
from jax.experimental.pallas import tpu as pltpu
from jax.sharding import PartitionSpec as P

D = 1536
HD = 64
STEP = 10
STRIPE = 512

EPSILON = 1e-06
BETA_ONE = 0.9
BETA_TWO = 0.999
RATE = 0.02
DECAY = 0.1

BF = jnp.bfloat16
F32 = jnp.float32


def dot(a, b):
    return lax.dot_general(a, b, (((a.ndim - 1,), (0,)), ((), ())), preferred_element_type=F32)


def dot_nt(a, b):
    return lax.dot_general(a, b, (((a.ndim - 1,), (1,)), ((), ())), preferred_element_type=F32)


def dot_tn(a, b):
    return lax.dot_general(a, b, (((0,), (0,)), ((), ())), preferred_element_type=F32)


MESH = pl.DeviceIdType.MESH
VMEM = pl.BlockSpec(memory_space=pltpu.VMEM)
ANY = pl.BlockSpec(memory_space=pl.ANY)


def remote(src, dst, send, recv, **where):
    return pltpu.make_async_remote_copy(
        src_ref=src,
        dst_ref=dst,
        send_sem=send,
        recv_sem=recv,
        device_id=where,
        device_id_type=MESH,
    )


def near_first(z, n, j):
    alternate = jnp.where(j % 2 == 1, z - (j + 1) // 2, z + j // 2)
    reach = jnp.minimum(z, n - 1 - z)
    beyond = jnp.where(z <= n - 1 - z, j, n - 1 - j)
    return jnp.where(j <= 2 * reach, alternate, beyond)


def greet(n, fused=False, more=()):
    z, c = lax.axis_index("row"), lax.axis_index("col")
    barrier = pltpu.get_barrier_semaphore()
    pl.semaphore_signal(barrier, inc=1, device_id={"col": 1 - c}, device_id_type=MESH)

    @pl.when(z > 0)
    def _():
        pl.semaphore_signal(barrier, inc=1, device_id={"row": z - 1}, device_id_type=MESH)

    @pl.when(z < n - 1)
    def _():
        pl.semaphore_signal(barrier, inc=1, device_id={"row": z + 1}, device_id_type=MESH)

    if fused:
        b = lax.axis_index("batch")
        for other in (b + 1 - 2 * (b % 2), (b + 2) % 4):
            pl.semaphore_signal(barrier, inc=1, device_id={"batch": other}, device_id_type=MESH)
    ends = jnp.where(z > 0, 1, 0) + jnp.where(z < n - 1, 1, 0)
    for where in more:
        pl.semaphore_signal(barrier, inc=1, device_id=where, device_id_type=MESH)
    pl.semaphore_wait(barrier, ends + (3 if fused else 1) + len(more))


class Gather:
    def __init__(self, full, send, recv, n):
        self.full, self.send, self.recv, self.n = full, send, recv, n
        self.z = lax.axis_index("row")

    def copy(self, k, step):
        there = (self.z + step + self.n) % self.n
        way = 0 if step > 0 else 1
        return remote(
            self.full.at[k], self.full.at[k], self.send.at[way, k], self.recv.at[k], row=there
        )

    def push(self, k):
        @pl.when((k <= self.z) & (self.z < self.n - 1))
        def _():
            self.copy(k, 1).start()

        @pl.when((k >= self.z) & (self.z > 0))
        def _():
            self.copy(k, -1).start()

    def arrive(self, k):
        @pl.when(k != self.z)
        def _():
            self.copy(k, 1).wait_recv()

        self.push(k)

    def arrive_after_own(self, k):
        @pl.when(k != self.z)
        def _():
            self.arrive(k)

    def finish(self):
        @pl.loop(0, self.n)
        def _(k):
            @pl.when((k <= self.z) & (self.z < self.n - 1))
            def _():
                self.copy(k, 1).wait_send()

            @pl.when((k >= self.z) & (self.z > 0))
            def _():
                self.copy(k, -1).wait_send()


class Reduce:
    def __init__(self, acc, out, inbox, send, recv, n):
        self.acc, self.out, self.inbox, self.send, self.recv, self.n = acc, out, inbox, send, recv, n
        self.z = lax.axis_index("row")

    def copy(self, o):
        slot = jnp.where(o > self.z, o + 1, o)
        there = (self.z + jnp.where(o > self.z, 1, -1) + self.n) % self.n
        return remote(
            self.out.at[o], self.inbox.at[slot], self.send.at[o], self.recv.at[slot], row=there
        )

    def take(self, slot):
        remote(
            self.out.at[0],
            self.inbox.at[slot],
            self.send.at[0],
            self.recv.at[slot],
            row=(self.z + 1) % self.n,
        ).wait_recv()
        self.acc[...] += self.inbox[slot].astype(F32)

    def add(self, o):
        @pl.when((o >= self.z) & (self.z > 0))
        def _():
            self.take(o + 1)

        @pl.when((o <= self.z) & (self.z < self.n - 1))
        def _():
            self.take(o)

        @pl.when(o != self.z)
        def _():
            self.out[o] = self.acc[...].astype(BF)
            self.copy(o).start()

    def finish(self):
        @pl.loop(0, self.n)
        def _(o):
            @pl.when(o != self.z)
            def _():
                self.copy(o).wait_send()


class Swap:
    def __init__(self, out, into, send, recv):
        self.out, self.into, self.send, self.recv = out, into, send, recv

    def copy(self, k):
        return remote(
            self.out.at[k],
            self.into.at[k],
            self.send.at[k],
            self.recv.at[k],
            col=1 - lax.axis_index("col"),
        )

    def start(self, k):
        self.copy(k).start()

    def arrive(self, k):
        self.copy(k).wait_recv()

    def finish(self, n):
        @pl.loop(0, n)
        def _(k):
            self.copy(k).wait_send()


def sums_of(a, b):
    lane = lax.broadcasted_iota(jnp.int32, (a.shape[0], 128), 1)
    one, two = jnp.sum(a, axis=1, keepdims=True), jnp.sum(b, axis=1, keepdims=True)
    return jnp.where(lane == 0, one, jnp.where(lane == 1, two, 0.0)).T[:8]


def columns(stat):
    rows = stat[0]
    turned = jnp.concatenate([rows, jnp.zeros((120, rows.shape[1]), F32)], 0).T
    return turned[:, 0:1] / D, turned[:, 1:2] / D


def moments(stat):
    mean, square = columns(stat)
    return mean, lax.rsqrt(square - mean * mean + EPSILON)


def exchange(stat, stat_in, send, recv):
    swap = Swap(stat, stat_in, send, recv)
    swap.start(0)
    swap.arrive(0)
    swap.finish(1)
    stat[0] += stat_in[0]


def dma(*shape):
    return pltpu.SemaphoreType.DMA(shape)


def call(kernel, ident, outs, scratch, cost, *operands, far=()):
    return pl.pallas_call(
        kernel,
        out_shape=[jax.ShapeDtypeStruct(s, t) for s, t in outs],
        in_specs=[ANY if i in far else VMEM for i in range(len(operands))],
        out_specs=[VMEM] * len(outs),
        scratch_shapes=scratch,
        compiler_params=pltpu.CompilerParams(
            collective_id=ident, has_side_effects=True, vmem_limit_bytes=60 * 2**20
        ),
        cost_estimate=pl.CostEstimate(flops=cost, bytes_accessed=10**7, transcendentals=0),
    )(*operands)


def parts_of(lay):
    return ((0, slice(0, lay.img)), (1, slice(lay.img, lay.rows)))


def attend_kernel(lay, x_ref, w_ref, full_ref, qkv_ref, stat_ref, *scratch):
    own, out, into, stat_in, g_send, g_recv, s_send, s_recv, t_send, t_recv = scratch
    n = lay.n_row
    z, c = lax.axis_index("row"), lax.axis_index("col")
    half = qkv_ref.shape[2]
    greet(n)
    x = x_ref[...].astype(F32)
    stat_ref[0] = sums_of(x, x * x)
    exchange(stat_ref, stat_in, t_send, t_recv)
    mean, inverse = moments(stat_ref)
    full_ref[z] = ((x - mean) * inverse).astype(BF)
    gather = Gather(full_ref, g_send, g_recv, n)
    swap = Swap(out, into, s_send, s_recv)

    @pl.loop(0, n)
    def _(j):
        k = near_first(z, n, j)
        gather.arrive(k)
        for part, rows in parts_of(lay):
            p = dot(full_ref[k, rows], w_ref[part])
            low, high = p[:, :half], p[:, half:]
            own[k, rows] = jnp.where(c == 0, low, high)
            out[k, rows] = jnp.where(c == 0, high, low).astype(BF)
        swap.start(k)

    @pl.loop(0, n)
    def _(j):
        k = near_first(z, n, j)
        swap.arrive(k)
        qkv_ref[k] = (own[k] + into[k].astype(F32)).astype(BF)

    gather.finish()
    swap.finish(n)


def attend(lay, x, w):
    n, r, half, d = lay.n_row, lay.rows, w.shape[2] // 2, x.shape[1]
    return call(
        partial(attend_kernel, lay),
        1,
        [((n, r, d), BF), ((n, r, half), BF), ((1, 8, r), F32)],
        [
            pltpu.VMEM((n, r, half), F32),
            pltpu.VMEM((n, r, half), BF),
            pltpu.VMEM((n, r, half), BF),
            pltpu.VMEM((1, 8, r), F32),
            dma(2, n),
            dma(n),
            dma(n),
            dma(n),
            dma(1),
            dma(1),
        ],
        2 * n * r * w.shape[1] * w.shape[2],
        x,
        w,
    )


def split_heads(lay, qkv_ref, q_ref, k_ref, v_ref, fill):
    n, img, txt = lay.n_row, lay.img, lay.txt_pad
    heads = qkv_ref.shape[2] // (3 * HD)

    @pl.loop(0, n)
    def _(k):
        first = pl.ds(pl.multiple_of(k * img, 16), img)
        second = pl.ds(pl.multiple_of(n * img + k * txt, 16), txt)
        for h in range(heads):
            at = h * 3 * HD
            rows = qkv_ref[k, :, at : at + 3 * HD]
            q_ref[h, k] = rows[:, :HD] * jnp.asarray(HD**-0.5, BF)
            for ref, lo in ((k_ref, HD), (v_ref, 2 * HD)):
                value = rows[:, lo : lo + HD]
                if ref is v_ref and fill:
                    value = jnp.concatenate([value, jnp.ones_like(value)], 1)
                ref[h, first] = value[:img]
                ref[h, second] = value[img:]


def text_bias(lay):
    lane = lax.broadcasted_iota(jnp.int32, (1, lay.n_row * lay.txt_pad), 1)
    return jnp.where(lane % lay.txt_pad < lay.txt, 0.0, -1e30)


def middle_kernel(
    lay, loads, qkv_ref, x_ref, cot_ref, wo_ref, wr_ref, o_ref, lse_ref, cb_ref, dg_ref, mid_ref, low_ref, stat_ref, *scratch
):
    (
        q_s, k_s, v_s, o_out, o_in, dg_out, dg_in, acc, r_out, inbox, stat_in,
        g_send, g_recv, o_send, o_recv, d_send, d_recv, r_send, r_recv, t_send, t_recv,
    ) = scratch
    n, far = lay.n_row, lay.n_row * lay.img
    z, c = lax.axis_index("row"), lax.axis_index("col")
    heads, hid = q_s.shape[0], dg_ref.shape[2]
    greet(n)
    gather = Gather(cb_ref, g_send, g_recv, n)
    cb_ref[z] = cot_ref[...]
    gather.push(z)
    swap_o = Swap(o_out, o_in, o_send, o_recv)
    swap_d = Swap(dg_out, dg_in, d_send, d_recv)
    reduce = Reduce(acc, r_out, inbox, r_send, r_recv, n)
    split_heads(lay, qkv_ref, q_s, k_s, v_s, True)
    bias = text_bias(lay)
    lane = lax.broadcasted_iota(jnp.int32, (lay.rows, 128), 1)

    def attention(k):
        outs, lse = [], jnp.zeros((lay.rows, 128), F32)
        for h in range(heads):
            q = q_s[h, k]
            s1 = dot_nt(q, k_s[h, :far])
            s2 = dot_nt(q, k_s[h, far:]) + bias
            peak = jnp.maximum(
                jnp.max(s1, axis=1, keepdims=True), jnp.max(s2, axis=1, keepdims=True)
            )
            e1, e2 = jnp.exp(s1 - peak).astype(BF), jnp.exp(s2 - peak).astype(BF)
            o = dot(e1, v_s[h, :far]) + dot(e2, v_s[h, far:])
            total = o[:, HD : HD + 1]
            outs.append((o[:, :HD] / total).astype(BF))
            lse = jnp.where(lane == h, peak + jnp.log(total), lse)
        lse_ref[k] = lse
        o_out[k] = jnp.concatenate(outs, 1)

    def project(k):
        swap_o.arrive(k)
        own, other = o_out[k], o_in[k]
        o_ref[k] = jnp.concatenate(
            [jnp.where(c == 0, own, other), jnp.where(c == 0, other, own)], 1
        )
        for part, rows in parts_of(lay):
            acc[rows] = dot(o_ref[k, rows], wo_ref[part])
        reduce.add(k)

    def step(j):
        k = near_first(z, n, n - 1 - j)
        attention(k)
        swap_o.start(k)

        @pl.when(j == 0)
        def _():
            loads[0].wait()
            loads[1].wait()

        near = near_first(z, n, j)
        gather.arrive_after_own(near)
        for part, rows in parts_of(lay):
            dg_out[near, rows] = dot_nt(
                cb_ref[near, rows], wr_ref[part, pl.ds(pl.multiple_of((1 - c) * hid, 128), hid), :]
            ).astype(BF)
        swap_d.start(near)
        for part, rows in parts_of(lay):
            dg_ref[near, rows] = dot_nt(
                cb_ref[near, rows], wr_ref[part, pl.ds(pl.multiple_of(c * hid, 128), hid), :]
            )

    lag = 1 + jnp.minimum(z, n - 1 - z)

    @pl.loop(0, n + 1 + (n - 1) // 2)
    def _(j):
        @pl.when(j < n)
        def _():
            step(j)

        i = j - lag

        @pl.when((i >= 0) & (i < n))
        def _():
            project(near_first(z, n, n - 1 - i))

    mid = x_ref[...].astype(F32) + acc[...]
    mid_ref[...] = mid
    stat_ref[0] = sums_of(mid, mid * mid)
    exchange(stat_ref, stat_in, t_send, t_recv)
    mean, inverse = moments(stat_ref)
    low_ref[...] = ((mid - mean) * inverse).astype(BF)

    def settle():
        @pl.loop(0, n)
        def _(j):
            k = near_first(z, n, j)
            swap_d.arrive(k)
            dg_ref[k] += dg_in[k].astype(F32)

        gather.finish()
        swap_o.finish(n)
        swap_d.finish(n)
        reduce.finish()

    return settle


SLOPE = (2.0 / math.pi) ** 0.5
CUBIC = 0.044715


def gelu_pair(u):
    square = u * u
    t = jnp.tanh(SLOPE * u * (1.0 + CUBIC * square))
    half = 0.5 * (1.0 + t)
    slope = half + 0.5 * u * (1.0 - t * t) * (SLOPE * (1.0 + 3.0 * CUBIC * square))
    return u * half, slope


def hidden_kernel(
    lay, settle, low_ref, dg_ref, mid_ref, cot_ref, stat_ref, we_ref, full_ref, act_ref, dh_ref, dmid_ref, dy_ref, *scratch
):
    (
        own, out, into, acc, r_out, inbox, stat_out, stat_in,
        g_send, g_recv, s_send, s_recv, d_send, d_recv, r_send, r_recv, t_send, t_recv,
    ) = scratch
    n = lay.n_row
    z, c = lax.axis_index("row"), lax.axis_index("col")
    hid = dg_ref.shape[2]
    mine = pl.ds(pl.multiple_of(c * hid, 128), hid)
    theirs = pl.ds(pl.multiple_of((1 - c) * hid, 128), hid)
    gather = Gather(full_ref, g_send, g_recv, n)
    full_ref[z] = low_ref[...]
    gather.push(z)
    swap = Swap(out, into, s_send, s_recv)
    reduce = Reduce(acc, r_out, inbox, r_send, r_recv, n)

    def dh_copy(k):
        half = dh_ref.at[k, :, mine]
        return remote(half, half, d_send.at[k], d_recv.at[k], col=1 - c)

    @pl.loop(0, n)
    def _(j):
        k = near_first(z, n, j)
        gather.arrive_after_own(k)
        for part, rows in parts_of(lay):
            out[k, rows] = dot(full_ref[k, rows], we_ref[part, :, theirs]).astype(BF)
        swap.start(k)
        for part, rows in parts_of(lay):
            own[k, rows] = dot(full_ref[k, rows], we_ref[part, :, mine])

    def back(k):
        half = dh_ref.at[k, :, theirs]
        remote(half, half, d_send.at[k], d_recv.at[k], col=1 - c).wait_recv()
        for part, rows in parts_of(lay):
            acc[rows] = dot_nt(dh_ref[k, rows], we_ref[part])
        reduce.add(k)

    settle()

    @pl.loop(0, n + 2)
    def _(j):
        @pl.when(j < n)
        def _():
            k = near_first(z, n, n - 1 - j)
            swap.arrive(k)
            act, slope = gelu_pair(own[k] + into[k].astype(F32))
            act_ref[k] = act.astype(BF)
            dh_ref[k, :, mine] = (dg_ref[k] * slope).astype(BF)
            dh_copy(k).start()

        @pl.when(j > 1)
        def _():
            back(near_first(z, n, n + 1 - j))

    mean, inverse = moments(stat_ref)
    normed = (mid_ref[...] - mean) * inverse
    grad = acc[...]
    stat_out[0] = sums_of(grad, grad * normed)
    exchange(stat_out, stat_in, t_send, t_recv)
    back_one, back_two = columns(stat_out)
    dmid = cot_ref[...].astype(F32) + inverse * (grad - back_one - normed * back_two)
    dmid_ref[...] = dmid
    dy_ref[...] = dmid.astype(BF)
    gather.finish()
    swap.finish(n)
    reduce.finish()

    @pl.loop(0, n)
    def _(k):
        dh_copy(k).wait_send()


def forward_kernel(
    lay, qkv_ref, x_ref, cot_ref, wo_ref, wr_any, we_any,
    o_ref, lse_ref, cb_ref, mid_ref, a2_ref, act_ref, dh_ref, dmid_ref, dy_ref, *scratch
):
    dg_ref, low_ref, stat_ref, wr_ref, we_ref, w_load = scratch[:6]
    loads = [
        pltpu.make_async_copy(wr_any, wr_ref, w_load.at[0]),
        pltpu.make_async_copy(we_any, we_ref, w_load.at[1]),
    ]
    for each in loads:
        each.start()
    settle = middle_kernel(
        lay, loads, qkv_ref, x_ref, cot_ref, wo_ref, wr_ref, o_ref, lse_ref, cb_ref, dg_ref, mid_ref, low_ref, stat_ref, *scratch[6:27]
    )
    hidden_kernel(
        lay, settle, low_ref, dg_ref, mid_ref, cot_ref, stat_ref, we_ref, a2_ref, act_ref, dh_ref, dmid_ref, dy_ref, *scratch[27:]
    )


def forward(lay, qkv, x, cot, wo, wr, we):
    n, r, d = lay.n_row, lay.rows, x.shape[1]
    heads, hid = qkv.shape[2] // (3 * HD), wr.shape[1] // 2
    keys = n * r
    return call(
        partial(forward_kernel, lay),
        2,
        [
            ((n, r, 2 * heads * HD), BF),
            ((n, r, 128), F32),
            ((n, r, d), BF),
            ((r, d), F32),
            ((n, r, d), BF),
            ((n, r, hid), BF),
            ((n, r, 2 * hid), BF),
            ((r, d), F32),
            ((r, d), BF),
        ],
        [
            pltpu.VMEM((n, r, hid), F32),
            pltpu.VMEM((r, d), BF),
            pltpu.VMEM((1, 8, r), F32),
            pltpu.VMEM(wr.shape, BF),
            pltpu.VMEM(we.shape, BF),
            dma(2),
            pltpu.VMEM((heads, n, r, HD), BF),
            pltpu.VMEM((heads, keys, HD), BF),
            pltpu.VMEM((heads, keys, 2 * HD), BF),
            pltpu.VMEM((n, r, heads * HD), BF),
            pltpu.VMEM((n, r, heads * HD), BF),
            pltpu.VMEM((n, r, hid), BF),
            pltpu.VMEM((n, r, hid), BF),
            pltpu.VMEM((r, d), F32),
            pltpu.VMEM((n, r, d), BF),
            pltpu.VMEM((n + 1, r, d), BF),
            pltpu.VMEM((1, 8, r), F32),
            dma(2, n),
            dma(n),
            dma(n),
            dma(n),
            dma(n),
            dma(n),
            dma(n),
            dma(n + 1),
            dma(1),
            dma(1),
            pltpu.VMEM((n, r, hid), F32),
            pltpu.VMEM((n, r, hid), BF),
            pltpu.VMEM((n, r, hid), BF),
            pltpu.VMEM((r, d), F32),
            pltpu.VMEM((n, r, d), BF),
            pltpu.VMEM((n + 1, r, d), BF),
            pltpu.VMEM((1, 8, r), F32),
            pltpu.VMEM((1, 8, r), F32),
            dma(2, n),
            dma(n),
            dma(n),
            dma(n),
            dma(n),
            dma(n),
            dma(n),
            dma(n + 1),
            dma(1),
            dma(1),
        ],
        10**10,
        qkv,
        x,
        cot,
        wo,
        wr,
        we,
        far=(4, 5),
    )


class BatchSum:
    def __init__(self, local, first, out, second, sems):
        self.local, self.first, self.out, self.second = local, first, out, second
        self.f_send, self.f_recv, self.s_send, self.s_recv = sems
        b = lax.axis_index("batch")
        self.x, self.core = b // 2, b % 2
        self.to_core, self.to_x = 2 * self.x + 1 - self.core, 2 * (1 - self.x) + self.core
        self.s = out.shape[1]

    def rows(self, block):
        return pl.ds(pl.multiple_of(block * self.s, 16), self.s)

    def core_copy(self, q):
        block = 2 * q + 1 - self.core
        return remote(
            self.local.at[:, self.rows(block), :],
            self.first.at[q],
            self.f_send.at[q],
            self.f_recv.at[q],
            batch=self.to_core,
        )

    def x_copy(self):
        return remote(self.out, self.second, self.s_send.at[0], self.s_recv.at[0], batch=self.to_x)

    def start(self):
        self.core_copy(1 - self.x).start()
        self.core_copy(self.x).start()

    def block(self, q):
        self.core_copy(q).wait_recv()
        mine = self.local[:, self.rows(2 * q + self.core), :].astype(F32)
        return mine + self.first[q].astype(F32)

    def pass_on(self):
        self.out[...] = self.block(1 - self.x).astype(BF)
        self.x_copy().start()

    def total(self):
        near = self.block(self.x)
        self.x_copy().wait_recv()
        return near + self.second[...].astype(F32)

    def finish(self):
        self.core_copy(0).wait_send()
        self.core_copy(1).wait_send()
        self.x_copy().wait_send()


def batch_scratch(rows, cols):
    s = rows // 4
    return [
        pltpu.VMEM((2, rows, cols), BF),
        pltpu.VMEM((2, 2, s, cols), BF),
        pltpu.VMEM((2, s, cols), BF),
        pltpu.VMEM((2, s, cols), BF),
        dma(2),
        dma(2),
        dma(1),
        dma(1),
    ]


def batch_of(scratch):
    return BatchSum(*scratch[:4], scratch[4:])


def squares_of(ref):
    total = jnp.zeros((1, 1), F32)
    for m in range(2):
        lanes = jnp.sum(ref[m] * ref[m], axis=0, keepdims=True)
        total += jnp.sum(lanes, axis=1, keepdims=True)
    return jnp.broadcast_to(total, (8, 128))


class Norm:
    def __init__(self, n_batch, n_row, plane, line, p_send, p_recv, b_send, b_recv):
        self.n_batch, self.plane, self.line = n_batch, plane, line
        self.p_send, self.p_recv, self.b_send, self.b_recv = p_send, p_recv, b_send, b_recv
        self.b, z, c = lax.axis_index("batch"), lax.axis_index("row"), lax.axis_index("col")
        self.me = z * 2 + c
        self.peers = [((z + i) % n_row, (c + j) % 2) for i in range(n_row) for j in range(2)][1:]

    def where(self):
        return [{"row": row, "col": col} for row, col in self.peers] + [
            {"batch": (self.b + i) % self.n_batch} for i in range(1, self.n_batch)
        ]

    def to_plane(self, i, slot):
        row, col = self.peers[i]
        block = self.plane.at[slot]
        return remote(block, block, self.p_send.at[i], self.p_recv.at[slot], row=row, col=col)

    def to_line(self, i, slot):
        block = self.line.at[slot]
        other = (self.b + i) % self.n_batch
        return remote(block, block, self.b_send.at[i], self.b_recv.at[slot], batch=other)

    def total(self, tile):
        b, n_batch = self.b, self.n_batch
        self.plane[self.me] = tile
        for i in range(len(self.peers)):
            self.to_plane(i, self.me).start()
        for i, (row, col) in enumerate(self.peers):
            self.to_plane(i, row * 2 + col).wait_recv()
        self.line[b] = jnp.sum(self.plane[...], axis=0)
        for i in range(1, n_batch):
            self.to_line(i, b).start()
        for i in range(1, n_batch):
            self.to_line(i, (b + i) % n_batch).wait_recv()
        for i in range(len(self.peers)):
            self.to_plane(i, self.me).wait_send()
        for i in range(1, n_batch):
            self.to_line(i, b).wait_send()
        return jnp.sum(self.line[...], axis=0)


def norm_scratch(n_batch, n_row):
    return [
        pltpu.VMEM((2 * n_row, 8, 128), F32),
        pltpu.VMEM((n_batch, 8, 128), F32),
        dma(2 * n_row - 1),
        dma(2 * n_row),
        dma(n_batch),
        dma(n_batch),
    ]


def transpose_rows(lay, left, turned):
    n, img, far = lay.n_row, lay.img, lay.n_row * lay.img
    for k in range(n):
        turned[:, k * img : (k + 1) * img] = left[k, :img, :].T
    turned[:, far:] = jnp.concatenate([left[k, img:, :] for k in range(n)], 0).T


def weight_gradient(lay, turned, right, local, part, cols):
    n, img, far = lay.n_row, lay.img, lay.n_row * lay.img
    if part == 0:
        total = dot(turned[:, :img], right[0, :img, cols])
        for k in range(1, n):
            total += dot(turned[:, k * img : (k + 1) * img], right[k, :img, cols])
    else:
        text = jnp.concatenate([right[k, img:, cols] for k in range(n)], 0)
        total = dot(turned[:, far:], text)
    local[part, :, cols] = total.astype(BF)


def pull_kernel(
    lay, fused, low_ref, qkv_ref, lse_ref, wo_ref, act_ref, wr_any, mid_ref, a2_ref, dh_ref, o_ref,
    dqkv_ref, g_ref, res_ref, exp_ref, out_ref, square_ref, *scratch
):
    (
        q_s, k_s, v_s, do_own, do_out, do_in, do_s, dq_s, dk_s, dv_s, acc, r_out, inbox, turned, wr_ref, full_ref, a_load, w_load,
        g_send, g_recv, s_send, s_recv, a_send, a_recv, r_send, r_recv,
    ) = scratch[:26]
    n, img, txt, far = lay.n_row, lay.img, lay.txt_pad, lay.n_row * lay.img
    z, c = lax.axis_index("row"), lax.axis_index("col")
    heads, half, hid = q_s.shape[0], do_own.shape[2], act_ref.shape[2]
    mine = pl.ds(pl.multiple_of(c * half, 16), half)
    theirs = pl.ds(pl.multiple_of((1 - c) * half, 16), half)
    my_act = pl.ds(pl.multiple_of(c * hid, 128), hid)
    their_act = pl.ds(pl.multiple_of((1 - c) * hid, 128), hid)
    greet(n, fused)
    gather = Gather(full_ref, g_send, g_recv, n)
    full_ref[z] = low_ref[...]
    gather.push(z)
    swap = Swap(do_out, do_in, s_send, s_recv)
    reduce = Reduce(acc, r_out, inbox, r_send, r_recv, n)
    local, local_out = exp_ref, out_ref
    if fused:
        batch, batch_out = batch_of(scratch[26:34]), batch_of(scratch[34:42])
        local, local_out = batch.local, batch_out.local
    split_heads(lay, qkv_ref, q_s, k_s, v_s, False)
    bias = text_bias(lay)
    dk_s[...] = jnp.zeros_like(dk_s)
    dv_s[...] = jnp.zeros_like(dv_s)
    lag = jnp.minimum(z, n - 1 - z)

    def act_copy(k, where):
        block = g_ref.at[k, :, where]
        return remote(block, block, a_send.at[k], a_recv.at[k], col=1 - c)

    def load(k):
        return pltpu.make_async_copy(act_ref.at[k], g_ref.at[k, :, my_act], a_load.at[k])

    def wr_load():
        return pltpu.make_async_copy(wr_any, wr_ref, w_load.at[0])

    wr_load().start()
    for k in range(n):
        load(k).start()

    def arrive(k):
        gather.arrive_after_own(k)
        for part, rows in parts_of(lay):
            do_out[k, rows] = dot_nt(full_ref[k, rows], wo_ref[part, theirs, :]).astype(BF)
        swap.start(k)
        for part, rows in parts_of(lay):
            do_own[k, rows] = dot_nt(full_ref[k, rows], wo_ref[part, mine, :])

    def expand_gradient():
        transpose_rows(lay, a2_ref, turned)

        @pl.loop(0, 2 * hid // STRIPE)
        def _(i):
            cols = pl.ds(pl.multiple_of(i * STRIPE, 128), STRIPE)
            for part in range(2):
                weight_gradient(lay, turned, dh_ref, local, part, cols)

    def attention(k):
        swap.arrive(k)
        do_s[...] = (do_own[k] + do_in[k].astype(F32)).astype(BF)
        for h in range(heads):
            q, do = q_s[h, k], do_s[:, h * HD : (h + 1) * HD]
            lse = lse_ref[k, :, h : h + 1]
            p1 = jnp.exp(dot_nt(q, k_s[h, :far]) - lse)
            p2 = jnp.exp(dot_nt(q, k_s[h, far:]) + bias - lse)
            dp1 = dot_nt(do, v_s[h, :far])
            dp2 = dot_nt(do, v_s[h, far:])
            row = jnp.sum(p1 * dp1, axis=1, keepdims=True) + jnp.sum(
                p2 * dp2, axis=1, keepdims=True
            )
            ds1 = (p1 * (dp1 - row)).astype(BF)
            ds2 = (p2 * (dp2 - row)).astype(BF)
            dq = (dot(ds1, k_s[h, :far]) + dot(ds2, k_s[h, far:])) * HD**-0.5
            dq_s[h, k] = dq.astype(BF)
            dk_s[h, :, :far] += dot_tn(q, ds1)
            dk_s[h, :, far:] += dot_tn(q, ds2)
            dv_s[h, :, :far] += dot_tn(do, p1.astype(BF))
            dv_s[h, :, far:] += dot_tn(do, p2.astype(BF))

    def down(k):
        act_copy(k, their_act).wait_recv()
        for part, rows in parts_of(lay):
            acc[rows] = dot(g_ref[k, rows], wr_ref[part])
        reduce.add(k)

    @pl.loop(0, n + 1)
    def _(j):
        @pl.when(j < n)
        def _():
            arrive(near_first(z, n, j))

        @pl.when(j < 2)
        def _():
            load(near_first(z, n, n - 1 - j)).wait()
            act_copy(near_first(z, n, n - 1 - j), my_act).start()

        @pl.when(j == n - 1)
        def _():
            for i in range(2, n):
                load(near_first(z, n, n - 1 - i)).wait()
                act_copy(near_first(z, n, n - 1 - i), my_act).start()

        @pl.when(j == 0)
        def _():
            expand_gradient()
            wr_load().wait()
            if fused:
                batch.start()

        if fused:

            @pl.when(j == 2)
            def _():
                batch.pass_on()

        @pl.when((j > 0) & (j <= n))
        def _():
            attention(near_first(z, n, j - 1))

        i = j - 1 - lag

        @pl.when((i >= 0) & (i < 2))
        def _():
            down(near_first(z, n, n - 1 - i))

    turned_o = turned.at[: o_ref.shape[2]]
    transpose_rows(lay, o_ref, turned_o)
    for part in range(2):
        weight_gradient(lay, turned_o, full_ref, local_out, part, slice(0, full_ref.shape[2]))
    if fused:
        batch_out.start()
    for k in range(n):
        for h in range(heads):
            at = h * 3 * HD
            for rows, first, count in (
                (slice(0, img), k * img, img),
                (slice(img, lay.rows), far + k * txt, txt),
            ):
                dk = dk_s[h, :, first : first + count].T.astype(BF)
                dv = dv_s[h, :, first : first + count].T.astype(BF)
                dqkv_ref[k, rows, at : at + 3 * HD] = jnp.concatenate(
                    [dq_s[h, k, rows], dk, dv], 1
                )
    if fused:
        batch_out.pass_on()
    for i in range(2, n):
        down(near_first(z, n, n - 1 - i))
    res_ref[...] = (mid_ref[...] + acc[...]).astype(BF)
    if fused:
        exp_ref[...] = batch.total()
        out_ref[...] = batch_out.total()
        batch.finish()
        batch_out.finish()
        square_ref[...] = squares_of(exp_ref) + squares_of(out_ref)
    gather.finish()
    swap.finish(n)
    reduce.finish()

    @pl.loop(0, n)
    def _(k):
        act_copy(k, my_act).wait_send()


def pull(lay, fused, low, qkv, lse, wo, act, wr, mid, a2, dh, o):
    n, r, d, hid = lay.n_row, lay.rows, low.shape[1], act.shape[2]
    heads = qkv.shape[2] // (3 * HD)
    keys = n * r
    shapes = [(d, 2 * hid), (o.shape[2], d)]
    return call(
        partial(pull_kernel, lay, fused),
        4,
        [
            ((n, r, 3 * heads * HD), BF),
            ((n, r, 2 * hid), BF),
            ((r, d), BF),
            *[((2, s[0] // 4, s[1]), F32) if fused else ((2, *s), BF) for s in shapes],
            ((8, 128), F32),
        ],
        [
            pltpu.VMEM((heads, n, r, HD), BF),
            pltpu.VMEM((heads, keys, HD), BF),
            pltpu.VMEM((heads, keys, HD), BF),
            pltpu.VMEM((n, r, heads * HD), F32),
            pltpu.VMEM((n, r, heads * HD), BF),
            pltpu.VMEM((n, r, heads * HD), BF),
            pltpu.VMEM((r, heads * HD), BF),
            pltpu.VMEM((heads, n, r, HD), BF),
            pltpu.VMEM((heads, HD, keys), F32),
            pltpu.VMEM((heads, HD, keys), F32),
            pltpu.VMEM((r, d), F32),
            pltpu.VMEM((n, r, d), BF),
            pltpu.VMEM((n + 1, r, d), BF),
            pltpu.VMEM((d, keys), BF),
            pltpu.VMEM(wr.shape, BF),
            pltpu.VMEM((n, r, d), BF),
            dma(n),
            dma(1),
            dma(2, n),
            dma(n),
            dma(n),
            dma(n),
            dma(n),
            dma(n),
            dma(n),
            dma(n + 1),
            *([t for s in shapes for t in batch_scratch(*s)] if fused else []),
        ],
        10**10,
        low,
        qkv,
        lse,
        wo,
        act,
        wr,
        mid,
        a2,
        dh,
        o,
        far=(4, 5),
    )


def input_kernel(
    lay, fused, dqkv_ref, x_ref, dmid_ref, stat_ref, wa_any, a1_ref, g_ref, cb_ref, square_ref,
    dx_ref, att_ref, red_ref, norm_ref, *scratch
):
    (
        full, into, acc, r_out, inbox, stat_out, stat_in, turned, turned_g, wa_ref, w_load,
        s_send, s_recv, r_send, r_recv, t_send, t_recv,
    ) = scratch[:17]
    n = lay.n_row
    z, c = lax.axis_index("row"), lax.axis_index("col")
    half, d = dqkv_ref.shape[2], x_ref.shape[1]
    more = ()
    if fused:
        norm = Norm(4, n, *scratch[41:])
        more = norm.where()
    load = pltpu.make_async_copy(wa_any, wa_ref, w_load.at[0])
    load.start()
    greet(n, False, more)
    swap = Swap(dqkv_ref, into, s_send, s_recv)
    reduce = Reduce(acc, r_out, inbox, r_send, r_recv, n)
    own, other, red = (scratch[17 + 8 * i : 25 + 8 * i] for i in range(3)) if fused else (
        scratch[17:18], scratch[18:19], (red_ref,)
    )
    sums = [batch_of(s) for s in (own, other, red)] if fused else []

    @pl.loop(0, n)
    def _(j):
        swap.start(near_first(z, n, n - 1 - j))

    def gradient(turned, right, local, stripe):
        if stripe == right.shape[2]:
            for part in range(2):
                weight_gradient(lay, turned, right, local, part, slice(0, stripe))
            return

        @pl.loop(0, right.shape[2] // stripe)
        def _(i):
            cols = pl.ds(pl.multiple_of(i * stripe, 128), stripe)
            for part in range(2):
                weight_gradient(lay, turned, right, local, part, cols)

    transpose_rows(lay, a1_ref, turned)
    gradient(turned, dqkv_ref, own[0], half)
    if fused:
        sums[0].start()
    transpose_rows(lay, g_ref, turned_g)
    if fused:
        sums[0].pass_on()
    gradient(turned_g, cb_ref, red[0], STRIPE // 2)
    if fused:
        sums[2].start()
    lag = jnp.minimum(z, n - 1 - z)
    load.wait()

    @pl.loop(0, n + (n - 1) // 2)
    def _(j):
        i = j - lag

        @pl.when((i >= 0) & (i < n))
        def _():
            k = near_first(z, n, n - 1 - i)
            swap.arrive(k)
            mine, theirs = dqkv_ref[k], into[k]
            full[...] = jnp.concatenate(
                [jnp.where(c == 0, mine, theirs), jnp.where(c == 0, theirs, mine)], 1
            )
            for part, rows in parts_of(lay):
                acc[rows] = dot_nt(full[rows], wa_ref[part])

            @pl.when(i == n - 1)
            def _():
                gradient(turned, into, other[0], half)
                if fused:
                    sums[1].start()
                    sums[1].pass_on()

            reduce.add(k)

        if fused:

            @pl.when(j == 0)
            def _():
                sums[2].pass_on()

    mean, inverse = moments(stat_ref)
    normed = (x_ref[...].astype(F32) - mean) * inverse
    grad = acc[...]
    stat_out[0] = sums_of(grad, grad * normed)
    exchange(stat_out, stat_in, t_send, t_recv)
    back_one, back_two = columns(stat_out)
    dx_ref[...] = dmid_ref[...] + inverse * (grad - back_one - normed * back_two)
    if fused:
        red_ref[...] = sums[2].total()
        mine, theirs = sums[0].total(), sums[1].total()
    else:
        mine, theirs = own[0][...], other[0][...]
    att_ref[...] = jnp.concatenate(
        [jnp.where(c == 0, mine, theirs), jnp.where(c == 0, theirs, mine)], 2
    )
    if fused:
        squares = square_ref[...] + squares_of(att_ref) + squares_of(red_ref)
        norm_ref[...] = jnp.sqrt(norm.total(squares))
    for total in sums:
        total.finish()
    swap.finish(n)
    reduce.finish()


def inputs_back(lay, fused, dqkv, x, dmid, stat, wa, a1, g, cb, square):
    n, r, d, half = lay.n_row, lay.rows, x.shape[1], dqkv.shape[2]
    keys = n * r
    shapes = [(d, 2 * half), (g.shape[2], d)]
    return call(
        partial(input_kernel, lay, fused),
        5,
        [
            ((r, d), F32),
            *[((2, s[0] // 4, s[1]), F32) if fused else ((2, *s), BF) for s in shapes],
            ((8, 128), F32),
        ],
        [
            pltpu.VMEM((r, 2 * half), BF),
            pltpu.VMEM((n, r, half), BF),
            pltpu.VMEM((r, d), F32),
            pltpu.VMEM((n, r, d), BF),
            pltpu.VMEM((n + 1, r, d), BF),
            pltpu.VMEM((1, 8, r), F32),
            pltpu.VMEM((1, 8, r), F32),
            pltpu.VMEM((d, keys), BF),
            pltpu.VMEM((g.shape[2], keys), BF),
            pltpu.VMEM(wa.shape, BF),
            dma(1),
            dma(n),
            dma(n),
            dma(n),
            dma(n + 1),
            dma(1),
            dma(1),
            *(
                [
                    *batch_scratch(d, half),
                    *batch_scratch(d, half),
                    *batch_scratch(g.shape[2], d),
                    *norm_scratch(4, n),
                ]
                if fused
                else [pltpu.VMEM((2, d, half), BF)] * 2
            ),
        ],
        10**10,
        dqkv,
        x,
        dmid,
        stat,
        wa,
        a1,
        g,
        cb,
        square,
        far=(4,),
    )


def adamw(gradient, moment, square, weight, clip_factor):
    clipped = gradient * clip_factor
    moment_new = BETA_ONE * moment + (1.0 - BETA_ONE) * clipped
    square_new = BETA_TWO * square + (1.0 - BETA_TWO) * clipped * clipped
    corrected = (
        moment_new
        / (1.0 - BETA_ONE**STEP)
        / (jnp.sqrt(square_new / (1.0 - BETA_TWO**STEP)) + 1e-08)
    )
    return (moment_new, square_new, -RATE * (corrected + DECAY * weight))


def update_kernel(lay, norm_ref, res_ref, dx_ref, *refs):
    grads, moments_in, squares_in, weights = refs[0:4], refs[4:8], refs[8:12], refs[12:16]
    m_out, v_out, s_out, g_out = refs[16:20], refs[20:24], refs[24:28], refs[28:32]
    image_ref, image_grad_ref, text_grad_ref, one_ref = refs[32:36]
    g_s, m_s, v_s, w_s, t_s = (refs[36 + 4 * i : 40 + 4 * i] for i in range(5))
    load, store = refs[56:]
    b = lax.axis_index("batch")
    loads = []
    for i in range(4):
        rows = grads[i].shape[1]
        part = pl.ds(pl.multiple_of(b * rows, 16), rows)
        for m in range(2):
            for q, (src, dst) in enumerate(
                (
                    (grads[i].at[m], g_s[i]),
                    (moments_in[i].at[m], m_s[i]),
                    (squares_in[i].at[m], v_s[i]),
                    (weights[i].at[m, part, :], w_s[i]),
                )
            ):
                loads.append(pltpu.make_async_copy(src, dst.at[m], load.at[i, m, q]))
                loads[-1].start()
    clip = jnp.minimum(1.0, 1.0 / (norm_ref[0:1, 0:1] + 1e-06))
    image_ref[...] = res_ref[: lay.img]
    image_grad_ref[...] = dx_ref[: lay.img]
    text_grad_ref[...] = dx_ref[lay.img : lay.real]
    one_ref[...] = norm_ref[0:1, 0:1]
    stores = []
    for i in range(4):
        for m in range(2):
            for q in range(4):
                loads[8 * i + 4 * m + q].wait()
            stores.append(pltpu.make_async_copy(g_s[i].at[m], g_out[i].at[m], store.at[i, m, 3]))
            stores[-1].start()

            @pl.loop(0, grads[i].shape[1] // TILE)
            def _(r):
                part = pl.ds(pl.multiple_of(r * TILE, TILE), TILE)
                new_m, new_v, step = adamw(
                    g_s[i][m, part, :],
                    m_s[i][m, part, :],
                    v_s[i][m, part, :],
                    w_s[i][m, part, :].astype(F32),
                    clip,
                )
                m_s[i][m, part, :] = new_m
                v_s[i][m, part, :] = new_v
                t_s[i][m, part, :] = step

            for q, (src, dst) in enumerate(
                ((m_s[i], m_out[i]), (v_s[i], v_out[i]), (t_s[i], s_out[i]))
            ):
                stores.append(pltpu.make_async_copy(src.at[m], dst.at[m], store.at[i, m, q]))
                stores[-1].start()
    for each in stores:
        each.wait()


TILE = 16


def update(lay, norm, res, dx, grads, ms, vs, ws):
    d = dx.shape[1]
    shapes = [g.shape for g in grads]
    outs = pl.pallas_call(
        partial(update_kernel, lay),
        out_shape=[jax.ShapeDtypeStruct(s, F32) for _ in range(4) for s in shapes]
        + [
            jax.ShapeDtypeStruct((lay.img, d), BF),
            jax.ShapeDtypeStruct((lay.img, d), F32),
            jax.ShapeDtypeStruct((lay.txt, d), F32),
            jax.ShapeDtypeStruct((1, 1), F32),
        ],
        in_specs=[VMEM] * 3 + [ANY] * 16,
        out_specs=[ANY] * 16 + [VMEM] * 4,
        scratch_shapes=[
            *[pltpu.VMEM(s, t) for t in (F32, F32, F32, BF, F32) for s in shapes],
            dma(4, 2, 4),
            dma(4, 2, 4),
        ],
        compiler_params=pltpu.CompilerParams(vmem_limit_bytes=60 * 2**20),
        cost_estimate=pl.CostEstimate(flops=10**8, bytes_accessed=5 * 10**7, transcendentals=0),
    )(norm, res, dx, *grads, *ms, *vs, *ws)
    return outs[0:4], outs[4:8], outs[8:12], outs[12:16], outs[16:]


def weight_shard(weight, group_index, shard_rows):
    return lax.dynamic_slice_in_dim(weight, group_index * shard_rows, shard_rows, 1).astype(F32)


class Layout:
    def __init__(self, n_row, img, txt):
        self.n_row = n_row
        self.img = img
        self.txt = txt
        self.txt_pad = -(-txt // 16) * 16
        self.rows = img + self.txt_pad
        self.real = img + txt

    def pack(self, image, text):
        return jnp.concatenate(
            [image, text, jnp.zeros((self.txt_pad - self.txt, image.shape[1]), image.dtype)], 0
        )


def on_device(n_batch, n_row, *args):
    (
        image_input,
        text_input,
        image_cotan,
        text_cotan,
        seq_group,
        w_attend,
        w_output,
        w_expand,
        w_reduce,
        m_attend,
        m_output,
        m_expand,
        m_reduce,
        v_attend,
        v_output,
        v_expand,
        v_reduce,
    ) = args
    img, txt = image_input.shape[1], text_input.shape[1]
    lay = Layout(n_row, img, txt)
    group_index = lax.axis_index("batch")
    present = jnp.any(seq_group == group_index).astype(F32)

    low_x = lay.pack(image_input[0], text_input[0])
    low_cot = (lay.pack(image_cotan[0], text_cotan[0]).astype(F32) * present).astype(BF)
    fused = n_batch == 4

    a1_all, qkv, stat_one = attend(lay, low_x, w_attend)
    o_all, lse, cb_all, middle_x, a2_all, act, dh_all, grad_mid, low_mid = forward(
        lay, qkv, low_x, low_cot, w_output, w_reduce, w_expand
    )
    dqkv, g_all, result, g_exp, g_out, square = pull(
        lay, fused, low_mid, qkv, lse, w_output, act, w_reduce, middle_x, a2_all, dh_all, o_all
    )
    grad_in, g_att, g_red, norm = inputs_back(
        lay, fused, dqkv, low_x, grad_mid, stat_one, w_attend, a1_all, g_all, cb_all, square
    )
    sums = [g_att, g_out, g_exp, g_red]
    if not fused:
        sums = [
            lax.psum_scatter(g, "batch", scatter_dimension=1, tiled=True).astype(F32) for g in sums
        ]
    ms = (m_attend, m_output, m_expand, m_reduce)
    vs = (v_attend, v_output, v_expand, v_reduce)
    ws = (w_attend, w_output, w_expand, w_reduce)
    if fused:
        new_m, new_v, steps, sums, (image, image_grad, text_grad, one) = update(
            lay, norm, result, grad_in, sums, ms, vs, ws
        )
        grad_norm = one.reshape(())
    else:
        image, image_grad, text_grad = result[:img], grad_in[:img], grad_in[img : lay.real]
        squares = sum(jnp.sum(g * g) for g in sums)
        grad_norm = jnp.sqrt(lax.psum(lax.psum(lax.psum(squares, "batch"), "row"), "col"))
        clip_factor = jnp.minimum(1.0, 1.0 / (grad_norm + 1e-06))
        new_m, new_v, steps = zip(
            *[
                adamw(g, m, v, weight_shard(w, group_index, g.shape[1]), clip_factor)
                for g, m, v, w in zip(sums, ms, vs, ws)
            ]
        )
    return (
        image[None],
        result[img : lay.real][None],
        image_grad[None],
        text_grad[None],
        *sums,
        *new_m,
        *new_v,
        *steps,
        grad_norm,
    )


def solution(mesh):
    tokens = P("batch", "row", "col")
    wide = P(None, "col", "row")
    tall = P(None, "row", "col")
    wide_shard = P(None, ("col", "batch"), "row")
    tall_shard = P(None, ("row", "batch"), "col")
    shards = (wide_shard, tall_shard, wide_shard, tall_shard)
    return jax.shard_map(
        partial(on_device, mesh.shape["batch"], mesh.shape["row"]),
        mesh=mesh,
        in_specs=(*[tokens] * 4, P(), wide, tall, wide, tall, *shards, *shards),
        out_specs=(*[tokens] * 4, *shards * 4, P()),
        check_vma=False,
    )
```

```python
import math
from functools import partial

import jax
import jax.numpy as jnp
from jax import lax
from jax.experimental import pallas as pl
from jax.experimental.pallas import tpu as pltpu
from jax.sharding import PartitionSpec as P

D = 1536
HD = 64
STEP = 10
STRIPE = 512

EPSILON = 1e-06
BETA_ONE = 0.9
BETA_TWO = 0.999
RATE = 0.02
DECAY = 0.1

BF = jnp.bfloat16
F32 = jnp.float32


def dot(a, b):
    return lax.dot_general(a, b, (((a.ndim - 1,), (0,)), ((), ())), preferred_element_type=F32)


def dot_nt(a, b):
    return lax.dot_general(a, b, (((a.ndim - 1,), (1,)), ((), ())), preferred_element_type=F32)


def dot_tn(a, b):
    return lax.dot_general(a, b, (((0,), (0,)), ((), ())), preferred_element_type=F32)


MESH = pl.DeviceIdType.MESH
VMEM = pl.BlockSpec(memory_space=pltpu.VMEM)
ANY = pl.BlockSpec(memory_space=pl.ANY)


def remote(src, dst, send, recv, **where):
    return pltpu.make_async_remote_copy(
        src_ref=src,
        dst_ref=dst,
        send_sem=send,
        recv_sem=recv,
        device_id=where,
        device_id_type=MESH,
    )


def near_first(z, n, j):
    alternate = jnp.where(j % 2 == 1, z - (j + 1) // 2, z + j // 2)
    reach = jnp.minimum(z, n - 1 - z)
    beyond = jnp.where(z <= n - 1 - z, j, n - 1 - j)
    return jnp.where(j <= 2 * reach, alternate, beyond)


LOADS = []
STORES = []


def greet(n, fused=False, more=()):
    z, c = lax.axis_index("row"), lax.axis_index("col")
    barrier = pltpu.get_barrier_semaphore()
    pl.semaphore_signal(barrier, inc=1, device_id={"col": 1 - c}, device_id_type=MESH)

    @pl.when(z > 0)
    def _():
        pl.semaphore_signal(barrier, inc=1, device_id={"row": z - 1}, device_id_type=MESH)

    @pl.when(z < n - 1)
    def _():
        pl.semaphore_signal(barrier, inc=1, device_id={"row": z + 1}, device_id_type=MESH)

    if fused:
        b = lax.axis_index("batch")
        for other in (b + 1 - 2 * (b % 2), (b + 2) % 4):
            pl.semaphore_signal(barrier, inc=1, device_id={"batch": other}, device_id_type=MESH)
    ends = jnp.where(z > 0, 1, 0) + jnp.where(z < n - 1, 1, 0)
    for where in more:
        pl.semaphore_signal(barrier, inc=1, device_id=where, device_id_type=MESH)
    pl.semaphore_wait(barrier, ends + (3 if fused else 1) + len(more))
    for each in LOADS:
        each.wait()


class Gather:
    def __init__(self, full, send, recv, n):
        self.full, self.send, self.recv, self.n = full, send, recv, n
        self.z = lax.axis_index("row")

    def copy(self, k, step):
        there = (self.z + step + self.n) % self.n
        way = 0 if step > 0 else 1
        return remote(
            self.full.at[k], self.full.at[k], self.send.at[way, k], self.recv.at[k], row=there
        )

    def push(self, k):
        @pl.when((k <= self.z) & (self.z < self.n - 1))
        def _():
            self.copy(k, 1).start()

        @pl.when((k >= self.z) & (self.z > 0))
        def _():
            self.copy(k, -1).start()

    def arrive(self, k):
        @pl.when(k != self.z)
        def _():
            self.copy(k, 1).wait_recv()

        self.push(k)

    def arrive_after_own(self, k):
        @pl.when(k != self.z)
        def _():
            self.arrive(k)

    def finish(self):
        @pl.loop(0, self.n)
        def _(k):
            @pl.when((k <= self.z) & (self.z < self.n - 1))
            def _():
                self.copy(k, 1).wait_send()

            @pl.when((k >= self.z) & (self.z > 0))
            def _():
                self.copy(k, -1).wait_send()


class Reduce:
    def __init__(self, acc, out, inbox, send, recv, n):
        self.acc, self.out, self.inbox, self.send, self.recv, self.n = acc, out, inbox, send, recv, n
        self.z = lax.axis_index("row")

    def copy(self, o):
        slot = jnp.where(o > self.z, o + 1, o)
        there = (self.z + jnp.where(o > self.z, 1, -1) + self.n) % self.n
        return remote(
            self.out.at[o], self.inbox.at[slot], self.send.at[o], self.recv.at[slot], row=there
        )

    def take(self, slot):
        remote(
            self.out.at[0],
            self.inbox.at[slot],
            self.send.at[0],
            self.recv.at[slot],
            row=(self.z + 1) % self.n,
        ).wait_recv()
        self.acc[...] += self.inbox[slot].astype(F32)

    def add(self, o):
        @pl.when((o >= self.z) & (self.z > 0))
        def _():
            self.take(o + 1)

        @pl.when((o <= self.z) & (self.z < self.n - 1))
        def _():
            self.take(o)

        @pl.when(o != self.z)
        def _():
            self.out[o] = self.acc[...].astype(BF)
            self.copy(o).start()

    def finish(self):
        @pl.loop(0, self.n)
        def _(o):
            @pl.when(o != self.z)
            def _():
                self.copy(o).wait_send()


class Swap:
    def __init__(self, out, into, send, recv):
        self.out, self.into, self.send, self.recv = out, into, send, recv

    def copy(self, k):
        return remote(
            self.out.at[k],
            self.into.at[k],
            self.send.at[k],
            self.recv.at[k],
            col=1 - lax.axis_index("col"),
        )

    def start(self, k):
        self.copy(k).start()

    def arrive(self, k):
        self.copy(k).wait_recv()

    def finish(self, n):
        @pl.loop(0, n)
        def _(k):
            self.copy(k).wait_send()


def sums_of(a, b):
    lane = lax.broadcasted_iota(jnp.int32, (a.shape[0], 128), 1)
    one, two = jnp.sum(a, axis=1, keepdims=True), jnp.sum(b, axis=1, keepdims=True)
    return jnp.where(lane == 0, one, jnp.where(lane == 1, two, 0.0)).T[:8]


def columns(stat):
    rows = stat[0]
    turned = jnp.concatenate([rows, jnp.zeros((120, rows.shape[1]), F32)], 0).T
    return turned[:, 0:1] / D, turned[:, 1:2] / D


def moments(stat):
    mean, square = columns(stat)
    return mean, lax.rsqrt(square - mean * mean + EPSILON)


def exchange(stat, stat_in, send, recv):
    swap = Swap(stat, stat_in, send, recv)
    swap.start(0)
    swap.arrive(0)
    swap.finish(1)
    stat[0] += stat_in[0]


def dma(*shape):
    return pltpu.SemaphoreType.DMA(shape)


def call(kernel, ident, outs, scratch, cost, *operands, far=(), early=0):
    large = [i for i, o in enumerate(operands) if i not in far and o.size > 2**15]
    count = len(operands)

    def body(*refs):
        refs = list(refs)
        extra = len(large) + early
        buffers, (load, store) = refs[-extra - 2 : -2], refs[-2:]
        LOADS.clear()
        STORES.clear()
        for q, i in enumerate(large):
            LOADS.append(pltpu.make_async_copy(refs[i], buffers[q], load.at[q]))
            LOADS[-1].start()
            refs[i] = buffers[q]
        for q in range(early):
            held = buffers[len(large) + q]
            STORES.append(pltpu.make_async_copy(held, refs[count + q], store.at[q]))
            refs[count + q] = held
        kernel(*refs[: -extra - 2])
        for each in STORES:
            each.wait()

    return pl.pallas_call(
        body,
        out_shape=[jax.ShapeDtypeStruct(s, t) for s, t in outs],
        in_specs=[ANY if i in far or i in large else VMEM for i in range(count)],
        out_specs=[ANY if i < early else VMEM for i in range(len(outs))],
        scratch_shapes=[
            *scratch,
            *[pltpu.VMEM(operands[i].shape, operands[i].dtype) for i in large],
            *[pltpu.VMEM(*outs[i]) for i in range(early)],
            dma(len(large)),
            dma(max(early, 1)),
        ],
        compiler_params=pltpu.CompilerParams(
            collective_id=ident, has_side_effects=True, vmem_limit_bytes=60 * 2**20
        ),
        cost_estimate=pl.CostEstimate(flops=cost, bytes_accessed=10**7, transcendentals=0),
    )(*operands)


def parts_of(lay):
    return ((0, slice(0, lay.img)), (1, slice(lay.img, lay.rows)))


def attend_kernel(lay, x_ref, w_ref, full_ref, qkv_ref, stat_ref, *scratch):
    own, out, into, stat_in, g_send, g_recv, s_send, s_recv, t_send, t_recv = scratch
    n = lay.n_row
    z, c = lax.axis_index("row"), lax.axis_index("col")
    half = qkv_ref.shape[2]
    greet(n)
    x = x_ref[...].astype(F32)
    stat_ref[0] = sums_of(x, x * x)
    exchange(stat_ref, stat_in, t_send, t_recv)
    mean, inverse = moments(stat_ref)
    full_ref[z] = ((x - mean) * inverse).astype(BF)
    gather = Gather(full_ref, g_send, g_recv, n)
    swap = Swap(out, into, s_send, s_recv)

    @pl.loop(0, n)
    def _(j):
        k = near_first(z, n, j)
        gather.arrive(k)
        for part, rows in parts_of(lay):
            p = dot(full_ref[k, rows], w_ref[part])
            low, high = p[:, :half], p[:, half:]
            own[k, rows] = jnp.where(c == 0, low, high)
            out[k, rows] = jnp.where(c == 0, high, low).astype(BF)
        swap.start(k)

    @pl.loop(0, n)
    def _(j):
        k = near_first(z, n, j)
        swap.arrive(k)
        qkv_ref[k] = (own[k] + into[k].astype(F32)).astype(BF)

    gather.finish()
    swap.finish(n)


def attend(lay, x, w):
    n, r, half, d = lay.n_row, lay.rows, w.shape[2] // 2, x.shape[1]
    return call(
        partial(attend_kernel, lay),
        1,
        [((n, r, d), BF), ((n, r, half), BF), ((1, 8, r), F32)],
        [
            pltpu.VMEM((n, r, half), F32),
            pltpu.VMEM((n, r, half), BF),
            pltpu.VMEM((n, r, half), BF),
            pltpu.VMEM((1, 8, r), F32),
            dma(2, n),
            dma(n),
            dma(n),
            dma(n),
            dma(1),
            dma(1),
        ],
        2 * n * r * w.shape[1] * w.shape[2],
        x,
        w,
    )


def split_heads(lay, qkv_ref, q_ref, k_ref, v_ref, fill):
    n, img, txt = lay.n_row, lay.img, lay.txt_pad
    heads = qkv_ref.shape[2] // (3 * HD)

    @pl.loop(0, n)
    def _(k):
        first = pl.ds(pl.multiple_of(k * img, 16), img)
        second = pl.ds(pl.multiple_of(n * img + k * txt, 16), txt)
        for h in range(heads):
            at = h * 3 * HD
            rows = qkv_ref[k, :, at : at + 3 * HD]
            q_ref[h, k] = rows[:, :HD] * jnp.asarray(HD**-0.5, BF)
            for ref, lo in ((k_ref, HD), (v_ref, 2 * HD)):
                value = rows[:, lo : lo + HD]
                if ref is v_ref and fill:
                    value = jnp.concatenate([value, jnp.ones_like(value)], 1)
                ref[h, first] = value[:img]
                ref[h, second] = value[img:]


def text_bias(lay):
    lane = lax.broadcasted_iota(jnp.int32, (1, lay.n_row * lay.txt_pad), 1)
    return jnp.where(lane % lay.txt_pad < lay.txt, 0.0, -1e30)


def middle_kernel(
    lay, loads, qkv_ref, x_ref, cot_ref, wo_ref, wr_ref, o_ref, lse_ref, cb_ref, dg_ref, mid_ref, low_ref, stat_ref, *scratch
):
    (
        q_s, k_s, v_s, o_out, o_in, dg_out, dg_in, acc, r_out, inbox, stat_in,
        g_send, g_recv, o_send, o_recv, d_send, d_recv, r_send, r_recv, t_send, t_recv,
    ) = scratch
    n, far = lay.n_row, lay.n_row * lay.img
    z, c = lax.axis_index("row"), lax.axis_index("col")
    heads, hid = q_s.shape[0], dg_ref.shape[2]
    greet(n)
    gather = Gather(cb_ref, g_send, g_recv, n)
    cb_ref[z] = cot_ref[...]
    gather.push(z)
    swap_o = Swap(o_out, o_in, o_send, o_recv)
    swap_d = Swap(dg_out, dg_in, d_send, d_recv)
    reduce = Reduce(acc, r_out, inbox, r_send, r_recv, n)
    split_heads(lay, qkv_ref, q_s, k_s, v_s, True)
    bias = text_bias(lay)
    lane = lax.broadcasted_iota(jnp.int32, (lay.rows, 128), 1)

    def attention(k):
        outs, lse = [], jnp.zeros((lay.rows, 128), F32)
        for h in range(heads):
            q = q_s[h, k]
            s1 = dot_nt(q, k_s[h, :far])
            s2 = dot_nt(q, k_s[h, far:]) + bias
            peak = jnp.maximum(
                jnp.max(s1, axis=1, keepdims=True), jnp.max(s2, axis=1, keepdims=True)
            )
            e1, e2 = jnp.exp(s1 - peak).astype(BF), jnp.exp(s2 - peak).astype(BF)
            o = dot(e1, v_s[h, :far]) + dot(e2, v_s[h, far:])
            total = o[:, HD : HD + 1]
            outs.append((o[:, :HD] / total).astype(BF))
            lse = jnp.where(lane == h, peak + jnp.log(total), lse)
        lse_ref[k] = lse
        o_out[k] = jnp.concatenate(outs, 1)

    def project(k):
        swap_o.arrive(k)
        own, other = o_out[k], o_in[k]
        o_ref[k] = jnp.concatenate(
            [jnp.where(c == 0, own, other), jnp.where(c == 0, other, own)], 1
        )
        for part, rows in parts_of(lay):
            acc[rows] = dot(o_ref[k, rows], wo_ref[part])
        reduce.add(k)

    def step(j):
        k = near_first(z, n, n - 1 - j)
        attention(k)
        swap_o.start(k)

        @pl.when(j == 0)
        def _():
            loads[0].wait()
            loads[1].wait()

        near = near_first(z, n, j)
        gather.arrive_after_own(near)
        for part, rows in parts_of(lay):
            dg_out[near, rows] = dot_nt(
                cb_ref[near, rows], wr_ref[part, pl.ds(pl.multiple_of((1 - c) * hid, 128), hid), :]
            ).astype(BF)
        swap_d.start(near)
        for part, rows in parts_of(lay):
            dg_ref[near, rows] = dot_nt(
                cb_ref[near, rows], wr_ref[part, pl.ds(pl.multiple_of(c * hid, 128), hid), :]
            )

    lag = 1 + jnp.minimum(z, n - 1 - z)

    @pl.loop(0, n + 1 + (n - 1) // 2)
    def _(j):
        @pl.when(j < n)
        def _():
            step(j)

        i = j - lag

        @pl.when((i >= 0) & (i < n))
        def _():
            project(near_first(z, n, n - 1 - i))

    mid = x_ref[...].astype(F32) + acc[...]
    mid_ref[...] = mid
    stat_ref[0] = sums_of(mid, mid * mid)
    exchange(stat_ref, stat_in, t_send, t_recv)
    mean, inverse = moments(stat_ref)
    low_ref[...] = ((mid - mean) * inverse).astype(BF)

    def settle():
        @pl.loop(0, n)
        def _(j):
            k = near_first(z, n, j)
            swap_d.arrive(k)
            dg_ref[k] += dg_in[k].astype(F32)

        gather.finish()
        swap_o.finish(n)
        swap_d.finish(n)
        reduce.finish()

    return settle


SLOPE = (2.0 / math.pi) ** 0.5
CUBIC = 0.044715


def gelu_pair(u):
    square = u * u
    t = jnp.tanh(SLOPE * u * (1.0 + CUBIC * square))
    half = 0.5 * (1.0 + t)
    slope = half + 0.5 * u * (1.0 - t * t) * (SLOPE * (1.0 + 3.0 * CUBIC * square))
    return u * half, slope


def hidden_kernel(
    lay, settle, low_ref, dg_ref, mid_ref, cot_ref, stat_ref, we_ref, full_ref, act_ref, dh_ref, dmid_ref, dy_ref, *scratch
):
    (
        own, out, into, acc, r_out, inbox, stat_out, stat_in,
        g_send, g_recv, s_send, s_recv, d_send, d_recv, r_send, r_recv, t_send, t_recv,
    ) = scratch
    n = lay.n_row
    z, c = lax.axis_index("row"), lax.axis_index("col")
    hid = dg_ref.shape[2]
    mine = pl.ds(pl.multiple_of(c * hid, 128), hid)
    theirs = pl.ds(pl.multiple_of((1 - c) * hid, 128), hid)
    gather = Gather(full_ref, g_send, g_recv, n)
    full_ref[z] = low_ref[...]
    gather.push(z)
    swap = Swap(out, into, s_send, s_recv)
    reduce = Reduce(acc, r_out, inbox, r_send, r_recv, n)

    def dh_copy(k):
        half = dh_ref.at[k, :, mine]
        return remote(half, half, d_send.at[k], d_recv.at[k], col=1 - c)

    @pl.loop(0, n)
    def _(j):
        k = near_first(z, n, j)
        gather.arrive_after_own(k)
        for part, rows in parts_of(lay):
            out[k, rows] = dot(full_ref[k, rows], we_ref[part, :, theirs]).astype(BF)
        swap.start(k)
        for part, rows in parts_of(lay):
            own[k, rows] = dot(full_ref[k, rows], we_ref[part, :, mine])

    def back(k):
        half = dh_ref.at[k, :, theirs]
        remote(half, half, d_send.at[k], d_recv.at[k], col=1 - c).wait_recv()
        for part, rows in parts_of(lay):
            acc[rows] = dot_nt(dh_ref[k, rows], we_ref[part])
        reduce.add(k)

    settle()
    for each in STORES[:5]:
        each.start()

    @pl.loop(0, n + 2)
    def _(j):
        @pl.when(j < n)
        def _():
            k = near_first(z, n, n - 1 - j)
            swap.arrive(k)
            act, slope = gelu_pair(own[k] + into[k].astype(F32))
            act_ref[k] = act.astype(BF)
            dh_ref[k, :, mine] = (dg_ref[k] * slope).astype(BF)
            dh_copy(k).start()

        @pl.when(j > 1)
        def _():
            back(near_first(z, n, n + 1 - j))

    for each in STORES[5:]:
        each.start()
    mean, inverse = moments(stat_ref)
    normed = (mid_ref[...] - mean) * inverse
    grad = acc[...]
    stat_out[0] = sums_of(grad, grad * normed)
    exchange(stat_out, stat_in, t_send, t_recv)
    back_one, back_two = columns(stat_out)
    dmid = cot_ref[...].astype(F32) + inverse * (grad - back_one - normed * back_two)
    dmid_ref[...] = dmid
    dy_ref[...] = dmid.astype(BF)
    gather.finish()
    swap.finish(n)
    reduce.finish()

    @pl.loop(0, n)
    def _(k):
        dh_copy(k).wait_send()


def forward_kernel(
    lay, qkv_ref, x_ref, cot_ref, wo_ref, wr_any, we_any,
    o_ref, lse_ref, cb_ref, mid_ref, a2_ref, act_ref, dh_ref, dmid_ref, dy_ref, *scratch
):
    dg_ref, low_ref, stat_ref, wr_ref, we_ref, w_load = scratch[:6]
    loads = [
        pltpu.make_async_copy(wr_any, wr_ref, w_load.at[0]),
        pltpu.make_async_copy(we_any, we_ref, w_load.at[1]),
    ]
    for each in loads:
        each.start()
    settle = middle_kernel(
        lay, loads, qkv_ref, x_ref, cot_ref, wo_ref, wr_ref, o_ref, lse_ref, cb_ref, dg_ref, mid_ref, low_ref, stat_ref, *scratch[6:27]
    )
    hidden_kernel(
        lay, settle, low_ref, dg_ref, mid_ref, cot_ref, stat_ref, we_ref, a2_ref, act_ref, dh_ref, dmid_ref, dy_ref, *scratch[27:]
    )


def forward(lay, qkv, x, cot, wo, wr, we):
    n, r, d = lay.n_row, lay.rows, x.shape[1]
    heads, hid = qkv.shape[2] // (3 * HD), wr.shape[1] // 2
    keys = n * r
    return call(
        partial(forward_kernel, lay),
        2,
        [
            ((n, r, 2 * heads * HD), BF),
            ((n, r, 128), F32),
            ((n, r, d), BF),
            ((r, d), F32),
            ((n, r, d), BF),
            ((n, r, hid), BF),
            ((n, r, 2 * hid), BF),
            ((r, d), F32),
            ((r, d), BF),
        ],
        [
            pltpu.VMEM((n, r, hid), F32),
            pltpu.VMEM((r, d), BF),
            pltpu.VMEM((1, 8, r), F32),
            pltpu.VMEM(wr.shape, BF),
            pltpu.VMEM(we.shape, BF),
            dma(2),
            pltpu.VMEM((heads, n, r, HD), BF),
            pltpu.VMEM((heads, keys, HD), BF),
            pltpu.VMEM((heads, keys, 2 * HD), BF),
            pltpu.VMEM((n, r, heads * HD), BF),
            pltpu.VMEM((n, r, heads * HD), BF),
            pltpu.VMEM((n, r, hid), BF),
            pltpu.VMEM((n, r, hid), BF),
            pltpu.VMEM((r, d), F32),
            pltpu.VMEM((n, r, d), BF),
            pltpu.VMEM((n + 1, r, d), BF),
            pltpu.VMEM((1, 8, r), F32),
            dma(2, n),
            dma(n),
            dma(n),
            dma(n),
            dma(n),
            dma(n),
            dma(n),
            dma(n + 1),
            dma(1),
            dma(1),
            pltpu.VMEM((n, r, hid), F32),
            pltpu.VMEM((n, r, hid), BF),
            pltpu.VMEM((n, r, hid), BF),
            pltpu.VMEM((r, d), F32),
            pltpu.VMEM((n, r, d), BF),
            pltpu.VMEM((n + 1, r, d), BF),
            pltpu.VMEM((1, 8, r), F32),
            pltpu.VMEM((1, 8, r), F32),
            dma(2, n),
            dma(n),
            dma(n),
            dma(n),
            dma(n),
            dma(n),
            dma(n),
            dma(n + 1),
            dma(1),
            dma(1),
        ],
        10**10,
        qkv,
        x,
        cot,
        wo,
        wr,
        we,
        far=(4, 5),
        early=7,
    )


class BatchSum:
    def __init__(self, local, first, out, second, sems):
        self.local, self.first, self.out, self.second = local, first, out, second
        self.f_send, self.f_recv, self.s_send, self.s_recv = sems
        b = lax.axis_index("batch")
        self.x, self.core = b // 2, b % 2
        self.to_core, self.to_x = 2 * self.x + 1 - self.core, 2 * (1 - self.x) + self.core
        self.s = out.shape[1]

    def rows(self, block):
        return pl.ds(pl.multiple_of(block * self.s, 16), self.s)

    def core_copy(self, q):
        block = 2 * q + 1 - self.core
        return remote(
            self.local.at[:, self.rows(block), :],
            self.first.at[q],
            self.f_send.at[q],
            self.f_recv.at[q],
            batch=self.to_core,
        )

    def x_copy(self):
        return remote(self.out, self.second, self.s_send.at[0], self.s_recv.at[0], batch=self.to_x)

    def start(self):
        self.core_copy(1 - self.x).start()
        self.core_copy(self.x).start()

    def block(self, q):
        self.core_copy(q).wait_recv()
        mine = self.local[:, self.rows(2 * q + self.core), :].astype(F32)
        return mine + self.first[q].astype(F32)

    def pass_on(self):
        self.out[...] = self.block(1 - self.x).astype(BF)
        self.x_copy().start()

    def total(self):
        near = self.block(self.x)
        self.x_copy().wait_recv()
        return near + self.second[...].astype(F32)

    def finish(self):
        self.core_copy(0).wait_send()
        self.core_copy(1).wait_send()
        self.x_copy().wait_send()


def batch_scratch(rows, cols):
    s = rows // 4
    return [
        pltpu.VMEM((2, rows, cols), BF),
        pltpu.VMEM((2, 2, s, cols), BF),
        pltpu.VMEM((2, s, cols), BF),
        pltpu.VMEM((2, s, cols), BF),
        dma(2),
        dma(2),
        dma(1),
        dma(1),
    ]


def batch_of(scratch):
    return BatchSum(*scratch[:4], scratch[4:])


def squares_of(ref):
    total = jnp.zeros((1, 1), F32)
    for m in range(2):
        lanes = jnp.sum(ref[m] * ref[m], axis=0, keepdims=True)
        total += jnp.sum(lanes, axis=1, keepdims=True)
    return jnp.broadcast_to(total, (8, 128))


class Norm:
    def __init__(self, n_batch, n_row, plane, line, p_send, p_recv, b_send, b_recv):
        self.n_batch, self.plane, self.line = n_batch, plane, line
        self.p_send, self.p_recv, self.b_send, self.b_recv = p_send, p_recv, b_send, b_recv
        self.b, z, c = lax.axis_index("batch"), lax.axis_index("row"), lax.axis_index("col")
        self.me = z * 2 + c
        self.peers = [((z + i) % n_row, (c + j) % 2) for i in range(n_row) for j in range(2)][1:]

    def where(self):
        return [{"row": row, "col": col} for row, col in self.peers] + [
            {"batch": (self.b + i) % self.n_batch} for i in range(1, self.n_batch)
        ]

    def to_plane(self, i, slot):
        row, col = self.peers[i]
        block = self.plane.at[slot]
        return remote(block, block, self.p_send.at[i], self.p_recv.at[slot], row=row, col=col)

    def to_line(self, i, slot):
        block = self.line.at[slot]
        other = (self.b + i) % self.n_batch
        return remote(block, block, self.b_send.at[i], self.b_recv.at[slot], batch=other)

    def total(self, tile):
        b, n_batch = self.b, self.n_batch
        self.plane[self.me] = tile
        for i in range(len(self.peers)):
            self.to_plane(i, self.me).start()
        for i, (row, col) in enumerate(self.peers):
            self.to_plane(i, row * 2 + col).wait_recv()
        self.line[b] = jnp.sum(self.plane[...], axis=0)
        for i in range(1, n_batch):
            self.to_line(i, b).start()
        for i in range(1, n_batch):
            self.to_line(i, (b + i) % n_batch).wait_recv()
        for i in range(len(self.peers)):
            self.to_plane(i, self.me).wait_send()
        for i in range(1, n_batch):
            self.to_line(i, b).wait_send()
        return jnp.sum(self.line[...], axis=0)


def norm_scratch(n_batch, n_row):
    return [
        pltpu.VMEM((2 * n_row, 8, 128), F32),
        pltpu.VMEM((n_batch, 8, 128), F32),
        dma(2 * n_row - 1),
        dma(2 * n_row),
        dma(n_batch),
        dma(n_batch),
    ]


def transpose_rows(lay, left, turned):
    n, img, far = lay.n_row, lay.img, lay.n_row * lay.img
    for k in range(n):
        turned[:, k * img : (k + 1) * img] = left[k, :img, :].T
    turned[:, far:] = jnp.concatenate([left[k, img:, :] for k in range(n)], 0).T


def weight_gradient(lay, turned, right, local, part, cols):
    n, img, far = lay.n_row, lay.img, lay.n_row * lay.img
    if part == 0:
        total = dot(turned[:, :img], right[0, :img, cols])
        for k in range(1, n):
            total += dot(turned[:, k * img : (k + 1) * img], right[k, :img, cols])
    else:
        text = jnp.concatenate([right[k, img:, cols] for k in range(n)], 0)
        total = dot(turned[:, far:], text)
    local[part, :, cols] = total.astype(BF)


def pull_kernel(
    lay, fused, low_ref, qkv_ref, lse_ref, wo_ref, act_ref, wr_any, mid_ref, a2_ref, dh_ref, o_ref,
    dqkv_ref, g_ref, res_ref, exp_ref, out_ref, square_ref, *scratch
):
    (
        q_s, k_s, v_s, do_own, do_out, do_in, do_s, dq_s, dk_s, dv_s, acc, r_out, inbox, turned, wr_ref, full_ref, a_load, w_load,
        g_send, g_recv, s_send, s_recv, a_send, a_recv, r_send, r_recv,
    ) = scratch[:26]
    n, img, txt, far = lay.n_row, lay.img, lay.txt_pad, lay.n_row * lay.img
    z, c = lax.axis_index("row"), lax.axis_index("col")
    heads, half, hid = q_s.shape[0], do_own.shape[2], act_ref.shape[2]
    mine = pl.ds(pl.multiple_of(c * half, 16), half)
    theirs = pl.ds(pl.multiple_of((1 - c) * half, 16), half)
    my_act = pl.ds(pl.multiple_of(c * hid, 128), hid)
    their_act = pl.ds(pl.multiple_of((1 - c) * hid, 128), hid)
    greet(n, fused)
    gather = Gather(full_ref, g_send, g_recv, n)
    full_ref[z] = low_ref[...]
    gather.push(z)
    swap = Swap(do_out, do_in, s_send, s_recv)
    reduce = Reduce(acc, r_out, inbox, r_send, r_recv, n)
    local, local_out = exp_ref, out_ref
    if fused:
        batch, batch_out = batch_of(scratch[26:34]), batch_of(scratch[34:42])
        local, local_out = batch.local, batch_out.local
    split_heads(lay, qkv_ref, q_s, k_s, v_s, False)
    bias = text_bias(lay)
    dk_s[...] = jnp.zeros_like(dk_s)
    dv_s[...] = jnp.zeros_like(dv_s)
    lag = jnp.minimum(z, n - 1 - z)

    def act_copy(k, where):
        block = g_ref.at[k, :, where]
        return remote(block, block, a_send.at[k], a_recv.at[k], col=1 - c)

    def load(k):
        return pltpu.make_async_copy(act_ref.at[k], g_ref.at[k, :, my_act], a_load.at[k])

    def wr_load():
        return pltpu.make_async_copy(wr_any, wr_ref, w_load.at[0])

    wr_load().start()
    for k in range(n):
        load(k).start()

    def arrive(k):
        gather.arrive_after_own(k)
        for part, rows in parts_of(lay):
            do_out[k, rows] = dot_nt(full_ref[k, rows], wo_ref[part, theirs, :]).astype(BF)
        swap.start(k)
        for part, rows in parts_of(lay):
            do_own[k, rows] = dot_nt(full_ref[k, rows], wo_ref[part, mine, :])

    def expand_gradient():
        transpose_rows(lay, a2_ref, turned)

        @pl.loop(0, 2 * hid // STRIPE)
        def _(i):
            cols = pl.ds(pl.multiple_of(i * STRIPE, 128), STRIPE)
            for part in range(2):
                weight_gradient(lay, turned, dh_ref, local, part, cols)

    def attention(k):
        swap.arrive(k)
        do_s[...] = (do_own[k] + do_in[k].astype(F32)).astype(BF)
        for h in range(heads):
            q, do = q_s[h, k], do_s[:, h * HD : (h + 1) * HD]
            lse = lse_ref[k, :, h : h + 1]
            p1 = jnp.exp(dot_nt(q, k_s[h, :far]) - lse)
            p2 = jnp.exp(dot_nt(q, k_s[h, far:]) + bias - lse)
            dp1 = dot_nt(do, v_s[h, :far])
            dp2 = dot_nt(do, v_s[h, far:])
            row = jnp.sum(p1 * dp1, axis=1, keepdims=True) + jnp.sum(
                p2 * dp2, axis=1, keepdims=True
            )
            ds1 = (p1 * (dp1 - row)).astype(BF)
            ds2 = (p2 * (dp2 - row)).astype(BF)
            dq = (dot(ds1, k_s[h, :far]) + dot(ds2, k_s[h, far:])) * HD**-0.5
            dq_s[h, k] = dq.astype(BF)
            dk_s[h, :, :far] += dot_tn(q, ds1)
            dk_s[h, :, far:] += dot_tn(q, ds2)
            dv_s[h, :, :far] += dot_tn(do, p1.astype(BF))
            dv_s[h, :, far:] += dot_tn(do, p2.astype(BF))

    def down(k):
        act_copy(k, their_act).wait_recv()
        for part, rows in parts_of(lay):
            acc[rows] = dot(g_ref[k, rows], wr_ref[part])
        reduce.add(k)

    @pl.loop(0, n + 1)
    def _(j):
        @pl.when(j < n)
        def _():
            arrive(near_first(z, n, j))

        @pl.when(j < 2)
        def _():
            load(near_first(z, n, n - 1 - j)).wait()
            act_copy(near_first(z, n, n - 1 - j), my_act).start()

        @pl.when(j == n - 1)
        def _():
            for i in range(2, n):
                load(near_first(z, n, n - 1 - i)).wait()
                act_copy(near_first(z, n, n - 1 - i), my_act).start()

        @pl.when(j == 0)
        def _():
            expand_gradient()
            wr_load().wait()
            if fused:
                batch.start()

        if fused:

            @pl.when(j == 2)
            def _():
                batch.pass_on()

        @pl.when((j > 0) & (j <= n))
        def _():
            attention(near_first(z, n, j - 1))

        i = j - 1 - lag

        @pl.when((i >= 0) & (i < 2))
        def _():
            down(near_first(z, n, n - 1 - i))

    turned_o = turned.at[: o_ref.shape[2]]
    transpose_rows(lay, o_ref, turned_o)
    for part in range(2):
        weight_gradient(lay, turned_o, full_ref, local_out, part, slice(0, full_ref.shape[2]))
    if fused:
        batch_out.start()
    for k in range(n):
        for h in range(heads):
            at = h * 3 * HD
            for rows, first, count in (
                (slice(0, img), k * img, img),
                (slice(img, lay.rows), far + k * txt, txt),
            ):
                dk = dk_s[h, :, first : first + count].T.astype(BF)
                dv = dv_s[h, :, first : first + count].T.astype(BF)
                dqkv_ref[k, rows, at : at + 3 * HD] = jnp.concatenate(
                    [dq_s[h, k, rows], dk, dv], 1
                )
    if fused:
        batch_out.pass_on()
    for i in range(2, n):
        down(near_first(z, n, n - 1 - i))
    res_ref[...] = (mid_ref[...] + acc[...]).astype(BF)
    if fused:
        exp_ref[...] = batch.total()
        out_ref[...] = batch_out.total()
        batch.finish()
        batch_out.finish()
        square_ref[...] = squares_of(exp_ref) + squares_of(out_ref)
    gather.finish()
    swap.finish(n)
    reduce.finish()

    @pl.loop(0, n)
    def _(k):
        act_copy(k, my_act).wait_send()


def pull(lay, fused, low, qkv, lse, wo, act, wr, mid, a2, dh, o):
    n, r, d, hid = lay.n_row, lay.rows, low.shape[1], act.shape[2]
    heads = qkv.shape[2] // (3 * HD)
    keys = n * r
    shapes = [(d, 2 * hid), (o.shape[2], d)]
    return call(
        partial(pull_kernel, lay, fused),
        4,
        [
            ((n, r, 3 * heads * HD), BF),
            ((n, r, 2 * hid), BF),
            ((r, d), BF),
            *[((2, s[0] // 4, s[1]), F32) if fused else ((2, *s), BF) for s in shapes],
            ((8, 128), F32),
        ],
        [
            pltpu.VMEM((heads, n, r, HD), BF),
            pltpu.VMEM((heads, keys, HD), BF),
            pltpu.VMEM((heads, keys, HD), BF),
            pltpu.VMEM((n, r, heads * HD), F32),
            pltpu.VMEM((n, r, heads * HD), BF),
            pltpu.VMEM((n, r, heads * HD), BF),
            pltpu.VMEM((r, heads * HD), BF),
            pltpu.VMEM((heads, n, r, HD), BF),
            pltpu.VMEM((heads, HD, keys), F32),
            pltpu.VMEM((heads, HD, keys), F32),
            pltpu.VMEM((r, d), F32),
            pltpu.VMEM((n, r, d), BF),
            pltpu.VMEM((n + 1, r, d), BF),
            pltpu.VMEM((d, keys), BF),
            pltpu.VMEM(wr.shape, BF),
            pltpu.VMEM((n, r, d), BF),
            dma(n),
            dma(1),
            dma(2, n),
            dma(n),
            dma(n),
            dma(n),
            dma(n),
            dma(n),
            dma(n),
            dma(n + 1),
            *([t for s in shapes for t in batch_scratch(*s)] if fused else []),
        ],
        10**10,
        low,
        qkv,
        lse,
        wo,
        act,
        wr,
        mid,
        a2,
        dh,
        o,
        far=(4, 5),
    )


def input_kernel(
    lay, fused, dqkv_ref, x_ref, dmid_ref, stat_ref, wa_any, a1_ref, g_ref, cb_ref, square_ref,
    dx_ref, att_ref, red_ref, norm_ref, *scratch
):
    (
        full, into, acc, r_out, inbox, stat_out, stat_in, turned, turned_g, wa_ref, w_load,
        s_send, s_recv, r_send, r_recv, t_send, t_recv,
    ) = scratch[:17]
    n = lay.n_row
    z, c = lax.axis_index("row"), lax.axis_index("col")
    half, d = dqkv_ref.shape[2], x_ref.shape[1]
    more = ()
    if fused:
        norm = Norm(4, n, *scratch[41:])
        more = norm.where()
    load = pltpu.make_async_copy(wa_any, wa_ref, w_load.at[0])
    load.start()
    greet(n, False, more)
    swap = Swap(dqkv_ref, into, s_send, s_recv)
    reduce = Reduce(acc, r_out, inbox, r_send, r_recv, n)
    own, other, red = (scratch[17 + 8 * i : 25 + 8 * i] for i in range(3)) if fused else (
        scratch[17:18], scratch[18:19], (red_ref,)
    )
    sums = [batch_of(s) for s in (own, other, red)] if fused else []

    @pl.loop(0, n)
    def _(j):
        swap.start(near_first(z, n, n - 1 - j))

    def gradient(turned, right, local, stripe):
        if stripe == right.shape[2]:
            for part in range(2):
                weight_gradient(lay, turned, right, local, part, slice(0, stripe))
            return

        @pl.loop(0, right.shape[2] // stripe)
        def _(i):
            cols = pl.ds(pl.multiple_of(i * stripe, 128), stripe)
            for part in range(2):
                weight_gradient(lay, turned, right, local, part, cols)

    transpose_rows(lay, a1_ref, turned)
    gradient(turned, dqkv_ref, own[0], half)
    if fused:
        sums[0].start()
    transpose_rows(lay, g_ref, turned_g)
    if fused:
        sums[0].pass_on()
    gradient(turned_g, cb_ref, red[0], STRIPE // 2)
    if fused:
        sums[2].start()
    lag = jnp.minimum(z, n - 1 - z)
    load.wait()

    @pl.loop(0, n + (n - 1) // 2)
    def _(j):
        i = j - lag

        @pl.when((i >= 0) & (i < n))
        def _():
            k = near_first(z, n, n - 1 - i)
            swap.arrive(k)
            mine, theirs = dqkv_ref[k], into[k]
            full[...] = jnp.concatenate(
                [jnp.where(c == 0, mine, theirs), jnp.where(c == 0, theirs, mine)], 1
            )
            for part, rows in parts_of(lay):
                acc[rows] = dot_nt(full[rows], wa_ref[part])

            @pl.when(i == n - 1)
            def _():
                gradient(turned, into, other[0], half)
                if fused:
                    sums[1].start()
                    sums[1].pass_on()

            reduce.add(k)

        if fused:

            @pl.when(j == 0)
            def _():
                sums[2].pass_on()

    mean, inverse = moments(stat_ref)
    normed = (x_ref[...].astype(F32) - mean) * inverse
    grad = acc[...]
    stat_out[0] = sums_of(grad, grad * normed)
    exchange(stat_out, stat_in, t_send, t_recv)
    back_one, back_two = columns(stat_out)
    dx_ref[...] = dmid_ref[...] + inverse * (grad - back_one - normed * back_two)
    if fused:
        red_ref[...] = sums[2].total()
        mine, theirs = sums[0].total(), sums[1].total()
    else:
        mine, theirs = own[0][...], other[0][...]
    att_ref[...] = jnp.concatenate(
        [jnp.where(c == 0, mine, theirs), jnp.where(c == 0, theirs, mine)], 2
    )
    if fused:
        squares = square_ref[...] + squares_of(att_ref) + squares_of(red_ref)
        norm_ref[...] = jnp.sqrt(norm.total(squares))
    for total in sums:
        total.finish()
    swap.finish(n)
    reduce.finish()


def inputs_back(lay, fused, dqkv, x, dmid, stat, wa, a1, g, cb, square):
    n, r, d, half = lay.n_row, lay.rows, x.shape[1], dqkv.shape[2]
    keys = n * r
    shapes = [(d, 2 * half), (g.shape[2], d)]
    return call(
        partial(input_kernel, lay, fused),
        5,
        [
            ((r, d), F32),
            *[((2, s[0] // 4, s[1]), F32) if fused else ((2, *s), BF) for s in shapes],
            ((8, 128), F32),
        ],
        [
            pltpu.VMEM((r, 2 * half), BF),
            pltpu.VMEM((n, r, half), BF),
            pltpu.VMEM((r, d), F32),
            pltpu.VMEM((n, r, d), BF),
            pltpu.VMEM((n + 1, r, d), BF),
            pltpu.VMEM((1, 8, r), F32),
            pltpu.VMEM((1, 8, r), F32),
            pltpu.VMEM((d, keys), BF),
            pltpu.VMEM((g.shape[2], keys), BF),
            pltpu.VMEM(wa.shape, BF),
            dma(1),
            dma(n),
            dma(n),
            dma(n),
            dma(n + 1),
            dma(1),
            dma(1),
            *(
                [
                    *batch_scratch(d, half),
                    *batch_scratch(d, half),
                    *batch_scratch(g.shape[2], d),
                    *norm_scratch(4, n),
                ]
                if fused
                else [pltpu.VMEM((2, d, half), BF)] * 2
            ),
        ],
        10**10,
        dqkv,
        x,
        dmid,
        stat,
        wa,
        a1,
        g,
        cb,
        square,
        far=(4,),
    )


def adamw(gradient, moment, square, weight, clip_factor):
    clipped = gradient * clip_factor
    moment_new = BETA_ONE * moment + (1.0 - BETA_ONE) * clipped
    square_new = BETA_TWO * square + (1.0 - BETA_TWO) * clipped * clipped
    corrected = (
        moment_new
        / (1.0 - BETA_ONE**STEP)
        / (jnp.sqrt(square_new / (1.0 - BETA_TWO**STEP)) + 1e-08)
    )
    return (moment_new, square_new, -RATE * (corrected + DECAY * weight))


def update_kernel(lay, norm_ref, res_ref, dx_ref, *refs):
    grads, moments_in, squares_in, weights = refs[0:4], refs[4:8], refs[8:12], refs[12:16]
    m_out, v_out, s_out, g_out = refs[16:20], refs[20:24], refs[24:28], refs[28:32]
    image_ref, image_grad_ref, text_grad_ref, one_ref = refs[32:36]
    g_s, m_s, v_s, w_s, t_s = (refs[36 + 4 * i : 40 + 4 * i] for i in range(5))
    load, store = refs[56:]
    b = lax.axis_index("batch")
    loads = []
    for i in range(4):
        rows = grads[i].shape[1]
        part = pl.ds(pl.multiple_of(b * rows, 16), rows)
        for m in range(2):
            for q, (src, dst) in enumerate(
                (
                    (grads[i].at[m], g_s[i]),
                    (moments_in[i].at[m], m_s[i]),
                    (squares_in[i].at[m], v_s[i]),
                    (weights[i].at[m, part, :], w_s[i]),
                )
            ):
                loads.append(pltpu.make_async_copy(src, dst.at[m], load.at[i, m, q]))
                loads[-1].start()
    clip = jnp.minimum(1.0, 1.0 / (norm_ref[0:1, 0:1] + 1e-06))
    image_ref[...] = res_ref[: lay.img]
    image_grad_ref[...] = dx_ref[: lay.img]
    text_grad_ref[...] = dx_ref[lay.img : lay.real]
    one_ref[...] = norm_ref[0:1, 0:1]
    stores = []
    for i in range(4):
        for m in range(2):
            for q in range(4):
                loads[8 * i + 4 * m + q].wait()
            stores.append(pltpu.make_async_copy(g_s[i].at[m], g_out[i].at[m], store.at[i, m, 3]))
            stores[-1].start()

            @pl.loop(0, grads[i].shape[1] // TILE)
            def _(r):
                part = pl.ds(pl.multiple_of(r * TILE, TILE), TILE)
                new_m, new_v, step = adamw(
                    g_s[i][m, part, :],
                    m_s[i][m, part, :],
                    v_s[i][m, part, :],
                    w_s[i][m, part, :].astype(F32),
                    clip,
                )
                m_s[i][m, part, :] = new_m
                v_s[i][m, part, :] = new_v
                t_s[i][m, part, :] = step

            for q, (src, dst) in enumerate(
                ((m_s[i], m_out[i]), (v_s[i], v_out[i]), (t_s[i], s_out[i]))
            ):
                stores.append(pltpu.make_async_copy(src.at[m], dst.at[m], store.at[i, m, q]))
                stores[-1].start()
    for each in stores:
        each.wait()


TILE = 16


def update(lay, norm, res, dx, grads, ms, vs, ws):
    d = dx.shape[1]
    shapes = [g.shape for g in grads]
    outs = pl.pallas_call(
        partial(update_kernel, lay),
        out_shape=[jax.ShapeDtypeStruct(s, F32) for _ in range(4) for s in shapes]
        + [
            jax.ShapeDtypeStruct((lay.img, d), BF),
            jax.ShapeDtypeStruct((lay.img, d), F32),
            jax.ShapeDtypeStruct((lay.txt, d), F32),
            jax.ShapeDtypeStruct((1, 1), F32),
        ],
        in_specs=[VMEM] * 3 + [ANY] * 16,
        out_specs=[ANY] * 16 + [VMEM] * 4,
        scratch_shapes=[
            *[pltpu.VMEM(s, t) for t in (F32, F32, F32, BF, F32) for s in shapes],
            dma(4, 2, 4),
            dma(4, 2, 4),
        ],
        compiler_params=pltpu.CompilerParams(vmem_limit_bytes=60 * 2**20),
        cost_estimate=pl.CostEstimate(flops=10**8, bytes_accessed=5 * 10**7, transcendentals=0),
    )(norm, res, dx, *grads, *ms, *vs, *ws)
    return outs[0:4], outs[4:8], outs[8:12], outs[12:16], outs[16:]


def weight_shard(weight, group_index, shard_rows):
    return lax.dynamic_slice_in_dim(weight, group_index * shard_rows, shard_rows, 1).astype(F32)


class Layout:
    def __init__(self, n_row, img, txt):
        self.n_row = n_row
        self.img = img
        self.txt = txt
        self.txt_pad = -(-txt // 16) * 16
        self.rows = img + self.txt_pad
        self.real = img + txt

    def pack(self, image, text):
        return jnp.concatenate(
            [image, text, jnp.zeros((self.txt_pad - self.txt, image.shape[1]), image.dtype)], 0
        )


def on_device(n_batch, n_row, *args):
    (
        image_input,
        text_input,
        image_cotan,
        text_cotan,
        seq_group,
        w_attend,
        w_output,
        w_expand,
        w_reduce,
        m_attend,
        m_output,
        m_expand,
        m_reduce,
        v_attend,
        v_output,
        v_expand,
        v_reduce,
    ) = args
    img, txt = image_input.shape[1], text_input.shape[1]
    lay = Layout(n_row, img, txt)
    group_index = lax.axis_index("batch")
    present = jnp.any(seq_group == group_index).astype(F32)

    low_x = lay.pack(image_input[0], text_input[0])
    low_cot = (lay.pack(image_cotan[0], text_cotan[0]).astype(F32) * present).astype(BF)
    fused = n_batch == 4

    a1_all, qkv, stat_one = attend(lay, low_x, w_attend)
    o_all, lse, cb_all, middle_x, a2_all, act, dh_all, grad_mid, low_mid = forward(
        lay, qkv, low_x, low_cot, w_output, w_reduce, w_expand
    )
    dqkv, g_all, result, g_exp, g_out, square = pull(
        lay, fused, low_mid, qkv, lse, w_output, act, w_reduce, middle_x, a2_all, dh_all, o_all
    )
    grad_in, g_att, g_red, norm = inputs_back(
        lay, fused, dqkv, low_x, grad_mid, stat_one, w_attend, a1_all, g_all, cb_all, square
    )
    sums = [g_att, g_out, g_exp, g_red]
    if not fused:
        sums = [
            lax.psum_scatter(g, "batch", scatter_dimension=1, tiled=True).astype(F32) for g in sums
        ]
    ms = (m_attend, m_output, m_expand, m_reduce)
    vs = (v_attend, v_output, v_expand, v_reduce)
    ws = (w_attend, w_output, w_expand, w_reduce)
    if fused:
        new_m, new_v, steps, sums, (image, image_grad, text_grad, one) = update(
            lay, norm, result, grad_in, sums, ms, vs, ws
        )
        grad_norm = one.reshape(())
    else:
        image, image_grad, text_grad = result[:img], grad_in[:img], grad_in[img : lay.real]
        squares = sum(jnp.sum(g * g) for g in sums)
        grad_norm = jnp.sqrt(lax.psum(lax.psum(lax.psum(squares, "batch"), "row"), "col"))
        clip_factor = jnp.minimum(1.0, 1.0 / (grad_norm + 1e-06))
        new_m, new_v, steps = zip(
            *[
                adamw(g, m, v, weight_shard(w, group_index, g.shape[1]), clip_factor)
                for g, m, v, w in zip(sums, ms, vs, ws)
            ]
        )
    return (
        image[None],
        result[img : lay.real][None],
        image_grad[None],
        text_grad[None],
        *sums,
        *new_m,
        *new_v,
        *steps,
        grad_norm,
    )


def solution(mesh):
    tokens = P("batch", "row", "col")
    wide = P(None, "col", "row")
    tall = P(None, "row", "col")
    wide_shard = P(None, ("col", "batch"), "row")
    tall_shard = P(None, ("row", "batch"), "col")
    shards = (wide_shard, tall_shard, wide_shard, tall_shard)
    return jax.shard_map(
        partial(on_device, mesh.shape["batch"], mesh.shape["row"]),
        mesh=mesh,
        in_specs=(*[tokens] * 4, P(), wide, tall, wide, tall, *shards, *shards),
        out_specs=(*[tokens] * 4, *shards * 4, P()),
        check_vma=False,
    )
```
